32 devices in a mesh: dp: 8 (over z, y), fsdp: 4 (over x, core).
Axes of the slice: x: 2, y: 2, z: 4, core: 2. Of those that a mesh axis runs over, the one named last changes fastest.
Arguments:
- tokens: bfloat16 [32768, 512], P(('dp', 'fsdp')), may hold values from -6 to 6
- first_gain: bfloat16 [512], P('fsdp'), may hold values from 0.5 to 1.5
- first_shift: bfloat16 [512], P('fsdp'), may hold values from -4 to 4
- w_query: bfloat16 [512, 512], P('fsdp'), may hold values from -0.375 to 0.375
- w_key: bfloat16 [512, 512], P('fsdp'), may hold values from -0.375 to 0.375
- w_value: bfloat16 [512, 512], P('fsdp'), may hold values from -0.25 to 0.25
- w_control: bfloat16 [512, 512], P('fsdp'), may hold values from -0.625 to 0.625
- w_output: bfloat16 [512, 512], P('fsdp'), may hold values from -0.375 to 0.375
- second_gain: bfloat16 [512], P('fsdp'), may hold values from 0.5 to 1.5
- second_shift: bfloat16 [512], P('fsdp'), may hold values from -4 to 4
- w_inner: bfloat16 [512, 2048], P('fsdp'), may hold values from -0.25 to 0.25
- inner_bias: bfloat16 [2048], P('fsdp'), may hold values from -4 to 4
- w_outer: bfloat16 [2048, 512], P('fsdp'), may hold values from -0.1875 to 0.1875
- outer_bias: bfloat16 [512], P('fsdp'), may hold values from -4 to 4
- cotangent: bfloat16 [32768, 512], P(('dp', 'fsdp')), may hold values from -6 to 6
Outputs:
- output: bfloat16 [32768, 512], P(('dp', 'fsdp'))
- grad_tokens: bfloat16 [32768, 512], P(('dp', 'fsdp'))
- grad_first_gain: float32 [512], P('fsdp')
- grad_first_shift: float32 [512], P('fsdp')
- grad_w_query: float32 [512, 512], P('fsdp')
- grad_w_key: float32 [512, 512], P('fsdp')
- grad_w_value: float32 [512, 512], P('fsdp')
- grad_w_control: float32 [512, 512], P('fsdp')
- grad_w_output: float32 [512, 512], P('fsdp')
- grad_second_gain: float32 [512], P('fsdp')
- grad_second_shift: float32 [512], P('fsdp')
- grad_w_inner: float32 [512, 2048], P('fsdp')
- grad_inner_bias: float32 [2048], P('fsdp')
- grad_w_outer: float32 [2048, 512], P('fsdp')
- grad_outer_bias: float32 [512], P('fsdp')
The draws below stay inside these ranges and needn't reach their ends.
All inputs are finite; a program needn't handle non-finite values.
Results may differ from the reference program's by a relative error of at most 0.022.
Values may be sent and summed in bfloat16 or wider, within the bound.
No kernel may reach another device: no remote copies, remote signals or barrier semaphores. Data moves between devices by JAX's collectives and lax.ppermute only.
A program may use at most 128 MiB of HBM per device.

```python
import jax
import jax.numpy as jnp
from jax import lax

D = 512
HEADS = 8
HEAD = 64
SLOTS = 64
FF = 2048
LEN = 1024
TOKENS = 32768


def block_scale(rng, dims, split, low, high):
    loudness = 1.0
    for position, shards_of in split:
        steps = jax.random.uniform(jax.random.fold_in(jax.random.fold_in(rng, 6), position), (shards_of,), jnp.float32, low / len(split), high / len(split))
        loudness = loudness * jnp.repeat(jnp.exp(steps), dims[position] // shards_of).reshape((-1,) + (1,) * (len(dims) - 1 - position))
    return loudness


def bell_draw(rng, shape, width, limit, pieces=(), kind=jnp.bfloat16):
    level = block_scale(rng, shape, pieces, -0.22, 0.18) if pieces else 1.0
    values = jax.random.normal(rng, shape, jnp.float32) * width * level
    return jnp.minimum(jnp.maximum(values, -limit), limit).astype(kind)


def setup_inputs(seed: int = 0) -> dict:
    streams_of = jax.random.split(jax.random.key(seed), 16)
    tokens = bell_draw(streams_of[0], (TOKENS, D), 1.0, 6.0, ((0, 32),))
    first_gain = jnp.clip(1.0 + 0.1 * jax.random.normal(streams_of[1], (D,), jnp.float32), 0.5, 1.5).astype(jnp.bfloat16)
    first_shift = bell_draw(streams_of[2], (D,), 0.3, 4.0, ((0, 4),))
    w_query = bell_draw(streams_of[3], (D, D), (D // 2) ** -0.5, 0.375, ((0, 4),))
    w_key = bell_draw(streams_of[4], (D, D), (D // 2) ** -0.5, 0.375, ((0, 4),))
    w_value = bell_draw(streams_of[5], (D, D), D ** -0.5, 0.25, ((0, 4),))
    w_control = bell_draw(streams_of[6], (D, HEADS * SLOTS), (D // 6) ** -0.5, 0.625, ((0, 4),))
    w_output = bell_draw(streams_of[7], (D, D), (D // 2) ** -0.5, 0.375, ((0, 4),))
    second_gain = jnp.clip(1.0 + 0.1 * jax.random.normal(streams_of[8], (D,), jnp.float32), 0.5, 1.5).astype(jnp.bfloat16)
    second_shift = bell_draw(streams_of[9], (D,), 0.3, 4.0, ((0, 4),))
    w_inner = bell_draw(streams_of[10], (D, FF), D ** -0.5, 0.25, ((0, 4),))
    inner_bias = bell_draw(streams_of[11], (FF,), 0.3, 4.0, ((0, 4),))
    w_outer = bell_draw(streams_of[12], (FF, D), (FF // 2) ** -0.5, 0.1875, ((0, 4),))
    outer_bias = bell_draw(streams_of[13], (D,), 0.3, 4.0, ((0, 4),))
    cotangent = bell_draw(streams_of[14], (TOKENS, D), 1.0, 6.0, ((0, 32),))
    return dict(tokens=tokens, first_gain=first_gain, first_shift=first_shift, w_query=w_query, w_key=w_key, w_value=w_value, w_control=w_control, w_output=w_output, second_gain=second_gain, second_shift=second_shift, w_inner=w_inner, inner_bias=inner_bias, w_outer=w_outer, outer_bias=outer_bias, cotangent=cotangent)


@jax.custom_vjp
def low(v):
    return lax.optimization_barrier(v.astype(jnp.bfloat16)).astype(jnp.float32)

@jax.custom_vjp
def low_back(v):
    return v

def low_keep(v):
    return (low(v), None)

def low_pass(kept, grad):
    return (grad,)

def back_keep(v):
    return (v, None)

def back_low(kept, grad):
    return (low(grad),)
low.defvjp(low_keep, low_pass)
low_back.defvjp(back_keep, back_low)

def layer_norm(values, gain, shift):
    average = lax.optimization_barrier(jnp.mean(values, axis=-1, keepdims=True))
    centred = values - average
    variance = lax.optimization_barrier(jnp.mean(centred * centred, axis=-1, keepdims=True))
    return centred * lax.rsqrt(variance + 1e-05) * gain + shift

def matmul(left, right):
    return jnp.dot(left, right, precision=lax.Precision.HIGHEST)

def abc_head(queries, keys, values, control):
    length = queries.shape[0]
    causal = jnp.arange(length)[:, None] >= jnp.arange(length)[None, :]
    scores = jnp.where(causal, low(low_back(matmul(queries, keys.T))), 0.0)
    numerator = low_back(matmul(scores, control))
    denominator = jnp.cumsum(control, axis=0)
    logits = numerator / denominator * queries.shape[1] ** (-0.5)
    probabilities = jax.nn.softmax(logits, axis=-1)
    weights = low(probabilities / denominator)
    mixing = jnp.where(causal, low(low_back(matmul(weights, control.T))), 0.0)
    return matmul(mixing, values)

def split_heads(array, item_width):
    return array.reshape(array.shape[0], -1, item_width).transpose(1, 0, 2)

def sequence_forward(sequence, params):
    first_gain, first_shift, w_query, w_key, w_value, w_control, w_output, second_gain, second_shift, w_inner, inner_bias, w_outer, outer_bias = params
    normed = low(layer_norm(sequence, first_gain, first_shift))
    queries = low(low_back(matmul(normed, w_query)))
    keys = low(low_back(matmul(normed, w_key)))
    values = low(low_back(matmul(normed, w_value)))
    control = low(jnp.exp(low_back(matmul(normed, w_control))))
    heads_out = jax.vmap(abc_head)(split_heads(queries, HEAD), split_heads(keys, HEAD), split_heads(values, HEAD), split_heads(control, SLOTS))
    mixed = low(low_back(heads_out.transpose(1, 0, 2).reshape(sequence.shape[0], -1)))
    resid = sequence + low_back(matmul(mixed, w_output))
    hidden = low(layer_norm(resid, second_gain, second_shift))
    inner = low_back(matmul(hidden, w_inner) + inner_bias)
    activated = low(jax.nn.gelu(inner))
    return resid + matmul(activated, w_outer) + outer_bias

def reference(tokens, first_gain, first_shift, w_query, w_key, w_value, w_control, w_output, second_gain, second_shift, w_inner, inner_bias, w_outer, outer_bias, cotangent):
    params = tuple((weight.astype(jnp.float32) for weight in (first_gain, first_shift, w_query, w_key, w_value, w_control, w_output, second_gain, second_shift, w_inner, inner_bias, w_outer, outer_bias)))
    tokens_f = tokens.astype(jnp.float32)
    stepper = jax.checkpoint(sequence_forward)

    def forward(inputs, weights):
        sequences = inputs.reshape(-1, LEN, D)

        def scan_step(carry, sequence):
            return (carry, stepper(sequence, weights))
        _, results = lax.scan(scan_step, None, sequences)
        return results.reshape(-1, D)
    result, pullback = jax.vjp(forward, tokens_f, params)
    grad_inputs, grad_params = pullback(cotangent.astype(jnp.float32))
    return (result.astype(jnp.bfloat16), grad_inputs.astype(jnp.bfloat16), grad_params[0], grad_params[1], grad_params[2], grad_params[3], grad_params[4], grad_params[5], grad_params[6], grad_params[7], grad_params[8], grad_params[9], grad_params[10], grad_params[11], grad_params[12])
```

```python
import functools
import jax
import jax.numpy as jnp
from jax import lax
from jax.experimental import pallas as pl
from jax.experimental.pallas import tpu as pltpu
from jax.sharding import PartitionSpec as P

F32 = jnp.float32
BF16 = jnp.bfloat16
PAIR = 128
SCALE = 64 ** -0.5


def mm(a, b):
    return lax.dot_general(a, b, (((1,), (0,)), ((), ())), preferred_element_type=F32)


def mm_nt(a, b):
    return lax.dot_general(a, b, (((1,), (1,)), ((), ())), preferred_element_type=F32)


def mm_tn(a, b):
    return lax.dot_general(a, b, (((0,), (0,)), ((), ())), preferred_element_type=F32)


def left_half(rows):
    return lax.broadcasted_iota(jnp.int32, (rows, PAIR), 1) < 64


def split_pair(x, left):
    zero = jnp.zeros((), x.dtype)
    return jnp.concatenate((jnp.where(left, x, zero), jnp.where(left, zero, x)), axis=0)


def same_head():
    r = lax.broadcasted_iota(jnp.int32, (PAIR, PAIR), 0) < 64
    c = lax.broadcasted_iota(jnp.int32, (PAIR, PAIR), 1) < 64
    return r == c


def causal_pair(rows):
    r = lax.broadcasted_iota(jnp.int32, (rows, 2 * rows), 0)
    c = lax.broadcasted_iota(jnp.int32, (rows, 2 * rows), 1)
    return r >= jnp.where(c >= rows, c - rows, c)


def half_reduce(x, left, fn, fill):
    a = fn(jnp.where(left, x, fill), axis=1, keepdims=True)
    b = fn(jnp.where(left, fill, x), axis=1, keepdims=True)
    return jnp.where(left, a, b)


def forward_kernel(C, qkvf, mixed, a_out, b_out, s_out, p_out, rden_out, s1_out, s2_out, s1, s2, carry):
    c = pl.program_id(0)

    @pl.when(c == 0)
    def _():
        s1[...] = jnp.zeros_like(s1)
        s2[...] = jnp.zeros_like(s2)
        carry[...] = jnp.zeros_like(carry)

    left = left_half(C)
    causal = causal_pair(C)
    same = same_head()
    lower = (lax.broadcasted_iota(jnp.int32, (C, C), 0) >= lax.broadcasted_iota(jnp.int32, (C, C), 1)).astype(BF16)
    zero = jnp.zeros((), BF16)
    denom = mm(lower, qkvf[:, 1536:2048]) + carry[0:1, :]
    carry[0:1, :] = denom[C - 1 :, :]
    rden_all = 1.0 / denom
    rden_out[...] = rden_all
    for j in range(4):
        sl = slice(PAIR * j, PAIR * (j + 1))
        q = qkvf[:, PAIR * j : PAIR * (j + 1)]
        k = qkvf[:, 512 + PAIR * j : 512 + PAIR * (j + 1)]
        v = qkvf[:, 1024 + PAIR * j : 1024 + PAIR * (j + 1)]
        f = qkvf[:, 1536 + PAIR * j : 1536 + PAIR * (j + 1)]
        rden = rden_all[:, sl]
        f2 = split_pair(f, left)
        a2 = jnp.where(causal, mm_nt(q, split_pair(k, left)).astype(BF16), zero)
        a_out[:, 2 * C * j : 2 * C * (j + 1)] = a2
        s1b = s1[j].astype(BF16)
        s2b = s2[j].astype(BF16)
        s1_out[0, :, sl] = s1b
        s2_out[0, :, sl] = s2b
        numer = mm(a2, f2) + mm(q, s1b)
        s = numer * rden * SCALE
        s_out[:, sl] = s
        top = half_reduce(s, left, jnp.max, -jnp.inf)
        e = jnp.exp(s - top)
        p = e / half_reduce(e, left, jnp.sum, 0.0)
        p_out[:, sl] = p
        g = (p * rden).astype(BF16)
        b2 = jnp.where(causal, mm_nt(g, f2).astype(BF16), zero)
        b_out[:, 2 * C * j : 2 * C * (j + 1)] = b2
        o = mm(b2, split_pair(v, left)) + mm(g, s2b)
        mixed[:, sl] = o.astype(BF16)
        s1[j] += jnp.where(same, mm_tn(k, f), 0.0)
        s2[j] += jnp.where(same, mm_tn(f, v), 0.0)


def attention_forward(qkvf, C=128):
    T = qkvf.shape[0]
    n = T // C
    row = lambda w: pl.BlockSpec((C, w), lambda i: (i, 0))
    st = pl.BlockSpec((1, PAIR, 512), lambda i: (i, 0, 0))
    return pl.pallas_call(
        functools.partial(forward_kernel, C),
        grid=(n,),
        in_specs=[row(2048)],
        out_specs=[row(512), row(8 * C), row(8 * C), row(512), row(512), row(512), st, st],
        out_shape=[
            jax.ShapeDtypeStruct((T, 512), BF16),
            jax.ShapeDtypeStruct((T, 8 * C), BF16),
            jax.ShapeDtypeStruct((T, 8 * C), BF16),
            jax.ShapeDtypeStruct((T, 512), F32),
            jax.ShapeDtypeStruct((T, 512), F32),
            jax.ShapeDtypeStruct((T, 512), F32),
            jax.ShapeDtypeStruct((n, PAIR, 512), BF16),
            jax.ShapeDtypeStruct((n, PAIR, 512), BF16),
        ],
        scratch_shapes=[pltpu.VMEM((4, PAIR, PAIR), F32), pltpu.VMEM((4, PAIR, PAIR), F32), pltpu.VMEM((8, 512), F32)],
        compiler_params=pltpu.CompilerParams(vmem_limit_bytes=48 << 20),
        name="attention_forward",
    )(qkvf)


def backward_kernel(C, qkvf, a_in, b_in, s_in, p_in, rden_in, s1_in, s2_in, do_in, grad, r1, r2, carry):
    c = pl.program_id(0)

    @pl.when(c == 0)
    def _():
        r1[...] = jnp.zeros_like(r1)
        r2[...] = jnp.zeros_like(r2)
        carry[...] = jnp.zeros_like(carry)

    left = left_half(C)
    causal = causal_pair(C)
    same = same_head()
    upper = (lax.broadcasted_iota(jnp.int32, (C, C), 0) <= lax.broadcasted_iota(jnp.int32, (C, C), 1)).astype(BF16)
    upper2 = jnp.concatenate((upper, upper), axis=1)
    zero = jnp.zeros((), BF16)
    for j in range(4):
        sl = slice(PAIR * j, PAIR * (j + 1))
        sl2 = slice(2 * C * j, 2 * C * (j + 1))
        q = qkvf[:, PAIR * j : PAIR * (j + 1)]
        k = qkvf[:, 512 + PAIR * j : 512 + PAIR * (j + 1)]
        v = qkvf[:, 1024 + PAIR * j : 1024 + PAIR * (j + 1)]
        f = qkvf[:, 1536 + PAIR * j : 1536 + PAIR * (j + 1)]
        do = do_in[:, sl]
        a2 = a_in[:, sl2]
        b2 = b_in[:, sl2]
        s = s_in[:, sl]
        p = p_in[:, sl]
        rden = rden_in[:, sl]
        s1b = s1_in[0, :, sl]
        s2b = s2_in[0, :, sl]
        f2 = split_pair(f, left)
        g = (p * rden).astype(BF16)
        db2 = jnp.where(causal, mm_nt(do, split_pair(v, left)).astype(BF16), zero)
        dg = mm(db2, f2) + mm_nt(do, s2b)
        dp = dg * rden
        dpp = dp * p
        ds = dpp - p * half_reduce(dpp, left, jnp.sum, 0.0)
        ddenom = -(dpp + ds * s) * rden
        dn = (ds * SCALE * rden).astype(BF16)
        da2 = jnp.where(causal, mm_nt(dn, f2).astype(BF16), zero)
        r1b = r1[j].astype(BF16)
        r2b = r2[j].astype(BF16)
        dq = mm(da2, split_pair(k, left)) + mm_nt(dn, s1b)
        grad[:, PAIR * j : PAIR * (j + 1)] = dq.astype(BF16)
        dk2 = mm_tn(da2, q)
        dk = jnp.where(left, dk2[:C], dk2[C:]) + mm_nt(f, r1b)
        grad[:, 512 + PAIR * j : 512 + PAIR * (j + 1)] = dk.astype(BF16)
        dv2 = mm_tn(b2, do)
        dv = jnp.where(left, dv2[:C], dv2[C:]) + mm(f, r2b)
        grad[:, 1024 + PAIR * j : 1024 + PAIR * (j + 1)] = dv.astype(BF16)
        df2 = mm_tn(db2, g) + mm_tn(a2, dn)
        hi = ddenom.astype(BF16)
        lo = (ddenom - hi.astype(F32)).astype(BF16)
        df = jnp.where(left, df2[:C], df2[C:]) + mm_nt(v, r2b) + mm(k, r1b)
        df = df + mm(upper2, jnp.concatenate((hi, lo), axis=0)) + carry[0:1, sl]
        grad[:, 1536 + PAIR * j : 1536 + PAIR * (j + 1)] = (df * f.astype(F32)).astype(BF16)
        carry[0:1, sl] += jnp.sum(ddenom, axis=0, keepdims=True)
        r1[j] += jnp.where(same, mm_tn(q, dn), 0.0)
        r2[j] += jnp.where(same, mm_tn(g, do), 0.0)


def attention_backward(saved, d_o, C=128):
    qkvf, a, b, s, p, rden, s1, s2 = saved
    T = qkvf.shape[0]
    n = T // C
    row = lambda w: pl.BlockSpec((C, w), lambda i: (n - 1 - i, 0))
    st = pl.BlockSpec((1, PAIR, 512), lambda i: (n - 1 - i, 0, 0))
    return pl.pallas_call(
        functools.partial(backward_kernel, C),
        grid=(n,),
        in_specs=[row(2048), row(8 * C), row(8 * C), row(512), row(512), row(512), st, st, row(512)],
        out_specs=row(2048),
        out_shape=jax.ShapeDtypeStruct((T, 2048), BF16),
        scratch_shapes=[pltpu.VMEM((4, PAIR, PAIR), F32), pltpu.VMEM((4, PAIR, PAIR), F32), pltpu.VMEM((8, 512), F32)],
        compiler_params=pltpu.CompilerParams(vmem_limit_bytes=48 << 20),
        name="attention_backward",
    )(qkvf, a, b, s, p, rden, s1, s2, d_o)


EPS = 1e-5
MASKS = (0, 2, 1, 3)
ROWS = 256


def blocks_of(me):
    return [me ^ mask for mask in MASKS]


def take_blocks(ref, blocks, width):
    return jnp.concatenate([ref[:, pl.ds(pl.multiple_of(b * width, width), width)] for b in blocks], axis=1)


def put_blocks(ref, values, blocks, width):
    for i, b in enumerate(blocks):
        ref[:, pl.ds(pl.multiple_of(b * width, width), width)] = values[:, i * width : (i + 1) * width]


def stats(x):
    mean = jnp.mean(x, axis=1, keepdims=True)
    centred = x - mean
    inv = lax.rsqrt(jnp.mean(centred * centred, axis=1, keepdims=True) + EPS)
    return centred * inv, inv


def vector(refs, start, width):
    return jnp.concatenate([r[0:1, start : start + width] for r in refs], axis=1).astype(F32)


def project_kernel(me_ref, tokens, w0, w1, w2, w3, v0, v1, v2, v3, qkvf, n1_out, a1, scr):
    t = pl.program_id(0)

    @pl.when(t == 0)
    def _():
        blocks = blocks_of(me_ref[0])
        gain = vector((v0, v1, v2, v3), 0, 128)
        shift = vector((v0, v1, v2, v3), 128, 128)

        def chunk(c, carry):
            rows = pl.ds(pl.multiple_of(c * ROWS, ROWS), ROWS)
            n, _ = stats(tokens[rows, :].astype(F32))
            scr[...] = n
            n_rel = take_blocks(scr, blocks, 128)
            n1_out[rows, :] = n_rel.astype(BF16)
            a1[rows, :] = (n_rel * gain + shift).astype(BF16)
            return carry

        lax.fori_loop(0, tokens.shape[0] // ROWS, chunk, 0)

    w = jnp.concatenate((w0[...], w1[...], w2[...], w3[...]), axis=0)
    out = mm(a1[...], w)

    @pl.when(t < 6)
    def _():
        qkvf[...] = out.astype(BF16)

    @pl.when(t >= 6)
    def _():
        qkvf[...] = jnp.exp(out).astype(BF16)


SMEM = pl.BlockSpec(memory_space=pltpu.SMEM)


def whole(shape):
    return pl.BlockSpec(shape, lambda i: (0,) * len(shape))


def params():
    return pltpu.CompilerParams(vmem_limit_bytes=56 << 20)


VEC = pl.BlockSpec((16, 2048), lambda i: (8, 0))


def project(me, tokens, packs):
    T = tokens.shape[0]
    return pl.pallas_call(
        project_kernel,
        grid=(8,),
        in_specs=[SMEM, whole((T, 512))] + [pl.BlockSpec((128, 256), lambda t: (0, t))] * 4 + [VEC] * 4,
        out_specs=[pl.BlockSpec((T, 256), lambda t: (0, t)), whole((T, 512))],
        out_shape=[jax.ShapeDtypeStruct((T, 2048), BF16), jax.ShapeDtypeStruct((T, 512), BF16)],
        scratch_shapes=[pltpu.VMEM((T, 512), BF16), pltpu.VMEM((ROWS, 512), F32)],
        compiler_params=params(),
        name="project",
    )(me, tokens, *packs, *packs)


def gelu_parts(v):
    c = 0.7978845608028654
    v2 = v * v
    t = jnp.tanh(c * v * (1.0 + 0.044715 * v2))
    half = 0.5 * (1.0 + t)
    slope = half + 0.5 * v * (1.0 - t * t) * (c * (1.0 + 3 * 0.044715 * v2))
    return v * half, slope


def ffn_forward_kernel(me_ref, tokens, mixed, dy, o0, o1, o2, o3, i0, i1, i2, i3, u0, u1, u2, u3, v0, v1, v2, v3,
                       out, n2_out, r2_out, slope_out, keep, send, acc, scr, bias):
    c = pl.program_id(0)
    blocks = blocks_of(me_ref[0])
    vs = (v0, v1, v2, v3)

    @pl.when(c == 0)
    def _():
        acc[...] = jnp.zeros_like(acc)
        put_blocks(bias, jnp.broadcast_to(vector(vs, 512, 128), (8, 512)), blocks, 128)

    wo = jnp.concatenate((o0[...], o1[...], o2[...], o3[...]), axis=0)
    resid = tokens[...].astype(F32) + mm(take_blocks(mixed, blocks, 128), wo)
    n2, r2 = stats(resid)
    scr[...] = n2
    n2 = take_blocks(scr, blocks, 128)
    n2_out[...] = n2.astype(BF16)
    r2_out[...] = jnp.broadcast_to(r2, r2_out.shape)
    a2 = (n2 * vector(vs, 256, 128) + vector(vs, 384, 128)).astype(BF16)
    total = resid + bias[0:1, :]
    dyt = dy[...].T
    for i, (u, v) in enumerate(zip((u0, u1, u2, u3), vs)):
        cols = pl.ds(pl.multiple_of(blocks[i] * 512, 512), 512)
        w = jnp.concatenate((i0[:, cols], i1[:, cols], i2[:, cols], i3[:, cols]), axis=0)
        act, slope = gelu_parts(mm(a2, w) + v[0:1, 640:1152].astype(F32))
        act = act.astype(BF16)
        slope_out[:, 512 * i : 512 * (i + 1)] = slope.astype(BF16)
        total = total + mm(act, u[...])
        acc[i] += mm(dyt, act)
    out[...] = total.astype(BF16)

    @pl.when(c == pl.num_programs(0) - 1)
    def _():
        keep[...] = acc[0:2].astype(BF16)
        send[...] = acc[2:4].astype(BF16)


def ffn_forward(me, tokens, mixed, dy, wo, wi, wu, packs):
    T = tokens.shape[0]
    row = lambda w: pl.BlockSpec((ROWS, w), lambda i: (i, 0))
    S = jax.ShapeDtypeStruct
    return pl.pallas_call(
        ffn_forward_kernel,
        grid=(T // ROWS,),
        in_specs=[SMEM, row(512), row(512), row(512)] + [whole((128, 512))] * 4 + [whole((128, 2048))] * 4 + [whole((512, 512))] * 4 + [VEC] * 4,
        out_specs=[row(512), row(512), row(128), row(2048), whole((2, 512, 512)), whole((2, 512, 512))],
        out_shape=[S((T, 512), BF16), S((T, 512), BF16), S((T, 128), F32), S((T, 2048), BF16), S((2, 512, 512), BF16), S((2, 512, 512), BF16)],
        scratch_shapes=[pltpu.VMEM((4, 512, 512), F32), pltpu.VMEM((ROWS, 512), F32), pltpu.VMEM((8, 512), F32)],
        compiler_params=params(),
        name="ffn_forward",
    )(me, tokens, mixed, dy, *wo, *wi, *wu, *packs)


def ffn_backward_kernel(me_ref, dy_ref, n2_ref, r2_ref, slope, mixed, o0, o1, o2, o3, i0, i1, i2, i3, u0, u1, u2, u3, v0, v1, v2, v3,
                        dres_out, do_out, keep, send, keep_o, send_o, acc, acc_o, sums, scr):
    c = pl.program_id(0)
    blocks = blocks_of(me_ref[0])
    vs = (v0, v1, v2, v3)

    @pl.when(c == 0)
    def _():
        acc[...] = jnp.zeros_like(acc)
        acc_o[...] = jnp.zeros_like(acc_o)
        sums[...] = jnp.zeros_like(sums)

    dy = dy_ref[...]
    n2b = n2_ref[...]
    n2t = n2b.T
    da2 = jnp.zeros((ROWS, 512), F32)
    for i, u in enumerate((u0, u1, u2, u3)):
        cols = pl.ds(pl.multiple_of(blocks[i] * 512, 512), 512)
        w = jnp.concatenate((i0[:, cols], i1[:, cols], i2[:, cols], i3[:, cols]), axis=0)
        din = (mm_nt(dy, u[...]) * slope[:, 512 * i : 512 * (i + 1)].astype(F32)).astype(BF16)
        da2 = da2 + mm_nt(din, w)
        acc[:, cols] += mm(n2t, din)
        sums[0:1, cols] += jnp.sum(din.astype(F32), axis=0, keepdims=True)
    n2 = n2b.astype(F32)
    e = da2 * vector(vs, 256, 128)
    dn = r2_ref[:, 0:1] * (e - jnp.mean(e, axis=1, keepdims=True) - n2 * jnp.mean(e * n2, axis=1, keepdims=True))
    put_blocks(scr, dn, blocks, 128)
    dyf = dy.astype(F32)
    sums[1:2, 0:512] += jnp.sum(dyf, axis=0, keepdims=True)
    dres = dyf + scr[...]
    dres_out[...] = dres
    dattn = dres.astype(BF16)
    wo = jnp.concatenate((o0[...], o1[...], o2[...], o3[...]), axis=0)
    acc_o[...] += mm_tn(take_blocks(mixed, blocks, 128), dattn)
    put_blocks(do_out, mm_nt(dattn, wo).astype(BF16), blocks, 128)

    @pl.when(c == pl.num_programs(0) - 1)
    def _():
        tail = jnp.concatenate((sums[...], jnp.zeros_like(sums)), axis=0).astype(BF16)
        for i in range(2):
            keep[i, 0:128, :] = acc[128 * i : 128 * (i + 1), :].astype(BF16)
            send[i, 0:128, :] = acc[128 * (i + 2) : 128 * (i + 3), :].astype(BF16)
            keep[i, 128:144, :] = tail
            send[i, 128:144, :] = tail
            keep_o[i] = acc_o[128 * i : 128 * (i + 1), :].astype(BF16)
            send_o[i] = acc_o[128 * (i + 2) : 128 * (i + 3), :].astype(BF16)


def ffn_backward(me, dy, n2, r2, slope, mixed, wo, wi, wu, packs):
    T = dy.shape[0]
    row = lambda w: pl.BlockSpec((ROWS, w), lambda i: (i, 0))
    S = jax.ShapeDtypeStruct
    return pl.pallas_call(
        ffn_backward_kernel,
        grid=(T // ROWS,),
        in_specs=[SMEM, row(512), row(512), row(128), row(2048), row(512)]
        + [whole((128, 512))] * 4 + [whole((128, 2048))] * 4 + [whole((512, 512))] * 4 + [VEC] * 4,
        out_specs=[row(512), row(512), whole((2, 144, 2048)), whole((2, 144, 2048)), whole((2, 128, 512)), whole((2, 128, 512))],
        out_shape=[S((T, 512), F32), S((T, 512), BF16), S((2, 144, 2048), BF16), S((2, 144, 2048), BF16), S((2, 128, 512), BF16), S((2, 128, 512), BF16)],
        scratch_shapes=[pltpu.VMEM((512, 2048), F32), pltpu.VMEM((512, 512), F32), pltpu.VMEM((8, 2048), F32), pltpu.VMEM((ROWS, 512), F32)],
        compiler_params=params(),
        name="ffn_backward",
    )(me, dy, n2, r2, slope, mixed, *wo, *wi, *wu, *packs)


def project_grad_kernel(n1, d, keep, send, n1t):
    @pl.when(pl.program_id(0) == 0)
    def _():
        n1t[...] = n1[...].T

    dv = d[...]
    out = mm(n1t[...], dv).astype(BF16)
    total = jnp.sum(dv.astype(F32), axis=0, keepdims=True)
    tail = jnp.broadcast_to(total, (16, total.shape[1])).astype(BF16)
    for i in range(2):
        keep[i, 0:128, :] = out[128 * i : 128 * (i + 1)]
        send[i, 0:128, :] = out[128 * (i + 2) : 128 * (i + 3)]
        keep[i, 128:144, :] = tail
        send[i, 128:144, :] = tail


def project_grad(n1, d):
    T = n1.shape[0]
    spec = pl.BlockSpec((2, 144, 256), lambda t: (0, 0, t))
    S = jax.ShapeDtypeStruct((2, 144, 2048), BF16)
    return pl.pallas_call(
        project_grad_kernel,
        grid=(8,),
        in_specs=[whole((T, 512)), pl.BlockSpec((T, 256), lambda t: (0, t))],
        out_specs=[spec, spec],
        out_shape=[S, S],
        scratch_shapes=[pltpu.VMEM((512, T), BF16)],
        compiler_params=params(),
        name="project_grad",
    )(n1, d)


def input_grad_kernel(me_ref, tokens, d, dres, w0, w1, w2, w3, v0, v1, v2, v3, out, scr):
    blocks = blocks_of(me_ref[0])
    n, r = stats(tokens[...].astype(F32))
    scr[...] = n
    n = take_blocks(scr, blocks, 128)
    w = jnp.concatenate((w0[...], w1[...], w2[...], w3[...]), axis=0)
    e = mm_nt(d[...], w) * vector((v0, v1, v2, v3), 0, 128)
    dn = r * (e - jnp.mean(e, axis=1, keepdims=True) - n * jnp.mean(e * n, axis=1, keepdims=True))
    put_blocks(scr, dn, blocks, 128)
    out[...] = (dres[...] + scr[...]).astype(BF16)


def input_grad(me, tokens, d, dres, packs):
    T = tokens.shape[0]
    row = lambda w: pl.BlockSpec((ROWS, w), lambda i: (i, 0))
    return pl.pallas_call(
        input_grad_kernel,
        grid=(T // ROWS,),
        in_specs=[SMEM, row(512), row(2048), row(512)] + [whole((128, 2048))] * 4 + [VEC] * 4,
        out_specs=row(512),
        out_shape=jax.ShapeDtypeStruct((T, 512), BF16),
        scratch_shapes=[pltpu.VMEM((ROWS, 512), F32)],
        compiler_params=params(),
        name="input_grad",
    )(me, tokens, d, dres, *packs, *packs)


def add(a, b):
    return (a.astype(F32) + b.astype(F32)).astype(BF16)


def exchange(value, axis, size, mask):
    return lax.ppermute(value, axis, [(i, i ^ mask) for i in range(size)])


def gather(own):
    across = exchange(own, "fsdp", 4, 2)
    return own, across, exchange(own, "fsdp", 4, 1), exchange(across, "fsdp", 4, 1)


def reduce_to_owner(keep, send, dp):
    both = add(keep, exchange(send, "fsdp", 4, 1))
    part = add(both[0], exchange(both[1], "fsdp", 4, 2))
    odd = (lax.axis_index("dp") & 1) == 1
    half = part.shape[1] // 2
    low, high = part[:, :half], part[:, half:]
    part = add(jnp.where(odd, high, low), exchange(jnp.where(odd, low, high), "dp", dp, 1))
    mask = 2
    while mask < dp:
        part = add(part, exchange(part, "dp", dp, mask))
        mask *= 2
    other = exchange(part, "dp", dp, 1)
    return jnp.concatenate((jnp.where(odd, other, part), jnp.where(odd, part, other)), axis=1).astype(F32)


def per_device(dp, tokens, first_gain, first_shift, w_query, w_key, w_value, w_control, w_output, second_gain, second_shift, w_inner, inner_bias, w_outer, outer_bias, cotangent):
    me = lax.axis_index("fsdp").astype(jnp.int32)
    me_arr = me.reshape(1)
    vec = jnp.concatenate((first_gain, first_shift, second_gain, second_shift, outer_bias, inner_bias, jnp.zeros((896,), BF16)))
    own = jnp.concatenate((jnp.concatenate((w_query, w_key, w_value, w_control), axis=1), jnp.broadcast_to(vec, (16, 2048))), axis=0)
    packs = gather(own)
    wo = gather(w_output)
    wi = gather(w_inner)
    wu = gather(w_outer)
    qkvf, n1 = project(me_arr, tokens, packs)
    mixed, *saved = attention_forward(qkvf, ROWS)
    output, n2, r2, slope, keep_u, send_u = ffn_forward(me_arr, tokens, mixed, cotangent, wo, wi, wu, packs)
    dres, d_o, keep_i, send_i, keep_o, send_o = ffn_backward(me_arr, cotangent, n2, r2, slope, mixed, wo, wi, wu, packs)
    grad = attention_backward((qkvf, *saved), d_o, ROWS)
    keep_p, send_p = project_grad(n1, grad)
    grad_tokens = input_grad(me_arr, tokens, grad, dres, packs)
    sum_u = reduce_to_owner(keep_u, send_u, dp)
    sum_i = reduce_to_owner(keep_i, send_i, dp)
    sum_o = reduce_to_owner(keep_o, send_o, dp)
    sum_p = reduce_to_owner(keep_p, send_p, dp)
    f32 = lambda v: v.astype(F32)
    col = sum_i[128]
    grad_inner = f32(second_gain)[:, None] * sum_i[:128] + f32(second_shift)[:, None] * col
    grad_second_gain = jnp.sum(f32(w_inner) * sum_i[:128], axis=1)
    grad_second_shift = jnp.sum(f32(w_inner) * col, axis=1)
    grad_inner_bias = lax.dynamic_slice(col, (me * 512,), (512,))
    grad_outer_bias = lax.dynamic_slice(sum_i[129], (me * 128,), (128,))
    colp = sum_p[128]
    grad_p = f32(first_gain)[:, None] * sum_p[:128] + f32(first_shift)[:, None] * colp
    wp = f32(own[:128])
    grad_first_gain = jnp.sum(wp * sum_p[:128], axis=1)
    grad_first_shift = jnp.sum(wp * colp, axis=1)
    return (
        output, grad_tokens, grad_first_gain, grad_first_shift,
        grad_p[:, :512], grad_p[:, 512:1024], grad_p[:, 1024:1536], grad_p[:, 1536:],
        sum_o, grad_second_gain, grad_second_shift, grad_inner, grad_inner_bias, sum_u.T, grad_outer_bias,
    )


def solution(mesh):
    row, vec, mat = P(("dp", "fsdp"), None), P("fsdp"), P("fsdp", None)
    return jax.shard_map(
        functools.partial(per_device, mesh.shape["dp"]),
        mesh=mesh,
        in_specs=(row, vec, vec, mat, mat, mat, mat, mat, vec, vec, mat, vec, mat, vec, row),
        out_specs=(row, row, vec, vec, mat, mat, mat, mat, mat, vec, vec, mat, vec, mat, vec),
        check_vma=False,
    )
```

```python
import functools

import jax
import jax.numpy as jnp
from jax import lax
from jax.experimental import pallas as pl
from jax.experimental.pallas import tpu as pltpu
from jax.sharding import PartitionSpec as P

F32 = jnp.float32
BF16 = jnp.bfloat16
PAIR = 128
PAIRS = range(4)
SCALE = 64 ** -0.5
CHUNK = 128
UNROLL = 2
JOIN = 4
ROWS = 512
EPS = 1e-5
WEIGHT = 10**9
MASKS = (0, 2, 1, 3)
VM = pl.BlockSpec(memory_space=pltpu.VMEM)
SM = pl.BlockSpec(memory_space=pltpu.SMEM)
ANY = pl.BlockSpec(memory_space=pl.ANY)


def mm(a, b):
    return lax.dot_general(a, b, (((1,), (0,)), ((), ())), preferred_element_type=F32)


def mm_nt(a, b):
    return lax.dot_general(a, b, (((1,), (1,)), ((), ())), preferred_element_type=F32)


def mm_tn(a, b):
    return lax.dot_general(a, b, (((0,), (0,)), ((), ())), preferred_element_type=F32)


def shape(dims, dtype=BF16):
    return jax.ShapeDtypeStruct(dims, dtype)


class Clock:
    def __init__(self, me):
        self.me = me
        self.token = jnp.zeros((8, 128), F32)

    def sync(self, *values):
        self.token, values = lax.optimization_barrier((self.token, values))
        return values if len(values) > 1 else values[0]


def call(clock, kernel, name, outs, args, scratch=(), limit=8, outside=(), aliases=None):
    n_in, n_out = len(args), len(outs)

    def body(me, token, *refs):
        outs_at = n_in + n_out
        refs[outs_at][...] = token[...]
        kernel(me, *refs[:outs_at], *refs[outs_at + 1 :])

    place = lambda k, o: (pltpu.HBM if k in outside else pltpu.VMEM)(o.shape, o.dtype)
    *results, clock.token = pl.pallas_call(
        body,
        in_specs=[SM] + [VM] * (n_in + 1),
        out_specs=[ANY if k in outside else VM for k in range(n_out)] + [VM],
        out_shape=[place(k, o) for k, o in enumerate(outs)] + [pltpu.VMEM((8, 128), F32)],
        scratch_shapes=list(scratch),
        input_output_aliases={i + 2: o for i, o in (aliases or {}).items()},
        compiler_params=pltpu.CompilerParams(vmem_limit_bytes=limit << 20),
        cost_estimate=pl.CostEstimate(flops=WEIGHT, bytes_accessed=1 << 10, transcendentals=0),
        name=name,
    )(clock.me, *[pltpu.with_memory_space_constraint(a, pltpu.VMEM) for a in (clock.token, *args)])
    return results


def blocks_of(me):
    return [me ^ mask for mask in MASKS]


def wide(blocks, width):
    return [pl.ds(pl.multiple_of(b * width, width), width) for b in blocks]


def take_blocks(ref, rows, blocks, width):
    return jnp.concatenate([ref[rows, cols] for cols in wide(blocks, width)], axis=1)


def put_blocks(ref, rows, values, blocks, width):
    for i, cols in enumerate(wide(blocks, width)):
        ref[rows, cols] = values[:, i * width : (i + 1) * width]


def stack(refs, cols=slice(None)):
    return jnp.concatenate([r[:, cols] for r in refs], axis=0)


def vector(vecs, start, width):
    return jnp.concatenate([r[0:1, start : start + width] for r in vecs], axis=1).astype(F32)


def row_loop(T, body):
    def step(c, _):
        body(pl.ds(pl.multiple_of(c * ROWS, ROWS), ROWS))
        return 0

    lax.fori_loop(0, T // ROWS, step, 0)


def stats(x):
    mean = jnp.mean(x, axis=1, keepdims=True)
    centred = x - mean
    inv = lax.rsqrt(jnp.mean(centred * centred, axis=1, keepdims=True) + EPS)
    return centred * inv, inv


def norm_back(grad, normed, inv):
    return inv * (grad - jnp.mean(grad, axis=1, keepdims=True) - normed * jnp.mean(grad * normed, axis=1, keepdims=True))


def vectors_kernel(*refs):
    parts, out, bufs, sems = refs[:6], refs[6], refs[7:13], refs[13]
    copies = [pltpu.make_async_copy(src, dst, sems.at[i]) for i, (src, dst) in enumerate(zip(parts, bufs))]
    for copy in copies:
        copy.start()
    for copy in copies:
        copy.wait()
    vec = jnp.concatenate([b[...].reshape(1, -1).astype(F32) for b in bufs], axis=1)
    out[...] = jnp.broadcast_to(vec, out.shape).astype(BF16)


def pack_vectors(*parts):
    return pl.pallas_call(
        vectors_kernel,
        in_specs=[ANY] * len(parts),
        out_specs=VM,
        out_shape=shape((16, sum(p.shape[0] for p in parts))),
        scratch_shapes=[pltpu.VMEM(p.shape, BF16) for p in parts] + [pltpu.SemaphoreType.DMA((len(parts),))],
        compiler_params=pltpu.CompilerParams(vmem_limit_bytes=1 << 20),
        cost_estimate=pl.CostEstimate(flops=WEIGHT, bytes_accessed=1 << 10, transcendentals=0),
        name="pack_vectors",
    )(*parts)


def first_norm_kernel(me_ref, tokens, n1, n1_low, scr):
    blocks = blocks_of(me_ref[0])

    def body(rows):
        n, _ = stats(tokens[rows, :].astype(F32))
        scr[...] = n
        n = take_blocks(scr, slice(None), blocks, 128)
        n1[rows, :] = n
        n1_low[rows, :] = n.astype(BF16)

    row_loop(tokens.shape[0], body)


def first_norm(clock, tokens):
    T = tokens.shape[0]
    return call(clock, first_norm_kernel, "first_norm", [shape((T, 512), F32), shape((T, 512))], [tokens], [pltpu.VMEM((ROWS, 512), F32)])


def project_kernel(_, n1, *refs):
    weights, vecs, (qkvf, a1) = refs[:16], refs[16:20], refs[20:]
    a1[...] = (n1[...] * vector(vecs, 0, 128) + vector(vecs, 128, 128)).astype(BF16)
    for n in range(4):
        out = mm(a1[...], stack(weights[4 * n : 4 * n + 4]))
        qkvf[:, 512 * n : 512 * (n + 1)] = (jnp.exp(out) if n == 3 else out).astype(BF16)


def flat(weights):
    return [w for group in weights for w in group]


def project(clock, n1, weights, vecs):
    T = n1.shape[0]
    return call(clock, project_kernel, "project", [shape((T, 2048))], [n1, *flat(weights), *vecs], [pltpu.VMEM((T, 512), BF16)])[0]


def left_half(rows):
    return lax.broadcasted_iota(jnp.int32, (rows, PAIR), 1) < 64


def split_pair(x, left):
    zero = jnp.zeros((), x.dtype)
    return jnp.concatenate((jnp.where(left, x, zero), jnp.where(left, zero, x)), axis=0)


def same_head():
    r = lax.broadcasted_iota(jnp.int32, (PAIR, PAIR), 0) < 64
    c = lax.broadcasted_iota(jnp.int32, (PAIR, PAIR), 1) < 64
    return r == c


def causal_pair(rows):
    r = lax.broadcasted_iota(jnp.int32, (rows, 2 * rows), 0)
    c = lax.broadcasted_iota(jnp.int32, (rows, 2 * rows), 1)
    return r >= jnp.where(c >= rows, c - rows, c)


def triangle(rows):
    return lax.broadcasted_iota(jnp.int32, (rows, rows), 0) >= lax.broadcasted_iota(jnp.int32, (rows, rows), 1)


def half_reduce(x, left, fn, fill):
    a = fn(jnp.where(left, x, fill), axis=1, keepdims=True)
    b = fn(jnp.where(left, fill, x), axis=1, keepdims=True)
    return jnp.where(left, a, b)


def pair_of(j):
    return slice(PAIR * j, PAIR * (j + 1))


def a_of(j):
    return slice(256 * j, 256 * (j + 1))


def b_of(j):
    return slice(1024 + 256 * j, 1024 + 256 * (j + 1))


def s_of(j):
    return slice(2048 + PAIR * j, 2048 + PAIR * (j + 1))


def g_of(j):
    return slice(2560 + PAIR * j, 2560 + PAIR * (j + 1))


KEPT = 3072


def chunk_rows(c):
    return pl.ds(pl.multiple_of(c * CHUNK, CHUNK), CHUNK)


def forward_kernel(_, qkvf, mixed, kept, states, carry_out, s1, s2, carry):
    C = CHUNK
    s1[...] = jnp.zeros_like(s1)
    s2[...] = jnp.zeros_like(s2)
    carry[...] = jnp.zeros_like(carry)
    left = left_half(C)
    causal = causal_pair(C)
    same = same_head()
    lower = triangle(C).astype(BF16)
    zero = jnp.zeros((), BF16)

    def step(c, _):
        rows = chunk_rows(c)
        part = lambda n, j: qkvf[rows, 512 * n + PAIR * j : 512 * n + PAIR * (j + 1)]
        raw = [mm_nt(part(0, j), split_pair(part(1, j), left)) for j in PAIRS]
        carry_out[c] = carry[...]
        denom = mm(lower, qkvf[rows, 1536:2048]) + carry[0:1, :]
        carry[0:1, :] = denom[C - 1 :, :]
        rden_all = 1.0 / denom
        f2 = [split_pair(part(3, j), left) for j in PAIRS]
        numer = []
        for j in PAIRS:
            a2 = jnp.where(causal, raw[j].astype(BF16), zero)
            kept[rows, a_of(j)] = a2
            s1b = s1[j].astype(BF16)
            states[c, :, pair_of(j)] = s1b
            numer.append(mm(a2, f2[j]) + mm(part(0, j), s1b))
        g = []
        for j in PAIRS:
            rden = rden_all[:, pair_of(j)]
            s = numer[j] * rden * SCALE
            kept[rows, s_of(j)] = s.astype(BF16)
            e = jnp.exp(s - half_reduce(s, left, jnp.max, -jnp.inf))
            p = e / half_reduce(e, left, jnp.sum, 0.0)
            g.append((p * rden).astype(BF16))
            kept[rows, g_of(j)] = g[j]
        raw = [mm_nt(g[j], f2[j]) for j in PAIRS]
        for j in PAIRS:
            b2 = jnp.where(causal, raw[j].astype(BF16), zero)
            kept[rows, b_of(j)] = b2
            s2b = s2[j].astype(BF16)
            states[c, :, pair_of(4 + j)] = s2b
            o = mm(b2, split_pair(part(2, j), left)) + mm(g[j], s2b)
            mixed[rows, pair_of(j)] = o.astype(BF16)
        for j in PAIRS:
            s1[j] += jnp.where(same, mm_tn(part(1, j), part(3, j)), 0.0)
            s2[j] += jnp.where(same, mm_tn(part(3, j), part(2, j)), 0.0)
        return 0

    lax.fori_loop(0, qkvf.shape[0] // C, step, 0, unroll=UNROLL)


def state_scratch():
    return [pltpu.VMEM((4, PAIR, PAIR), F32), pltpu.VMEM((4, PAIR, PAIR), F32), pltpu.VMEM((8, 512), F32)]


def attention_forward(clock, qkvf):
    T = qkvf.shape[0]
    n = T // CHUNK
    outs = [shape((T, 512)), shape((T, KEPT)), shape((n, PAIR, 1024)), shape((n, 8, 512), F32)]
    return call(clock, forward_kernel, "attention_forward", outs, [qkvf], state_scratch())


def backward_kernel(first, count, last, _, qkvf, kept, states, carry_in, do_in, *refs):
    C = CHUNK
    r1, r2, carry = refs[-3:]
    begins, (grad, *ends) = (refs[:3], refs[3:-3]) if first < last else ((), refs[:-3])
    for ref, old in zip((r1, r2, carry), begins or (None,) * 3):
        ref[...] = jnp.zeros_like(ref) if old is None else old[...]
    left = left_half(C)
    causal = causal_pair(C)
    same = same_head()
    lower = triangle(C).astype(BF16)
    upper = lower.T
    upper2 = jnp.concatenate((upper, upper), axis=1)
    zero = jnp.zeros((), BF16)

    def step(t, _):
        c = first - t
        rows = chunk_rows(c)
        here = chunk_rows(count - 1 - t)
        part = lambda n, j: qkvf[rows, 512 * n + PAIR * j : 512 * n + PAIR * (j + 1)]
        do = [do_in[rows, pair_of(j)] for j in PAIRS]
        denoms = mm(lower, qkvf[rows, 1536:2048]) + carry_in[c][0:1, :]
        s1b = [states[c, :, pair_of(j)] for j in PAIRS]
        s2b = [states[c, :, pair_of(4 + j)] for j in PAIRS]
        r1b = [r1[j].astype(BF16) for j in PAIRS]
        r2b = [r2[j].astype(BF16) for j in PAIRS]
        g = [kept[rows, g_of(j)] for j in PAIRS]
        raw = [mm_nt(do[j], split_pair(part(2, j), left)) for j in PAIRS]
        f2 = [split_pair(part(3, j), left) for j in PAIRS]
        db2, dg, dn, dd = [], [], [], []
        for j in PAIRS:
            db2.append(jnp.where(causal, raw[j].astype(BF16), zero))
            dg.append(mm(db2[j], f2[j]) + mm_nt(do[j], s2b[j]))
        for j in PAIRS:
            dv2 = mm_tn(kept[rows, b_of(j)], do[j])
            dv = jnp.where(left, dv2[:C], dv2[C:]) + mm(part(3, j), r2b[j])
            grad[here, 1024 + PAIR * j : 1024 + PAIR * (j + 1)] = dv.astype(BF16)
        for j in PAIRS:
            denom = denoms[:, pair_of(j)]
            rden = 1.0 / denom
            p = g[j].astype(F32) * denom
            dpp = dg[j] * rden * p
            ds = dpp - p * half_reduce(dpp, left, jnp.sum, 0.0)
            dd.append(-(dpp + ds * kept[rows, s_of(j)].astype(F32)) * rden)
            dn.append((ds * SCALE * rden).astype(BF16))
        raw = [mm_nt(dn[j], f2[j]) for j in PAIRS]
        for j in PAIRS:
            df2 = mm_tn(db2[j], g[j]) + mm_tn(kept[rows, a_of(j)], dn[j])
            hi = dd[j].astype(BF16)
            lo = (dd[j] - hi.astype(F32)).astype(BF16)
            df = jnp.where(left, df2[:C], df2[C:]) + mm_nt(part(2, j), r2b[j]) + mm(part(1, j), r1b[j])
            df = df + mm(upper2, jnp.concatenate((hi, lo), axis=0)) + carry[0:1, pair_of(j)]
            grad[here, 1536 + PAIR * j : 1536 + PAIR * (j + 1)] = (df * part(3, j).astype(F32)).astype(BF16)
            carry[0:1, pair_of(j)] += jnp.sum(dd[j], axis=0, keepdims=True)
        for j in PAIRS:
            da2 = jnp.where(causal, raw[j].astype(BF16), zero)
            dq = mm(da2, split_pair(part(1, j), left)) + mm_nt(dn[j], s1b[j])
            grad[here, pair_of(j)] = dq.astype(BF16)
            dk2 = mm_tn(da2, part(0, j))
            dk = jnp.where(left, dk2[:C], dk2[C:]) + mm_nt(part(3, j), r1b[j])
            grad[here, 512 + PAIR * j : 512 + PAIR * (j + 1)] = dk.astype(BF16)
        for j in PAIRS:
            r1[j] += jnp.where(same, mm_tn(part(0, j), dn[j]), 0.0)
            r2[j] += jnp.where(same, mm_tn(g[j], do[j]), 0.0)
        return 0

    lax.fori_loop(0, count, step, 0, unroll=UNROLL)
    for ref, end in zip((r1, r2, carry), ends):
        end[...] = ref[...]


def attention_backward(clock, qkvf, saved, d_o, first, count, states=()):
    rows = count * CHUNK
    outs = [shape((rows, 2048))]
    if first - count >= 0:
        outs += [shape((4, PAIR, PAIR), F32), shape((4, PAIR, PAIR), F32), shape((8, 512), F32)]
    kernel = functools.partial(backward_kernel, first, count, qkvf.shape[0] // CHUNK - 1)
    return call(clock, kernel, "attention_backward", outs, [qkvf, *saved, d_o, *states], state_scratch())


def gelu_parts(v):
    c = 0.7978845608028654
    k = c * 0.044715
    v2 = v * v
    half = 0.5 * jnp.tanh(v * (c + k * v2)) + 0.5
    act = v * half
    return act, half + act * (1.0 - half) * (2 * c + (6 * k) * v2)


def ffn_inner_kernel(me_ref, tokens, mixed, *refs):
    wo, wi, vs = refs[:4], refs[4:8], refs[8:12]
    resid_out, n2_out, r2_out, act_out, slope_out, scr = refs[12:]
    blocks = blocks_of(me_ref[0])
    gain, shift = vector(vs, 256, 128), vector(vs, 384, 128)
    cols = wide(blocks, 512)

    def body(rows):
        resid = tokens[rows, :].astype(F32) + mm(take_blocks(mixed, rows, blocks, 128), stack(wo))
        resid_out[rows, :] = resid
        n2, r2 = stats(resid)
        scr[...] = n2
        n2 = take_blocks(scr, slice(None), blocks, 128)
        n2_out[rows, :] = n2.astype(BF16)
        r2_out[rows, :] = jnp.broadcast_to(r2, (ROWS, 128))
        a2 = (n2 * gain + shift).astype(BF16)
        inner = mm(a2, stack(wi, cols[0]))
        for i in range(4):
            after = mm(a2, stack(wi, cols[i + 1])) if i < 3 else None
            act, slope = gelu_parts(inner + vs[i][0:1, 640:1152].astype(F32))
            act_out[rows, 512 * i : 512 * (i + 1)] = act.astype(BF16)
            slope_out[rows, cols[i]] = slope.astype(BF16)
            inner = after

    row_loop(tokens.shape[0], body)


def ffn_inner(clock, tokens, mixed, wo, wi, vecs):
    T = tokens.shape[0]
    outs = [shape((T, 512), F32), shape((T, 512)), shape((T, 128), F32), shape((T, 2048)), shape((T, 2048))]
    return call(clock, ffn_inner_kernel, "ffn_inner", outs, [tokens, mixed, *wo, *wi, *vecs], [pltpu.VMEM((ROWS, 512), F32)])


def outer_grad_kernel(_, act, dy, keep, send):
    for i in range(4):
        out = mm_tn(act[:, 512 * i : 512 * (i + 1)], dy[...]).astype(BF16)
        (keep if i < 2 else send)[i % 2] = out


def outer_grad(clock, act, dy):
    return call(clock, outer_grad_kernel, "outer_grad", [shape((2, 512, 512))] * 2, [act, dy])


def ffn_outer_kernel(me_ref, resid, act, *refs):
    wu, vs, (out, bias, result, sem) = refs[:4], refs[4:8], refs[8:]
    put_blocks(bias, slice(None), jnp.broadcast_to(vector(vs, 512, 128), (8, 512)), blocks_of(me_ref[0]), 128)
    total = mm(act[...], stack(wu))
    result[...] = (total + resid[...] + bias[0:1, :]).astype(BF16)
    copy = pltpu.make_async_copy(result, out, sem)
    copy.start()
    copy.wait()


def ffn_outer(clock, resid, act, wu, vecs):
    scratch = [pltpu.VMEM((8, 512), F32), pltpu.VMEM(resid.shape, BF16), pltpu.SemaphoreType.DMA]
    return call(clock, ffn_outer_kernel, "ffn_outer", [shape(resid.shape)], [resid, act, *wu, *vecs], scratch, outside=(0,))[0]


def inner_back_kernel(me_ref, dy, slope, u0, u1, u2, u3, din, sums):
    cols = wide(blocks_of(me_ref[0]), 512)
    sums[...] = jnp.zeros_like(sums)
    sums[1:2, 0:512] = jnp.sum(dy[...].astype(F32), axis=0, keepdims=True)
    for i, u in enumerate((u0, u1, u2, u3)):
        d = (mm_nt(dy[...], u[...]) * slope[:, cols[i]].astype(F32)).astype(BF16)
        din[:, cols[i]] = d
        sums[0:1, cols[i]] = jnp.sum(d.astype(F32), axis=0, keepdims=True)


def inner_back(clock, dy, slope, wu):
    T = dy.shape[0]
    return call(clock, inner_back_kernel, "inner_back", [shape((T, 2048)), shape((8, 2048), F32)], [dy, slope, *wu], aliases={1: 0})


def inner_grad_kernel(_, n2, din, sums, keep, send):
    tail = jnp.concatenate((sums[...], jnp.zeros_like(sums)), axis=0).astype(BF16)
    for i in range(4):
        dest = keep if i < 2 else send
        dest[i % 2, 0:128, :] = mm_tn(n2[:, 128 * i : 128 * (i + 1)], din[...]).astype(BF16)
        dest[i % 2, 128:144, :] = tail


def inner_grad(clock, n2, din, sums):
    return call(clock, inner_grad_kernel, "inner_grad", [shape((2, 144, 2048))] * 2, [n2, din, sums])


def resid_back_kernel(me_ref, dy, n2, r2, din, *refs):
    wo, wi, vs = refs[:4], refs[4:8], refs[8:12]
    dres_out, do_out, scr = refs[12:]
    blocks = blocks_of(me_ref[0])
    gain = vector(vs, 256, 128)

    def body(rows):
        da2 = mm_nt(din[rows, :], stack(wi))
        put_blocks(scr, slice(None), norm_back(da2 * gain, n2[rows, :].astype(F32), r2[rows, 0:1]), blocks, 128)
        dres = dy[rows, :].astype(F32) + scr[...]
        dres_out[rows, :] = dres
        d_o = mm_nt(dres.astype(BF16), stack(wo))
        put_blocks(do_out, rows, d_o.astype(BF16), blocks, 128)

    row_loop(dy.shape[0], body)


def resid_back(clock, dy, n2, r2, din, wo, wi, vecs):
    T = dy.shape[0]
    return call(clock, resid_back_kernel, "resid_back", [shape((T, 512), F32), shape((T, 512))], [dy, n2, r2, din, *wo, *wi, *vecs], [pltpu.VMEM((ROWS, 512), F32)])


def project_grad_kernel(start, width, extra, me_ref, n1, early, late, *refs):
    keep, send = refs[-2:]
    cols = slice(start, start + width)
    half = early.shape[0]
    out = mm_tn(n1[0:half, :], early[:, cols]) + mm_tn(n1[half:, :], late[:, cols])
    out = out.astype(BF16)
    total = sum(jnp.sum(r[:, cols].astype(F32), axis=0, keepdims=True) for r in (early, late))
    tail = jnp.broadcast_to(total, (16, width)).astype(BF16)
    for i, block in enumerate(wide(blocks_of(me_ref[0]), 128)):
        dest = keep if i < 2 else send
        dest[i % 2, 0:128, 0:width] = out[128 * i : 128 * (i + 1)]
        dest[i % 2, 128:144, 0:width] = tail
        if extra:
            mixed, dres = refs[:2]
            m = mm_tn(mixed[:, block], dres[...].astype(BF16))
            dest[i % 2, 0:128, width:] = m.astype(BF16)
            dest[i % 2, 128:144, width:] = jnp.zeros((16, extra), BF16)


def project_grad(clock, n1, early, late, start, width, *more):
    extra = 512 if more else 0
    kernel = functools.partial(project_grad_kernel, start, width, extra)
    return call(clock, kernel, "project_grad", [shape((2, 144, width + extra))] * 2, [n1, early, late, *more])


def input_grad_kernel(me_ref, tokens, early, late, dres, *refs):
    weights, vecs, (out, scr, result, sems) = refs[:16], refs[16:20], refs[20:]
    blocks = blocks_of(me_ref[0])
    gain = vector(vecs, 0, 128)
    for h, d in enumerate((early, late)):
        rows = slice(ROWS * h, ROWS * (h + 1))
        e = mm_nt(d[:, 0:512], stack(weights[0:4]))
        for n in range(1, 4):
            e = e + mm_nt(d[:, 512 * n : 512 * (n + 1)], stack(weights[4 * n : 4 * n + 4]))
        n1, r1 = stats(tokens[rows, :].astype(F32))
        scr[...] = n1
        put_blocks(scr, slice(None), norm_back(e * gain, take_blocks(scr, slice(None), blocks, 128), r1), blocks, 128)
        result[rows, :] = (dres[rows, :] + scr[...]).astype(BF16)
        pltpu.make_async_copy(result.at[rows, :], out.at[rows, :], sems.at[h]).start()
    for h in range(2):
        rows = slice(ROWS * h, ROWS * (h + 1))
        pltpu.make_async_copy(result.at[rows, :], out.at[rows, :], sems.at[h]).wait()


def input_grad(clock, tokens, early, late, dres, weights, vecs):
    args = [tokens, early, late, dres, *flat(weights), *vecs]
    scratch = [pltpu.VMEM((ROWS, 512), F32), pltpu.VMEM(dres.shape, BF16), pltpu.SemaphoreType.DMA((2,))]
    return call(clock, input_grad_kernel, "input_grad", [shape(dres.shape)], args, scratch, outside=(0,))[0]


def exchange(value, axis, size, mask):
    return lax.ppermute(value, axis, [(i, i ^ mask) for i in range(size)])


def over_x(value):
    return exchange(value, "fsdp", 4, 2)


def over_core(value):
    return exchange(value, "fsdp", 4, 1)


def add(a, b):
    return a.astype(F32) + b.astype(F32)


def half_at(bit, width):
    return pl.ds(pl.multiple_of(bit * (width // 2), width // 2), width // 2)


def join_core_kernel(_, keep, got, mine, send):
    mine[...] = add(keep[0], got[0]).astype(BF16)
    send[...] = add(keep[1], got[1]).astype(BF16)


def join_kernel(split, place, me_ref, keep, got, *refs):
    if place is None:
        total = add(keep[...], got[...]).astype(BF16)
    if split is None:
        out = refs[0]
        if place is None:
            out[...] = total
        else:
            bit = lax.rem(lax.div(me_ref[1], place), 2)
            out[:, half_at(bit, out.shape[1])] = keep[...]
            out[:, half_at(1 - bit, out.shape[1])] = got[...]
    else:
        mine, send, whole = refs
        bit = lax.rem(lax.div(me_ref[1], split), 2)
        whole[...] = total
        mine[...] = whole[:, half_at(bit, whole.shape[1])]
        send[...] = whole[:, half_at(1 - bit, whole.shape[1])]


class Chain:
    def __init__(self, clock, dp, halved, pair):
        self.clock, self.dp = clock, dp
        masks = [1 << k for k in range(dp.bit_length() - 1)]
        self.todo = [("core", 0), ("x", 0)] + [("half" if m in halved else "all", m) for m in masks] + [("beside", m) for m in reversed(masks) if m in halved]
        self.keep, self.send = pair
        self.busy = True
        self.launch()

    def launch(self):
        self.kind, self.mask = self.todo.pop(0)
        if self.kind == "core":
            self.got = over_core(self.send)
        elif self.kind == "x":
            self.got = over_x(self.send)
        else:
            self.got = exchange(self.send, "dp", self.dp, self.mask)

    def step(self):
        rows, width = self.keep.shape[-2:]
        if self.kind == "core":
            self.keep, self.send = call(self.clock, join_core_kernel, "join_core", [shape((rows, width))] * 2, [self.keep, self.got], limit=JOIN)
        else:
            split = self.todo[0][1] if self.todo and self.todo[0][0] == "half" else None
            place = self.mask if self.kind == "beside" else None
            kernel = functools.partial(join_kernel, split, place)
            if split is None:
                outs, scratch = [shape((rows, 2 * width if place else width))], []
            else:
                outs, scratch = [shape((rows, width // 2))] * 2, [pltpu.VMEM((rows, width), BF16)]
            out = call(self.clock, kernel, "join", outs, [self.keep, self.got], scratch, limit=JOIN)
            self.keep, self.send = out if split else (out[0], out[0])
        self.busy = bool(self.todo)
        if self.busy:
            self.launch()


def steps(*chains):
    for chain in chains:
        chain.step()


def column(row):
    r = lax.broadcasted_iota(jnp.int32, (128, 128), 0)
    c = lax.broadcasted_iota(jnp.int32, (128, 128), 1)
    return jnp.sum(jnp.where(r == c, row, 0.0), axis=1, keepdims=True)


def as_row(col):
    r = lax.broadcasted_iota(jnp.int32, (128, 128), 0)
    c = lax.broadcasted_iota(jnp.int32, (128, 128), 1)
    return jnp.sum(jnp.where(r == c, col, 0.0), axis=0, keepdims=True)


def send_out(pairs, sems):
    copies = [pltpu.make_async_copy(src, dst, sems.at[k]) for k, (src, dst) in enumerate(pairs)]
    for copy in copies:
        copy.start()
    for copy in copies:
        copy.wait()


def finish_outer_kernel(_, u, out, buf, sems):
    buf[...] = u[...].astype(F32)
    send_out([(buf, out)], sems)


def finish_outer(clock, u):
    return call(clock, finish_outer_kernel, "finish_outer", [shape(u.shape, F32)], [u], [pltpu.VMEM(u.shape, F32), pltpu.SemaphoreType.DMA((1,))], limit=JOIN, outside=(0,))[0]


def finish_inner_kernel(me_ref, total, w, vec, out, gain_out, shift_out, inner_out, outer_out, buf, small, sems):
    gain, shift = (column(vec[0:1, k : k + 128].astype(F32)) for k in (256, 384))
    m = total[0:128, :].astype(F32)
    tail = total[128:144, :].astype(F32)
    buf[...] = gain * m + shift * tail[0:1, :]
    wf = w[...].astype(F32)
    small[0:1, 0:128] = as_row(jnp.sum(wf * m, axis=1, keepdims=True))
    small[1:2, 0:128] = as_row(jnp.sum(wf * tail[0:1, :], axis=1, keepdims=True))
    me = me_ref[0]
    small[2:3, :] = total[128:144, pl.ds(pl.multiple_of(me * 512, 512), 512)].astype(F32)[0:1, :]
    small[3:4, 0:128] = total[128:144, pl.ds(pl.multiple_of(me * 128, 128), 128)].astype(F32)[1:2, :]
    gain_out[...] = small[0:1, 0:128]
    shift_out[...] = small[1:2, 0:128]
    inner_out[...] = small[2:3, :]
    outer_out[...] = small[3:4, 0:128]
    send_out([(buf, out)], sems)


def finish_inner(clock, total, w, vec):
    outs = [shape((128, 2048), F32), shape((1, 128), F32), shape((1, 128), F32), shape((1, 512), F32), shape((1, 128), F32)]
    scratch = [pltpu.VMEM((128, 2048), F32), pltpu.VMEM((8, 512), F32), pltpu.SemaphoreType.DMA((1,))]
    return call(clock, finish_inner_kernel, "finish_inner", outs, [total, w, vec], scratch, limit=JOIN, outside=(0,))


def finish_project_kernel(more, _, total, w0, w1, vec, *refs):
    before, refs = refs[:1], refs[1:]
    out0, out1, *rest = refs
    sums = rest[1] if more else rest[0]
    buf, sems = rest[-2:]
    gain, shift = (column(vec[0:1, k : k + 128].astype(F32)) for k in (0, 128))
    m = total[0:128, 0:1024].astype(F32)
    tail = total[128:144, 0:1024].astype(F32)[0:1, :]
    buf[:, 0:1024] = gain * m + shift * tail
    w = jnp.concatenate((w0[...], w1[...]), axis=1).astype(F32)
    sums[0:1, :] = before[0][0:1, :] + as_row(jnp.sum(w * m, axis=1, keepdims=True))
    sums[1:2, :] = before[0][1:2, :] + as_row(jnp.sum(w * tail, axis=1, keepdims=True))
    pairs = [(buf.at[:, 0:512], out0), (buf.at[:, 512:1024], out1)]
    if more:
        buf[:, 1024:1536] = total[0:128, 1024:1536].astype(F32)
        pairs.append((buf.at[:, 1024:1536], rest[0]))
    send_out(pairs, sems)


def finish_project(clock, total, w0, w1, vec, before):
    more = total.shape[1] > 1024
    n = 3 if more else 2
    outs = [shape((128, 512), F32)] * n + [shape((8, 128), F32)]
    scratch = [pltpu.VMEM((128, 512 * n), F32), pltpu.SemaphoreType.DMA((n,))]
    return call(clock, functools.partial(finish_project_kernel, more), "finish_project", outs, [total, w0, w1, vec, before], scratch, limit=JOIN, outside=range(n))


def per_device(dp, tokens, first_gain, first_shift, w_query, w_key, w_value, w_control, w_output, second_gain, second_shift, w_inner, inner_bias, w_outer, outer_bias, cotangent):
    me = lax.axis_index("fsdp").astype(jnp.int32)
    place = lax.axis_index("dp").astype(jnp.int32)
    clock = Clock(jnp.stack((me, place)))
    own = [w_query, w_key, w_value, w_control, pack_vectors(first_gain, first_shift, second_gain, second_shift, outer_bias, inner_bias)]
    across = [over_x(v) for v in own]
    own_core = [over_core(v) for v in own]
    n1, n1_low = first_norm(clock, tokens)
    *across, w_output, w_inner, w_outer = clock.sync(*across, w_output, w_inner, w_outer)
    across_core = [over_core(v) for v in across]
    wo_x, wi_x = over_x(w_output), over_x(w_inner)
    *weights, vecs = [list(group) for group in zip(own, across, own_core, across_core)]
    qkvf = project(clock, n1, weights, vecs)
    wo_x, w_output, w_inner = clock.sync(wo_x, w_output, w_inner)
    wo = [w_output, wo_x, over_core(w_output), over_core(wo_x)]
    wi_c = over_core(w_inner)
    mixed, *saved = attention_forward(clock, qkvf)
    wi_x, w_outer = clock.sync(wi_x, w_outer)
    wi = [w_inner, wi_x, wi_c, over_core(wi_x)]
    wu_x, wu_c = over_x(w_outer), over_core(w_outer)
    resid, n2, r2, act, slope = ffn_inner(clock, tokens, mixed, wo, wi, vecs)
    u = Chain(clock, dp, (1, 2), outer_grad(clock, act, cotangent))
    wu_x = clock.sync(wu_x)
    wu = [w_outer, wu_x, wu_c, over_core(wu_x)]
    din, sums = inner_back(clock, cotangent, slope, wu)
    u.step()
    i = Chain(clock, dp, (1, 2), inner_grad(clock, n2, din, sums))
    dres, d_o = resid_back(clock, cotangent, n2, r2, din, wo, wi, vecs)
    i.step()
    early = attention_backward(clock, qkvf, saved, d_o, 7, 4)
    u.step()
    late = attention_backward(clock, qkvf, saved, d_o, 3, 4, early[1:])
    u.step()
    a = Chain(clock, dp, (1,), project_grad(clock, n1_low, late[0], early[0], 0, 1024, mixed, dres))
    b = Chain(clock, dp, (1,), project_grad(clock, n1_low, late[0], early[0], 1024, 1024))
    a.step()
    i.step()
    u.step()
    b.step()
    grad_tokens = input_grad(clock, tokens, late[0], early[0], dres, weights, vecs)
    i.step()
    u.step()
    a.step()
    output = ffn_outer(clock, resid, act, wu, vecs)
    chains = [a, b, i, u]
    while any(c.busy for c in chains):
        for c in chains:
            if c.busy:
                c.step()
    grad_outer = finish_outer(clock, u.keep)
    grad_inner, *vectors = finish_inner(clock, i.keep, w_inner, vecs[0])
    grad_query, grad_key, grad_output, before = finish_project(clock, a.keep, w_query, w_key, vecs[0], jnp.zeros((8, 128), F32))
    grad_value, grad_control, before = finish_project(clock, b.keep, w_value, w_control, vecs[0], before)
    second_gain_grad, second_shift_grad, inner_bias_grad, outer_bias_grad = [v.reshape(-1) for v in vectors]
    return (
        output, grad_tokens, before[0], before[1], grad_query, grad_key, grad_value, grad_control,
        grad_output, second_gain_grad, second_shift_grad, grad_inner, inner_bias_grad, grad_outer, outer_bias_grad,
    )


def solution(mesh):
    row, vec, mat = P(("dp", "fsdp"), None), P("fsdp"), P("fsdp", None)
    return jax.shard_map(
        functools.partial(per_device, mesh.shape["dp"]),
        mesh=mesh,
        in_specs=(row, vec, vec, mat, mat, mat, mat, mat, vec, vec, mat, vec, mat, vec, row),
        out_specs=(row, row, vec, vec, mat, mat, mat, mat, mat, vec, vec, mat, vec, mat, vec),
        check_vma=False,
    )
```

```python
import functools

import jax
import jax.numpy as jnp
from jax import lax
from jax.experimental import pallas as pl
from jax.experimental.pallas import tpu as pltpu
from jax.sharding import PartitionSpec as P

F32 = jnp.float32
BF16 = jnp.bfloat16
PAIR = 128
PAIRS = range(4)
SCALE = 64 ** -0.5
CHUNK = 128
UNROLL = 2
JOIN = 4
ROWS = 512
EPS = 1e-5
WEIGHT = 1000
MASKS = (0, 2, 1, 3)
VM = pl.BlockSpec(memory_space=pltpu.VMEM)
SM = pl.BlockSpec(memory_space=pltpu.SMEM)
ANY = pl.BlockSpec(memory_space=pl.ANY)


def mm(a, b):
    return lax.dot_general(a, b, (((1,), (0,)), ((), ())), preferred_element_type=F32)


def mm_nt(a, b):
    return lax.dot_general(a, b, (((1,), (1,)), ((), ())), preferred_element_type=F32)


def mm_tn(a, b):
    return lax.dot_general(a, b, (((0,), (0,)), ((), ())), preferred_element_type=F32)


def shape(dims, dtype=BF16):
    return jax.ShapeDtypeStruct(dims, dtype)


class Clock:
    def __init__(self, me, place):
        row = lax.broadcasted_iota(jnp.int32, (8, 128), 0)
        self.token = jnp.where(row == 0, me, place)

    def sync(self, *values):
        self.token, values = lax.optimization_barrier((self.token, values))
        return values if len(values) > 1 else values[0]


def call(clock, kernel, name, outs, args, scratch=(), limit=8, outside=(), raw=(), aliases=None):
    n_in, n_out = len(args), len(outs)

    def body(token, *refs):
        outs_at = n_in + n_out
        refs[outs_at][...] = token[...]
        kernel(token, *refs[:outs_at], *refs[outs_at + 1 :])

    place = lambda k, o: (pltpu.HBM if k in outside else pltpu.VMEM)(o.shape, o.dtype)
    args = [pltpu.with_memory_space_constraint(a, pltpu.HBM if k in raw else pltpu.VMEM) for k, a in enumerate(args)]
    *results, clock.token = pl.pallas_call(
        body,
        in_specs=[VM] + [ANY if k in raw else VM for k in range(n_in)],
        out_specs=[ANY if k in outside else VM for k in range(n_out)] + [VM],
        out_shape=[place(k, o) for k, o in enumerate(outs)] + [pltpu.VMEM((8, 128), jnp.int32)],
        scratch_shapes=list(scratch),
        input_output_aliases={i + 1: o for i, o in (aliases or {}).items()},
        compiler_params=pltpu.CompilerParams(vmem_limit_bytes=limit << 20),
        cost_estimate=pl.CostEstimate(flops=WEIGHT, bytes_accessed=1 << 10, transcendentals=0),
        name=name,
    )(pltpu.with_memory_space_constraint(clock.token, pltpu.VMEM), *args)
    return results


def position(token, row):
    return jnp.max(token[row : row + 1, :])


def blocks_of(token):
    me = position(token, 0)
    return [me ^ mask for mask in MASKS]


def wide(blocks, width):
    return [pl.ds(pl.multiple_of(b * width, width), width) for b in blocks]


def take_blocks(ref, rows, blocks, width):
    return jnp.concatenate([ref[rows, cols] for cols in wide(blocks, width)], axis=1)


def put_blocks(ref, rows, values, blocks, width):
    for i, cols in enumerate(wide(blocks, width)):
        ref[rows, cols] = values[:, i * width : (i + 1) * width]


def stack(refs, cols=slice(None)):
    return jnp.concatenate([r[:, cols] for r in refs], axis=0)


def stack_packs(packs, cols):
    return jnp.concatenate([r[0:128, cols] for r in packs], axis=0)


def vector(packs, start, width):
    return jnp.concatenate([r[128:129, start : start + width] for r in packs], axis=1).astype(F32)


def row_loop(T, body):
    def step(c, _):
        body(pl.ds(pl.multiple_of(c * ROWS, ROWS), ROWS))
        return 0

    lax.fori_loop(0, T // ROWS, step, 0)


def stats(x):
    mean = jnp.mean(x, axis=1, keepdims=True)
    centred = x - mean
    inv = lax.rsqrt(jnp.mean(centred * centred, axis=1, keepdims=True) + EPS)
    return centred * inv, inv


def norm_back(grad, normed, inv):
    return inv * (grad - jnp.mean(grad, axis=1, keepdims=True) - normed * jnp.mean(grad * normed, axis=1, keepdims=True))


def begin_kernel(token, *refs):
    weights, vecs, inner, (out, first, second, wi0, wi1), rest = refs[:4], refs[4:10], refs[10], refs[11:16], refs[16:]
    bufs, sems = rest[:6], rest[6]
    cols = [slice(512 * n, 512 * (n + 1)) for n in range(4)]
    copies = [pltpu.make_async_copy(w, out.at[0:128, c], sems.at[n]) for n, (w, c) in enumerate(zip(weights, cols))]
    copies += [pltpu.make_async_copy(v, b, sems.at[4 + n]) for n, (v, b) in enumerate(zip(vecs, bufs))]
    copies += [pltpu.make_async_copy(inner.at[64 * n : 64 * (n + 1), :], w, sems.at[10 + n]) for n, w in enumerate((wi0, wi1))]
    for copy in copies:
        copy.start()
    for copy in copies:
        copy.wait()
    vec = jnp.concatenate([b[...].reshape(1, -1).astype(F32) for b in bufs] + [jnp.zeros((1, 896), F32)], axis=1)
    out[128:144, :] = jnp.broadcast_to(vec, (16, 2048)).astype(BF16)
    odd = lax.rem(position(token, 1), 2)
    for k, piece in enumerate((first, second)):
        piece[...] = out[:, pl.ds(pl.multiple_of(odd * 1024 + 512 * k, 512), 512)]


def begin(clock, weights, vecs, inner):
    scratch = [pltpu.VMEM(v.shape, BF16) for v in vecs] + [pltpu.SemaphoreType.DMA((12,))]
    outs = [shape((144, 2048)), shape((144, 512)), shape((144, 512)), shape((64, 2048)), shape((64, 2048))]
    return call(clock, begin_kernel, "begin", outs, [*weights, *vecs, inner], scratch, limit=JOIN, raw=range(11))


def assemble_kernel(token, mine0, mine1, other0, other1, _, out):
    odd = lax.rem(position(token, 1), 2)
    for half, pieces in ((odd, (mine0, mine1)), (1 - odd, (other0, other1))):
        for k, piece in enumerate(pieces):
            out[:, pl.ds(pl.multiple_of(half * 1024 + 512 * k, 512), 512)] = piece[...]


def assemble(clock, mine, other, waited):
    return call(clock, assemble_kernel, "assemble", [shape((144, 2048))], [*mine, *other, waited], limit=JOIN)[0]


def first_norm_kernel(token, tokens, n1, n1_low, scr):
    blocks = blocks_of(token)

    def body(rows):
        n, _ = stats(tokens[rows, :].astype(F32))
        scr[...] = n
        n = take_blocks(scr, slice(None), blocks, 128)
        n1[rows, :] = n
        n1_low[rows, :] = n.astype(BF16)

    row_loop(tokens.shape[0], body)


def first_norm(clock, tokens):
    T = tokens.shape[0]
    return call(clock, first_norm_kernel, "first_norm", [shape((T, 512), F32), shape((T, 512))], [tokens], [pltpu.VMEM((ROWS, 512), F32)])


def project_kernel(_, n1, p0, p1, p2, p3, qkvf, a1):
    packs = (p0, p1, p2, p3)
    a1[...] = (n1[...] * vector(packs, 0, 128) + vector(packs, 128, 128)).astype(BF16)
    for n in range(4):
        cols = slice(512 * n, 512 * (n + 1))
        out = mm(a1[...], stack_packs(packs, cols))
        qkvf[:, cols] = (jnp.exp(out) if n == 3 else out).astype(BF16)


def project(clock, n1, packs):
    T = n1.shape[0]
    return call(clock, project_kernel, "project", [shape((T, 2048))], [n1, *packs], [pltpu.VMEM((T, 512), BF16)])[0]


def left_half(rows):
    return lax.broadcasted_iota(jnp.int32, (rows, PAIR), 1) < 64


def split_pair(x, left):
    zero = jnp.zeros((), x.dtype)
    return jnp.concatenate((jnp.where(left, x, zero), jnp.where(left, zero, x)), axis=0)


def same_head():
    r = lax.broadcasted_iota(jnp.int32, (PAIR, PAIR), 0) < 64
    c = lax.broadcasted_iota(jnp.int32, (PAIR, PAIR), 1) < 64
    return r == c


def causal_pair(rows):
    r = lax.broadcasted_iota(jnp.int32, (rows, 2 * rows), 0)
    c = lax.broadcasted_iota(jnp.int32, (rows, 2 * rows), 1)
    return r >= jnp.where(c >= rows, c - rows, c)


def triangle(rows):
    return lax.broadcasted_iota(jnp.int32, (rows, rows), 0) >= lax.broadcasted_iota(jnp.int32, (rows, rows), 1)


def half_reduce(x, left, fn, fill):
    a = fn(jnp.where(left, x, fill), axis=1, keepdims=True)
    b = fn(jnp.where(left, fill, x), axis=1, keepdims=True)
    return jnp.where(left, a, b)


def pair_of(j):
    return slice(PAIR * j, PAIR * (j + 1))


def a_of(j):
    return slice(256 * j, 256 * (j + 1))


def b_of(j):
    return slice(1024 + 256 * j, 1024 + 256 * (j + 1))


def s_of(j):
    return slice(2048 + PAIR * j, 2048 + PAIR * (j + 1))


def g_of(j):
    return slice(2560 + PAIR * j, 2560 + PAIR * (j + 1))


KEPT = 3072


def chunk_rows(c):
    return pl.ds(pl.multiple_of(c * CHUNK, CHUNK), CHUNK)


def forward_kernel(_, qkvf, mixed, kept, states, carry_out, s1, s2, carry):
    C = CHUNK
    s1[...] = jnp.zeros_like(s1)
    s2[...] = jnp.zeros_like(s2)
    carry[...] = jnp.zeros_like(carry)
    left = left_half(C)
    causal = causal_pair(C)
    same = same_head()
    lower = triangle(C).astype(BF16)
    zero = jnp.zeros((), BF16)

    def step(c, _):
        rows = chunk_rows(c)
        part = lambda n, j: qkvf[rows, 512 * n + PAIR * j : 512 * n + PAIR * (j + 1)]
        raw = [mm_nt(part(0, j), split_pair(part(1, j), left)) for j in PAIRS]
        carry_out[c] = carry[...]
        denom = mm(lower, qkvf[rows, 1536:2048]) + carry[0:1, :]
        carry[0:1, :] = denom[C - 1 :, :]
        rden_all = 1.0 / denom
        f2 = [split_pair(part(3, j), left) for j in PAIRS]
        numer = []
        for j in PAIRS:
            a2 = jnp.where(causal, raw[j].astype(BF16), zero)
            kept[rows, a_of(j)] = a2
            s1b = s1[j].astype(BF16)
            states[c, :, pair_of(j)] = s1b
            numer.append(mm(a2, f2[j]) + mm(part(0, j), s1b))
        g = []
        for j in PAIRS:
            rden = rden_all[:, pair_of(j)]
            s = numer[j] * rden * SCALE
            kept[rows, s_of(j)] = s.astype(BF16)
            e = jnp.exp(s - half_reduce(s, left, jnp.max, -jnp.inf))
            p = e / half_reduce(e, left, jnp.sum, 0.0)
            g.append((p * rden).astype(BF16))
            kept[rows, g_of(j)] = g[j]
        raw = [mm_nt(g[j], f2[j]) for j in PAIRS]
        for j in PAIRS:
            b2 = jnp.where(causal, raw[j].astype(BF16), zero)
            kept[rows, b_of(j)] = b2
            s2b = s2[j].astype(BF16)
            states[c, :, pair_of(4 + j)] = s2b
            o = mm(b2, split_pair(part(2, j), left)) + mm(g[j], s2b)
            mixed[rows, pair_of(j)] = o.astype(BF16)
        for j in PAIRS:
            s1[j] += jnp.where(same, mm_tn(part(1, j), part(3, j)), 0.0)
            s2[j] += jnp.where(same, mm_tn(part(3, j), part(2, j)), 0.0)
        return 0

    lax.fori_loop(0, qkvf.shape[0] // C, step, 0, unroll=UNROLL)


def state_scratch():
    return [pltpu.VMEM((4, PAIR, PAIR), F32), pltpu.VMEM((4, PAIR, PAIR), F32), pltpu.VMEM((8, 512), F32)]


def attention_forward(clock, qkvf):
    T = qkvf.shape[0]
    n = T // CHUNK
    outs = [shape((T, 512)), shape((T, KEPT)), shape((n, PAIR, 1024)), shape((n, 8, 512), F32)]
    return call(clock, forward_kernel, "attention_forward", outs, [qkvf], state_scratch())


def backward_kernel(first, count, last, _, qkvf, kept, states, carry_in, do_in, *refs):
    C = CHUNK
    r1, r2, carry = refs[-3:]
    begins, (grad, *ends) = (refs[:3], refs[3:-3]) if first < last else ((), refs[:-3])
    for ref, old in zip((r1, r2, carry), begins or (None,) * 3):
        ref[...] = jnp.zeros_like(ref) if old is None else old[...]
    left = left_half(C)
    causal = causal_pair(C)
    same = same_head()
    lower = triangle(C).astype(BF16)
    upper = lower.T
    upper2 = jnp.concatenate((upper, upper), axis=1)
    zero = jnp.zeros((), BF16)

    def step(t, _):
        c = first - t
        rows = chunk_rows(c)
        here = chunk_rows(count - 1 - t)
        part = lambda n, j: qkvf[rows, 512 * n + PAIR * j : 512 * n + PAIR * (j + 1)]
        do = [do_in[rows, pair_of(j)] for j in PAIRS]
        denoms = mm(lower, qkvf[rows, 1536:2048]) + carry_in[c][0:1, :]
        s1b = [states[c, :, pair_of(j)] for j in PAIRS]
        s2b = [states[c, :, pair_of(4 + j)] for j in PAIRS]
        r1b = [r1[j].astype(BF16) for j in PAIRS]
        r2b = [r2[j].astype(BF16) for j in PAIRS]
        g = [kept[rows, g_of(j)] for j in PAIRS]
        raw = [mm_nt(do[j], split_pair(part(2, j), left)) for j in PAIRS]
        f2 = [split_pair(part(3, j), left) for j in PAIRS]
        db2, dg, dn, dd = [], [], [], []
        for j in PAIRS:
            db2.append(jnp.where(causal, raw[j].astype(BF16), zero))
            dg.append(mm(db2[j], f2[j]) + mm_nt(do[j], s2b[j]))
        for j in PAIRS:
            dv2 = mm_tn(kept[rows, b_of(j)], do[j])
            dv = jnp.where(left, dv2[:C], dv2[C:]) + mm(part(3, j), r2b[j])
            grad[here, 1024 + PAIR * j : 1024 + PAIR * (j + 1)] = dv.astype(BF16)
        for j in PAIRS:
            denom = denoms[:, pair_of(j)]
            rden = 1.0 / denom
            p = g[j].astype(F32) * denom
            dpp = dg[j] * rden * p
            ds = dpp - p * half_reduce(dpp, left, jnp.sum, 0.0)
            dd.append(-(dpp + ds * kept[rows, s_of(j)].astype(F32)) * rden)
            dn.append((ds * SCALE * rden).astype(BF16))
        raw = [mm_nt(dn[j], f2[j]) for j in PAIRS]
        for j in PAIRS:
            df2 = mm_tn(db2[j], g[j]) + mm_tn(kept[rows, a_of(j)], dn[j])
            hi = dd[j].astype(BF16)
            lo = (dd[j] - hi.astype(F32)).astype(BF16)
            df = jnp.where(left, df2[:C], df2[C:]) + mm_nt(part(2, j), r2b[j]) + mm(part(1, j), r1b[j])
            df = df + mm(upper2, jnp.concatenate((hi, lo), axis=0)) + carry[0:1, pair_of(j)]
            grad[here, 1536 + PAIR * j : 1536 + PAIR * (j + 1)] = (df * part(3, j).astype(F32)).astype(BF16)
            carry[0:1, pair_of(j)] += jnp.sum(dd[j], axis=0, keepdims=True)
        for j in PAIRS:
            da2 = jnp.where(causal, raw[j].astype(BF16), zero)
            dq = mm(da2, split_pair(part(1, j), left)) + mm_nt(dn[j], s1b[j])
            grad[here, pair_of(j)] = dq.astype(BF16)
            dk2 = mm_tn(da2, part(0, j))
            dk = jnp.where(left, dk2[:C], dk2[C:]) + mm_nt(part(3, j), r1b[j])
            grad[here, 512 + PAIR * j : 512 + PAIR * (j + 1)] = dk.astype(BF16)
        for j in PAIRS:
            r1[j] += jnp.where(same, mm_tn(part(0, j), dn[j]), 0.0)
            r2[j] += jnp.where(same, mm_tn(g[j], do[j]), 0.0)
        return 0

    lax.fori_loop(0, count, step, 0, unroll=UNROLL)
    for ref, end in zip((r1, r2, carry), ends):
        end[...] = ref[...]


def attention_backward(clock, qkvf, saved, d_o, first, count, states=()):
    rows = count * CHUNK
    outs = [shape((rows, 2048))]
    if first - count >= 0:
        outs += [shape((4, PAIR, PAIR), F32), shape((4, PAIR, PAIR), F32), shape((8, 512), F32)]
    kernel = functools.partial(backward_kernel, first, count, qkvf.shape[0] // CHUNK - 1)
    return call(clock, kernel, "attention_backward", outs, [qkvf, *saved, d_o, *states], state_scratch())


def gelu_parts(v):
    c = 0.7978845608028654
    k = c * 0.044715
    v2 = v * v
    half = 0.5 * jnp.tanh(v * (c + k * v2)) + 0.5
    act = v * half
    return act, half + act * (1.0 - half) * (2 * c + (6 * k) * v2)


def middle_kernel(token, tokens, mixed, *refs):
    wo, packs, (resid_out, n2_out, r2_out, a2_out, scr) = refs[:4], refs[4:8], refs[8:]
    blocks = blocks_of(token)
    gain, shift = vector(packs, 256, 128), vector(packs, 384, 128)

    def body(rows):
        resid = tokens[rows, :].astype(F32) + mm(take_blocks(mixed, rows, blocks, 128), stack(wo))
        resid_out[rows, :] = resid
        n2, r2 = stats(resid)
        scr[...] = n2
        n2 = take_blocks(scr, slice(None), blocks, 128)
        n2_out[rows, :] = n2.astype(BF16)
        r2_out[rows, :] = jnp.broadcast_to(r2, (ROWS, 128))
        a2_out[rows, :] = (n2 * gain + shift).astype(BF16)

    row_loop(tokens.shape[0], body)


def middle(clock, tokens, mixed, wo, packs):
    T = tokens.shape[0]
    outs = [shape((T, 512), F32), shape((T, 512)), shape((T, 128), F32), shape((T, 512))]
    return call(clock, middle_kernel, "middle", outs, [tokens, mixed, *wo, *packs], [pltpu.VMEM((ROWS, 512), F32)])


def ffn_inner_kernel(token, a2_ref, *refs):
    wi, packs, (act_out, slope_out) = refs[:-6], refs[-6:-2], refs[-2:]
    cols = wide(blocks_of(token), 512)

    def body(rows):
        a2 = a2_ref[rows, :]
        inner = mm(a2, stack(wi, cols[0]))
        for i in range(4):
            after = mm(a2, stack(wi, cols[i + 1])) if i < 3 else None
            act, slope = gelu_parts(inner + packs[i][128:129, 640:1152].astype(F32))
            act_out[rows, 512 * i : 512 * (i + 1)] = act.astype(BF16)
            slope_out[rows, cols[i]] = slope.astype(BF16)
            inner = after

    row_loop(a2_ref.shape[0], body)


def ffn_inner(clock, a2, wi, packs):
    T = a2.shape[0]
    return call(clock, ffn_inner_kernel, "ffn_inner", [shape((T, 2048)), shape((T, 2048))], [a2, *wi, *packs])


def outer_grad_kernel(_, act, dy, keep, send):
    for i in range(4):
        out = mm_tn(act[:, 512 * i : 512 * (i + 1)], dy[...]).astype(BF16)
        (keep if i < 2 else send)[i % 2] = out


def outer_grad(clock, act, dy):
    return call(clock, outer_grad_kernel, "outer_grad", [shape((2, 512, 512))] * 2, [act, dy])


def ffn_outer_kernel(token, resid, act, *refs):
    wu, vs, (out, bias, result, sem) = refs[:4], refs[4:8], refs[8:]
    put_blocks(bias, slice(None), jnp.broadcast_to(vector(vs, 512, 128), (8, 512)), blocks_of(token), 128)
    total = mm(act[...], stack(wu))
    result[...] = (total + resid[...] + bias[0:1, :]).astype(BF16)
    copy = pltpu.make_async_copy(result, out, sem)
    copy.start()
    copy.wait()


def ffn_outer(clock, resid, act, wu, vecs):
    scratch = [pltpu.VMEM((8, 512), F32), pltpu.VMEM(resid.shape, BF16), pltpu.SemaphoreType.DMA]
    return call(clock, ffn_outer_kernel, "ffn_outer", [shape(resid.shape)], [resid, act, *wu, *vecs], scratch, outside=(0,))[0]


def inner_back_kernel(token, dy, slope, u0, u1, u2, u3, din, sums):
    cols = wide(blocks_of(token), 512)
    sums[...] = jnp.zeros_like(sums)
    sums[1:2, 0:512] = jnp.sum(dy[...].astype(F32), axis=0, keepdims=True)
    for i, u in enumerate((u0, u1, u2, u3)):
        d = (mm_nt(dy[...], u[...]) * slope[:, cols[i]].astype(F32)).astype(BF16)
        din[:, cols[i]] = d
        sums[0:1, cols[i]] = jnp.sum(d.astype(F32), axis=0, keepdims=True)


def inner_back(clock, dy, slope, wu):
    T = dy.shape[0]
    return call(clock, inner_back_kernel, "inner_back", [shape((T, 2048)), shape((8, 2048), F32)], [dy, slope, *wu], aliases={1: 0})


def inner_grad_kernel(n2, din, sums, keep, send):
    tail = jnp.concatenate((sums[...], jnp.zeros_like(sums)), axis=0).astype(BF16)
    for i in range(4):
        dest = keep if i < 2 else send
        dest[i % 2, 0:128, :] = mm_tn(n2[:, 128 * i : 128 * (i + 1)], din[...]).astype(BF16)
        dest[i % 2, 128:144, :] = tail


def resid_back_kernel(token, dy, n2, r2, din, sums, *refs):
    wo, wi, packs = refs[:4], refs[4:-9], refs[-9:-5]
    keep, send, dres_out, do_out, scr = refs[-5:]
    inner_grad_kernel(n2, din, sums, keep, send)
    blocks = blocks_of(token)
    gain = vector(packs, 256, 128)

    def body(rows):
        da2 = mm_nt(din[rows, :], stack(wi))
        put_blocks(scr, slice(None), norm_back(da2 * gain, n2[rows, :].astype(F32), r2[rows, 0:1]), blocks, 128)
        dres = dy[rows, :].astype(F32) + scr[...]
        dres_out[rows, :] = dres
        d_o = mm_nt(dres.astype(BF16), stack(wo))
        put_blocks(do_out, rows, d_o.astype(BF16), blocks, 128)

    row_loop(dy.shape[0], body)


def resid_back(clock, dy, n2, r2, din, sums, wo, wi, packs):
    T = dy.shape[0]
    outs = [shape((2, 144, 2048))] * 2 + [shape((T, 512), F32), shape((T, 512))]
    return call(clock, resid_back_kernel, "resid_back", outs, [dy, n2, r2, din, sums, *wo, *wi, *packs], [pltpu.VMEM((ROWS, 512), F32)])


def project_grad_kernel(token, n1, early, late, mixed, dres, *dests):
    half = early.shape[0]
    blocks = wide(blocks_of(token), 128)
    for keep, send, start in ((*dests[:2], 0), (*dests[2:], 1024)):
        cols = slice(start, start + 1024)
        out = (mm_tn(n1[0:half, :], early[:, cols]) + mm_tn(n1[half:, :], late[:, cols])).astype(BF16)
        total = sum(jnp.sum(r[:, cols].astype(F32), axis=0, keepdims=True) for r in (early, late))
        tail = jnp.broadcast_to(total, (16, 1024)).astype(BF16)
        for i in range(4):
            dest = keep if i < 2 else send
            dest[i % 2, 0:128, 0:1024] = out[128 * i : 128 * (i + 1)]
            dest[i % 2, 128:144, 0:1024] = tail
    keep, send = dests[:2]
    d = dres[...].astype(BF16)
    for i in range(4):
        dest = keep if i < 2 else send
        dest[i % 2, 0:128, 1024:] = mm_tn(mixed[:, blocks[i]], d).astype(BF16)
        dest[i % 2, 128:144, 1024:] = jnp.zeros((16, 512), BF16)


def project_grad(clock, n1, early, late, mixed, dres):
    outs = [shape((2, 144, 1536))] * 2 + [shape((2, 144, 1024))] * 2
    keep_a, send_a, keep_b, send_b = call(clock, project_grad_kernel, "project_grad", outs, [n1, early, late, mixed, dres])
    return (keep_a, send_a), (keep_b, send_b)


def input_grad_kernel(token, tokens, early, late, dres, p0, p1, p2, p3, out, scr, result, sems):
    packs = (p0, p1, p2, p3)
    blocks = blocks_of(token)
    gain = vector(packs, 0, 128)
    w = stack_packs(packs, slice(0, 2048))
    copies = []
    for h, d in enumerate((early, late)):
        rows = slice(ROWS * h, ROWS * (h + 1))
        e = mm_nt(d[...], w) * gain
        n1, r1 = stats(tokens[rows, :].astype(F32))
        scr[...] = n1
        put_blocks(scr, slice(None), norm_back(e, take_blocks(scr, slice(None), blocks, 128), r1), blocks, 128)
        result[rows, :] = (dres[rows, :] + scr[...]).astype(BF16)
        copies.append(pltpu.make_async_copy(result.at[rows, :], out.at[rows, :], sems.at[h]))
        copies[-1].start()
    for copy in copies:
        copy.wait()


def input_grad(clock, tokens, early, late, dres, packs):
    scratch = [pltpu.VMEM((ROWS, 512), F32), pltpu.VMEM(dres.shape, BF16), pltpu.SemaphoreType.DMA((2,))]
    return call(clock, input_grad_kernel, "input_grad", [shape(dres.shape)], [tokens, early, late, dres, *packs], scratch, outside=(0,))[0]


def exchange(value, axis, size, mask):
    return lax.ppermute(value, axis, [(i, i ^ mask) for i in range(size)])


def over_x(value):
    return exchange(value, "fsdp", 4, 2)


def over_core(value):
    return exchange(value, "fsdp", 4, 1)


def add(a, b):
    return a.astype(F32) + b.astype(F32)


def half_at(bit, width):
    return pl.ds(pl.multiple_of(bit * (width // 2), width // 2), width // 2)


def gate_kernel(*refs):
    pass


def gate(clock, waited, values):
    n = len(waited)
    outs = [shape(v.shape, v.dtype) for v in values]
    return call(clock, gate_kernel, "gate", outs, [*waited, *values], limit=1, aliases={n + k: k for k in range(len(values))})


def join_core_kernel(_, keep, got, mine, *pieces):
    mine[...] = add(keep[0], got[0]).astype(BF16)
    start = 0
    for piece in pieces:
        rows = slice(start, start + piece.shape[0])
        piece[...] = add(keep[1, rows, :], got[1, rows, :]).astype(BF16)
        start += piece.shape[0]


def join_kernel(split, place, token, keep, *refs):
    outs_at = len(refs) - (1 if split is None else 3)
    gots, refs = refs[:outs_at], refs[outs_at:]
    if place is not None:
        out = refs[0]
        bit = lax.rem(lax.div(position(token, 1), place), 2)
        out[:, half_at(bit, out.shape[1])] = keep[...]
        out[:, half_at(1 - bit, out.shape[1])] = gots[0][...]
        return
    whole = refs[-1]
    start = 0
    for got in gots:
        rows = slice(start, start + got.shape[0])
        whole[rows, :] = add(keep[rows, :], got[...]).astype(BF16)
        start += got.shape[0]
    if split is not None:
        mine, send, _ = refs
        bit = lax.rem(lax.div(position(token, 1), split), 2)
        mine[...] = whole[:, half_at(bit, whole.shape[1])]
        send[...] = whole[:, half_at(1 - bit, whole.shape[1])]


class Chain:
    def __init__(self, clock, dp, halved, pieces, pair):
        self.clock, self.dp, self.pieces = clock, dp, pieces
        masks = [1 << k for k in range(dp.bit_length() - 1)]
        self.todo = [("core", 0), ("x", 0)] + [("half" if m in halved else "all", m) for m in masks] + [("beside", m) for m in reversed(masks) if m in halved]
        self.keep, self.send = pair
        self.busy = True

    def launch(self):
        self.kind, self.mask = self.todo.pop(0)
        if self.kind == "core":
            self.got = [over_core(self.send)]
        elif self.kind == "x":
            self.got = [over_x(self.send.pop(0))]
        else:
            self.got = [exchange(self.send, "dp", self.dp, self.mask)]

    def more(self, *others):
        piece, *sends = gate(self.clock, [self.got[-1]], [self.send.pop(0)] + [c.send for c in others])
        self.got.append(over_x(piece))
        for chain, send in zip(others, sends):
            chain.send = send
            chain.launch()

    def step(self):
        rows, width = self.keep.shape[-2:]
        if self.kind == "core":
            outs = [shape((rows, width))] + [shape((n, width)) for n in self.pieces]
            self.keep, *self.send = call(self.clock, join_core_kernel, "join_core", outs, [self.keep, *self.got], limit=JOIN)
        else:
            split = self.todo[0][1] if self.todo and self.todo[0][0] == "half" else None
            place = self.mask if self.kind == "beside" else None
            kernel = functools.partial(join_kernel, split, place)
            if split is None:
                outs, scratch = [shape((rows, 2 * width if place else width))], []
            else:
                outs, scratch = [shape((rows, width // 2))] * 2, [pltpu.VMEM((rows, width), BF16)]
            out = call(self.clock, kernel, "join", outs, [self.keep, *self.got], scratch, limit=JOIN)
            self.keep, self.send = out if split else (out[0], out[0])
        self.busy = bool(self.todo)
        if self.busy:
            self.launch()


def column(row):
    r = lax.broadcasted_iota(jnp.int32, (128, 128), 0)
    c = lax.broadcasted_iota(jnp.int32, (128, 128), 1)
    return jnp.sum(jnp.where(r == c, row, 0.0), axis=1, keepdims=True)


def as_row(col):
    r = lax.broadcasted_iota(jnp.int32, (128, 128), 0)
    c = lax.broadcasted_iota(jnp.int32, (128, 128), 1)
    return jnp.sum(jnp.where(r == c, col, 0.0), axis=0, keepdims=True)


def send_out(pairs, sems):
    copies = [pltpu.make_async_copy(src, dst, sems.at[k]) for k, (src, dst) in enumerate(pairs)]
    for copy in copies:
        copy.start()
    for copy in copies:
        copy.wait()


def finish_outer_kernel(_, u, out, buf, sems):
    buf[...] = u[...].astype(F32)
    send_out([(buf, out)], sems)


def finish_outer(clock, u):
    return call(clock, finish_outer_kernel, "finish_outer", [shape(u.shape, F32)], [u], [pltpu.VMEM(u.shape, F32), pltpu.SemaphoreType.DMA((1,))], limit=JOIN, outside=(0,))[0]


def finish_inner_kernel(token, total, w, pack, out, gain_out, shift_out, inner_out, outer_out, buf, small, sems):
    gain, shift = (column(pack[128:129, k : k + 128].astype(F32)) for k in (256, 384))
    m = total[0:128, :].astype(F32)
    tail = total[128:144, :].astype(F32)
    buf[...] = gain * m + shift * tail[0:1, :]
    wf = w[...].astype(F32)
    small[0:1, 0:128] = as_row(jnp.sum(wf * m, axis=1, keepdims=True))
    small[1:2, 0:128] = as_row(jnp.sum(wf * tail[0:1, :], axis=1, keepdims=True))
    me = position(token, 0)
    small[2:3, :] = total[128:144, pl.ds(pl.multiple_of(me * 512, 512), 512)].astype(F32)[0:1, :]
    small[3:4, 0:128] = total[128:144, pl.ds(pl.multiple_of(me * 128, 128), 128)].astype(F32)[1:2, :]
    send_out([(buf, out), (small.at[0, 0:128], gain_out), (small.at[1, 0:128], shift_out), (small.at[2], inner_out), (small.at[3, 0:128], outer_out)], sems)


def finish_inner(clock, total, w, pack):
    outs = [shape((128, 2048), F32), shape((128,), F32), shape((128,), F32), shape((512,), F32), shape((128,), F32)]
    scratch = [pltpu.VMEM((128, 2048), F32), pltpu.VMEM((8, 512), F32), pltpu.SemaphoreType.DMA((5,))]
    return call(clock, finish_inner_kernel, "finish_inner", outs, [total, w, pack], scratch, limit=JOIN, outside=range(5))


def project_parts(total, pack, start, buf):
    gain, shift = (column(pack[128:129, k : k + 128].astype(F32)) for k in (0, 128))
    m = total[0:128, 0:1024].astype(F32)
    tail = total[128:144, 0:1024].astype(F32)[0:1, :]
    buf[:, 0:1024] = gain * m + shift * tail
    w = pack[0:128, start : start + 1024].astype(F32)
    return as_row(jnp.sum(w * m, axis=1, keepdims=True)), as_row(jnp.sum(w * tail, axis=1, keepdims=True))


def finish_first_kernel(_, total, pack, out0, out1, out2, before, buf, sems):
    gain, shift = project_parts(total, pack, 0, buf)
    buf[:, 1024:1536] = total[0:128, 1024:1536].astype(F32)
    before[0:1, :] = gain
    before[1:2, :] = shift
    send_out([(buf.at[:, 512 * n : 512 * (n + 1)], out) for n, out in enumerate((out0, out1, out2))], sems)


def finish_first(clock, total, pack):
    outs = [shape((128, 512), F32)] * 3 + [shape((8, 128), F32)]
    scratch = [pltpu.VMEM((128, 1536), F32), pltpu.SemaphoreType.DMA((3,))]
    return call(clock, finish_first_kernel, "finish_first", outs, [total, pack], scratch, limit=JOIN, outside=range(3))


def finish_last_kernel(_, total, pack, before, out0, out1, gain_out, shift_out, buf, small, sems):
    gain, shift = project_parts(total, pack, 1024, buf)
    small[0:1, :] = before[0:1, :] + gain
    small[1:2, :] = before[1:2, :] + shift
    send_out([(buf.at[:, 0:512], out0), (buf.at[:, 512:1024], out1), (small.at[0], gain_out), (small.at[1], shift_out)], sems)


def finish_last(clock, total, pack, before):
    outs = [shape((128, 512), F32)] * 2 + [shape((128,), F32)] * 2
    scratch = [pltpu.VMEM((128, 1024), F32), pltpu.VMEM((8, 128), F32), pltpu.SemaphoreType.DMA((4,))]
    return call(clock, finish_last_kernel, "finish_last", outs, [total, pack, before], scratch, limit=JOIN, outside=range(4))


def per_device(dp, tokens, first_gain, first_shift, w_query, w_key, w_value, w_control, w_output, second_gain, second_shift, w_inner, inner_bias, w_outer, outer_bias, cotangent):
    clock = Clock(lax.axis_index("fsdp").astype(jnp.int32), lax.axis_index("dp").astype(jnp.int32))
    vectors = (first_gain, first_shift, second_gain, second_shift, outer_bias, inner_bias)
    own, first, second, wi0, wi1 = begin(clock, (w_query, w_key, w_value, w_control), vectors, w_inner)
    mine = [over_x(first), over_x(second)]
    own_core, wi_c = over_core(own), over_core(w_inner)
    n1, n1_low = first_norm(clock, tokens)
    *mine, wi0, wi1, w_output = clock.sync(*mine, wi0, wi1, w_output)
    wi_x0 = over_x(wi0)
    across = assemble(clock, mine, [exchange(v, "dp", dp, 1) for v in mine], wi_x0)
    packs = [own, across, own_core, over_core(across)]
    wi1, w_output = clock.sync(wi1, w_output)
    wi_x1, wo_x, wo_c = over_x(wi1), over_x(w_output), over_core(w_output)
    qkvf = project(clock, n1, packs)
    mixed, *saved = attention_forward(clock, qkvf)
    wo_x, wi_x1, w_outer = clock.sync(wo_x, wi_x1, w_outer)
    wo = [w_output, wo_x, wo_c, over_core(wo_x)]
    wi = [w_inner, wi_x0, wi_x1, wi_c, over_core(wi_x0), over_core(wi_x1)]
    wu_x, wu_c = over_x(w_outer), over_core(w_outer)
    resid, n2, r2, a2 = middle(clock, tokens, mixed, wo, packs)
    act, slope = ffn_inner(clock, a2, wi, packs)
    u = Chain(clock, dp, (1, 2), (272, 240), outer_grad(clock, act, cotangent))
    u.launch()
    wu_x = clock.sync(wu_x)
    wu = [w_outer, wu_x, wu_c, over_core(wu_x)]
    din, sums = inner_back(clock, cotangent, slope, wu)
    u.step()
    *pair, dres, d_o = resid_back(clock, cotangent, n2, r2, din, sums, wo, wi, packs)
    i = Chain(clock, dp, (1, 2), (48, 32, 64), pair)
    u.more(i)
    early = attention_backward(clock, qkvf, saved, d_o, 7, 4)
    u.step()
    i.step()
    late = attention_backward(clock, qkvf, saved, d_o, 3, 4, early[1:])
    i.more()
    u.step()
    pair_a, pair_b = project_grad(clock, n1_low, late[0], early[0], mixed, dres)
    a, b = Chain(clock, dp, (1, 2), (144,), pair_a), Chain(clock, dp, (1,), (144,), pair_b)
    u.step()
    i.more(a, b)
    a.step()
    grad_tokens = input_grad(clock, tokens, late[0], early[0], dres, packs)
    for c in (u, b, i):
        c.step()
    output = ffn_outer(clock, resid, act, wu, packs)
    order = [a, u, i, a, i, b, a, u, b, i, a, b, i, a, i, b, a, b]
    while any(c.busy for c in (u, i, a, b)):
        c = order.pop(0) if order else next(c for c in (u, i, a, b) if c.busy)
        if not c.busy:
            continue
        c.step()
        if not c.busy and c is u:
            grad_outer = finish_outer(clock, u.keep)
        elif not c.busy and c is i:
            grad_inner, *vectors = finish_inner(clock, i.keep, w_inner, packs[0])
        elif not c.busy and c is a:
            grad_query, grad_key, grad_output, before = finish_first(clock, a.keep, packs[0])
    grad_value, grad_control, first_gain_grad, first_shift_grad = finish_last(clock, b.keep, packs[0], before)
    second_gain_grad, second_shift_grad, inner_bias_grad, outer_bias_grad = vectors
    return (
        output, grad_tokens, first_gain_grad, first_shift_grad, grad_query, grad_key, grad_value, grad_control,
        grad_output, second_gain_grad, second_shift_grad, grad_inner, inner_bias_grad, grad_outer, outer_bias_grad,
    )


def solution(mesh):
    row, vec, mat = P(("dp", "fsdp"), None), P("fsdp"), P("fsdp", None)
    return jax.shard_map(
        functools.partial(per_device, mesh.shape["dp"]),
        mesh=mesh,
        in_specs=(row, vec, vec, mat, mat, mat, mat, mat, vec, vec, mat, vec, mat, vec, row),
        out_specs=(row, row, vec, vec, mat, mat, mat, mat, mat, vec, vec, mat, vec, mat, vec),
        check_vma=False,
    )
```

```python
import functools

import jax
import jax.numpy as jnp
from jax import lax
from jax.experimental import pallas as pl
from jax.experimental.pallas import tpu as pltpu
from jax.sharding import PartitionSpec as P

F32 = jnp.float32
BF16 = jnp.bfloat16
PAIR = 128
PAIRS = range(4)
SCALE = 64 ** -0.5
CHUNK = 128
UNROLL = 2
JOIN = 4
ROWS = 512
EPS = 1e-5
WEIGHT = 1000
MASKS = (0, 2, 1, 3)
VM = pl.BlockSpec(memory_space=pltpu.VMEM)
SM = pl.BlockSpec(memory_space=pltpu.SMEM)
ANY = pl.BlockSpec(memory_space=pl.ANY)


def mm(a, b):
    return lax.dot_general(a, b, (((1,), (0,)), ((), ())), preferred_element_type=F32)


def mm_nt(a, b):
    return lax.dot_general(a, b, (((1,), (1,)), ((), ())), preferred_element_type=F32)


def mm_tn(a, b):
    return lax.dot_general(a, b, (((0,), (0,)), ((), ())), preferred_element_type=F32)


def shape(dims, dtype=BF16):
    return jax.ShapeDtypeStruct(dims, dtype)


class Clock:
    def __init__(self, me, place):
        row = lax.broadcasted_iota(jnp.int32, (8, 128), 0)
        self.token = jnp.where(row == 0, me, place)

    def sync(self, *values):
        self.token, values = lax.optimization_barrier((self.token, values))
        return values if len(values) > 1 else values[0]


def call(clock, kernel, name, outs, args, scratch=(), limit=8, outside=(), raw=(), aliases=None):
    n_in, n_out = len(args), len(outs)

    def body(token, *refs):
        outs_at = n_in + n_out
        refs[outs_at][...] = token[...]
        kernel(token, *refs[:outs_at], *refs[outs_at + 1 :])

    place = lambda k, o: (pltpu.HBM if k in outside else pltpu.VMEM)(o.shape, o.dtype)
    args = [pltpu.with_memory_space_constraint(a, pltpu.HBM if k in raw else pltpu.VMEM) for k, a in enumerate(args)]
    *results, clock.token = pl.pallas_call(
        body,
        in_specs=[VM] + [ANY if k in raw else VM for k in range(n_in)],
        out_specs=[ANY if k in outside else VM for k in range(n_out)] + [VM],
        out_shape=[place(k, o) for k, o in enumerate(outs)] + [pltpu.VMEM((8, 128), jnp.int32)],
        scratch_shapes=list(scratch),
        input_output_aliases={i + 1: o for i, o in (aliases or {}).items()},
        compiler_params=pltpu.CompilerParams(vmem_limit_bytes=limit << 20),
        cost_estimate=pl.CostEstimate(flops=WEIGHT, bytes_accessed=1 << 10, transcendentals=0),
        name=name,
    )(pltpu.with_memory_space_constraint(clock.token, pltpu.VMEM), *args)
    return results


def position(token, row):
    return jnp.max(token[row : row + 1, :])


def blocks_of(token):
    me = position(token, 0)
    return [me ^ mask for mask in MASKS]


def wide(blocks, width):
    return [pl.ds(pl.multiple_of(b * width, width), width) for b in blocks]


def take_blocks(ref, rows, blocks, width):
    return jnp.concatenate([ref[rows, cols] for cols in wide(blocks, width)], axis=1)


def put_blocks(ref, rows, values, blocks, width):
    for i, cols in enumerate(wide(blocks, width)):
        ref[rows, cols] = values[:, i * width : (i + 1) * width]


def stack(refs, cols=slice(None)):
    return jnp.concatenate([r[:, cols] for r in refs], axis=0)


def stack_packs(packs, cols):
    return jnp.concatenate([r[0:128, cols] for r in packs], axis=0)


def vector(packs, start, width):
    return jnp.concatenate([r[128:129, start : start + width] for r in packs], axis=1).astype(F32)


def row_loop(T, body):
    def step(c, _):
        body(pl.ds(pl.multiple_of(c * ROWS, ROWS), ROWS))
        return 0

    lax.fori_loop(0, T // ROWS, step, 0)


def stats(x):
    mean = jnp.mean(x, axis=1, keepdims=True)
    centred = x - mean
    inv = lax.rsqrt(jnp.mean(centred * centred, axis=1, keepdims=True) + EPS)
    return centred * inv, inv


def norm_back(grad, normed, inv):
    return inv * (grad - jnp.mean(grad, axis=1, keepdims=True) - normed * jnp.mean(grad * normed, axis=1, keepdims=True))


def parity(token):
    place = position(token, 1)
    return lax.rem(place + lax.div(place, 2), 2)


def begin_kernel(token, *refs):
    weights, vecs, inner, (out, first, second, wi0, wi1), rest = refs[:4], refs[4:10], refs[10], refs[11:16], refs[16:]
    bufs, sems = rest[:6], rest[6]
    cols = [slice(512 * n, 512 * (n + 1)) for n in range(4)]
    copies = [pltpu.make_async_copy(w, out.at[0:128, c], sems.at[n]) for n, (w, c) in enumerate(zip(weights, cols))]
    copies += [pltpu.make_async_copy(v, b, sems.at[4 + n]) for n, (v, b) in enumerate(zip(vecs, bufs))]
    copies += [pltpu.make_async_copy(inner.at[64 * n : 64 * (n + 1), :], w, sems.at[10 + n]) for n, w in enumerate((wi0, wi1))]
    for copy in copies:
        copy.start()
    for copy in copies:
        copy.wait()
    vec = jnp.concatenate([b[...].reshape(1, -1).astype(F32) for b in bufs] + [jnp.zeros((1, 896), F32)], axis=1)
    out[128:144, :] = jnp.broadcast_to(vec, (16, 2048)).astype(BF16)
    odd = parity(token)
    for k, piece in enumerate((first, second)):
        piece[...] = out[:, pl.ds(pl.multiple_of(odd * 1024 + 512 * k, 512), 512)]


def begin(clock, weights, vecs, inner):
    scratch = [pltpu.VMEM(v.shape, BF16) for v in vecs] + [pltpu.SemaphoreType.DMA((12,))]
    outs = [shape((144, 2048)), shape((144, 512)), shape((144, 512)), shape((64, 2048)), shape((64, 2048))]
    return call(clock, begin_kernel, "begin", outs, [*weights, *vecs, inner], scratch, limit=JOIN, raw=range(11))


def assemble_kernel(token, mine0, mine1, other0, other1, _, out):
    odd = parity(token)
    for half, pieces in ((odd, (mine0, mine1)), (1 - odd, (other0, other1))):
        for k, piece in enumerate(pieces):
            out[:, pl.ds(pl.multiple_of(half * 1024 + 512 * k, 512), 512)] = piece[...]


def assemble(clock, mine, other, waited):
    return call(clock, assemble_kernel, "assemble", [shape((144, 2048))], [*mine, *other, waited], limit=JOIN)[0]


def first_norm_kernel(token, tokens, n1, n1_low, scr):
    blocks = blocks_of(token)

    def body(rows):
        n, _ = stats(tokens[rows, :].astype(F32))
        scr[...] = n
        n = take_blocks(scr, slice(None), blocks, 128)
        n1[rows, :] = n
        n1_low[rows, :] = n.astype(BF16)

    row_loop(tokens.shape[0], body)


def first_norm(clock, tokens):
    T = tokens.shape[0]
    return call(clock, first_norm_kernel, "first_norm", [shape((T, 512), F32), shape((T, 512))], [tokens], [pltpu.VMEM((ROWS, 512), F32)])


def project_kernel(_, n1, p0, p1, p2, p3, qkvf):
    packs = (p0, p1, p2, p3)
    gain, shift = vector(packs, 0, 128), vector(packs, 128, 128)

    def body(rows):
        a1 = (n1[rows, :] * gain + shift).astype(BF16)
        for n in range(4):
            cols = slice(512 * n, 512 * (n + 1))
            out = mm(a1, stack_packs(packs, cols))
            qkvf[rows, cols] = (jnp.exp(out) if n == 3 else out).astype(BF16)

    row_loop(n1.shape[0], body)


def project(clock, n1, packs):
    T = n1.shape[0]
    return call(clock, project_kernel, "project", [shape((T, 2048))], [n1, *packs])[0]


def left_half(rows):
    return lax.broadcasted_iota(jnp.int32, (rows, PAIR), 1) < 64


def split_pair(x, left):
    zero = jnp.zeros((), x.dtype)
    return jnp.concatenate((jnp.where(left, x, zero), jnp.where(left, zero, x)), axis=0)


def same_head():
    r = lax.broadcasted_iota(jnp.int32, (PAIR, PAIR), 0) < 64
    c = lax.broadcasted_iota(jnp.int32, (PAIR, PAIR), 1) < 64
    return r == c


def causal_pair(rows):
    r = lax.broadcasted_iota(jnp.int32, (rows, 2 * rows), 0)
    c = lax.broadcasted_iota(jnp.int32, (rows, 2 * rows), 1)
    return r >= jnp.where(c >= rows, c - rows, c)


def triangle(rows):
    return lax.broadcasted_iota(jnp.int32, (rows, rows), 0) >= lax.broadcasted_iota(jnp.int32, (rows, rows), 1)


def half_reduce(x, left, fn, fill):
    a = fn(jnp.where(left, x, fill), axis=1, keepdims=True)
    b = fn(jnp.where(left, fill, x), axis=1, keepdims=True)
    return jnp.where(left, a, b)


def pair_of(j):
    return slice(PAIR * j, PAIR * (j + 1))


def a_of(j):
    return slice(256 * j, 256 * (j + 1))


def b_of(j):
    return slice(1024 + 256 * j, 1024 + 256 * (j + 1))


def s_of(j):
    return slice(2048 + PAIR * j, 2048 + PAIR * (j + 1))


def g_of(j):
    return slice(2560 + PAIR * j, 2560 + PAIR * (j + 1))


KEPT = 3072


def chunk_rows(c):
    return pl.ds(pl.multiple_of(c * CHUNK, CHUNK), CHUNK)


def forward_kernel(_, qkvf, mixed, kept, states, carry_out, s1, s2, carry):
    C = CHUNK
    s1[...] = jnp.zeros_like(s1)
    s2[...] = jnp.zeros_like(s2)
    carry[...] = jnp.zeros_like(carry)
    left = left_half(C)
    causal = causal_pair(C)
    same = same_head()
    lower = triangle(C).astype(BF16)
    zero = jnp.zeros((), BF16)

    def step(c, _):
        rows = chunk_rows(c)
        part = lambda n, j: qkvf[rows, 512 * n + PAIR * j : 512 * n + PAIR * (j + 1)]
        raw = [mm_nt(part(0, j), split_pair(part(1, j), left)) for j in PAIRS]
        carry_out[c] = carry[...]
        denom = mm(lower, qkvf[rows, 1536:2048]) + carry[0:1, :]
        carry[0:1, :] = denom[C - 1 :, :]
        rden_all = 1.0 / denom
        f2 = [split_pair(part(3, j), left) for j in PAIRS]
        numer = []
        for j in PAIRS:
            a2 = jnp.where(causal, raw[j].astype(BF16), zero)
            kept[rows, a_of(j)] = a2
            s1b = s1[j].astype(BF16)
            states[c, :, pair_of(j)] = s1b
            numer.append(mm(a2, f2[j]) + mm(part(0, j), s1b))
        g = []
        for j in PAIRS:
            rden = rden_all[:, pair_of(j)]
            s = numer[j] * rden * SCALE
            kept[rows, s_of(j)] = s.astype(BF16)
            e = jnp.exp(s - half_reduce(s, left, jnp.max, -jnp.inf))
            p = e / half_reduce(e, left, jnp.sum, 0.0)
            g.append((p * rden).astype(BF16))
            kept[rows, g_of(j)] = g[j]
        raw = [mm_nt(g[j], f2[j]) for j in PAIRS]
        for j in PAIRS:
            b2 = jnp.where(causal, raw[j].astype(BF16), zero)
            kept[rows, b_of(j)] = b2
            s2b = s2[j].astype(BF16)
            states[c, :, pair_of(4 + j)] = s2b
            o = mm(b2, split_pair(part(2, j), left)) + mm(g[j], s2b)
            mixed[rows, pair_of(j)] = o.astype(BF16)
        for j in PAIRS:
            s1[j] += jnp.where(same, mm_tn(part(1, j), part(3, j)), 0.0)
            s2[j] += jnp.where(same, mm_tn(part(3, j), part(2, j)), 0.0)
        return 0

    lax.fori_loop(0, qkvf.shape[0] // C, step, 0, unroll=UNROLL)


def state_scratch():
    return [pltpu.VMEM((4, PAIR, PAIR), F32), pltpu.VMEM((4, PAIR, PAIR), F32), pltpu.VMEM((8, 512), F32)]


def attention_forward(clock, qkvf):
    T = qkvf.shape[0]
    n = T // CHUNK
    outs = [shape((T, 512)), shape((T, KEPT)), shape((n, PAIR, 1024)), shape((n, 8, 512), F32)]
    return call(clock, forward_kernel, "attention_forward", outs, [qkvf], state_scratch())


def backward_kernel(first, count, last, _, qkvf, kept, states, carry_in, do_in, *refs):
    C = CHUNK
    r, carry = refs[-2:]
    begins, (grad, *ends) = (refs[:2], refs[2:-2]) if first < last else ((), refs[:-2])
    for ref, old in zip((r, carry), begins or (None,) * 2):
        ref[...] = jnp.zeros_like(ref) if old is None else old[...]
    left = left_half(C)
    causal = causal_pair(C)
    same = same_head()
    same2 = jnp.concatenate((same, same), axis=1)
    lower = triangle(C).astype(BF16)
    upper = lower.T
    upper2 = jnp.concatenate((upper, upper), axis=1)
    zero = jnp.zeros((), BF16)

    def step(t, _):
        c = first - t
        rows = chunk_rows(c)
        here = chunk_rows(count - 1 - t)
        part = lambda n, j: qkvf[rows, 512 * n + PAIR * j : 512 * n + PAIR * (j + 1)]
        do = [do_in[rows, pair_of(j)] for j in PAIRS]
        denoms = mm(lower, qkvf[rows, 1536:2048]) + carry_in[c][0:1, :]
        s1b = [states[c, :, pair_of(j)] for j in PAIRS]
        s2b = [states[c, :, pair_of(4 + j)] for j in PAIRS]
        rb = [r[j].astype(BF16) for j in PAIRS]
        g = [kept[rows, g_of(j)] for j in PAIRS]
        raw = [mm_nt(do[j], split_pair(part(2, j), left)) for j in PAIRS]
        f2 = [split_pair(part(3, j), left) for j in PAIRS]
        db2, dg, dn, dd, later = [], [], [], [], []
        for j in PAIRS:
            db2.append(jnp.where(causal, raw[j].astype(BF16), zero))
            dg.append(mm(db2[j], f2[j]) + mm_nt(do[j], s2b[j]))
        for j in PAIRS:
            later.append(mm(part(3, j), rb[j]))
            dv2 = mm_tn(kept[rows, b_of(j)], do[j])
            dv = jnp.where(left, dv2[:C], dv2[C:]) + later[j][:, :PAIR]
            grad[here, 1024 + PAIR * j : 1024 + PAIR * (j + 1)] = dv.astype(BF16)
        for j in PAIRS:
            denom = denoms[:, pair_of(j)]
            rden = 1.0 / denom
            p = g[j].astype(F32) * denom
            dpp = dg[j] * rden * p
            ds = dpp - p * half_reduce(dpp, left, jnp.sum, 0.0)
            dd.append(-(dpp + ds * kept[rows, s_of(j)].astype(F32)) * rden)
            dn.append((ds * SCALE * rden).astype(BF16))
        raw = [mm_nt(dn[j], f2[j]) for j in PAIRS]
        sums = []
        for k in (0, 2):
            d = jnp.concatenate((dd[k], dd[k + 1]), axis=1)
            hi = d.astype(BF16)
            lo = (d - hi.astype(F32)).astype(BF16)
            total = mm(upper2, jnp.concatenate((hi, lo), axis=0))
            sums += [total[:, :PAIR], total[:, PAIR:]]
        for j in PAIRS:
            df2 = mm_tn(jnp.concatenate((db2[j], kept[rows, a_of(j)]), axis=0), jnp.concatenate((g[j], dn[j]), axis=0))
            df = jnp.where(left, df2[:C], df2[C:]) + mm_nt(jnp.concatenate((part(2, j), part(1, j)), axis=1), rb[j])
            df = df + sums[j] + carry[0:1, pair_of(j)]
            grad[here, 1536 + PAIR * j : 1536 + PAIR * (j + 1)] = (df * part(3, j).astype(F32)).astype(BF16)
            carry[0:1, pair_of(j)] += jnp.sum(dd[j], axis=0, keepdims=True)
        for j in PAIRS:
            da2 = jnp.where(causal, raw[j].astype(BF16), zero)
            dq = mm(da2, split_pair(part(1, j), left)) + mm_nt(dn[j], s1b[j])
            grad[here, pair_of(j)] = dq.astype(BF16)
            dk2 = mm_tn(da2, part(0, j))
            dk = jnp.where(left, dk2[:C], dk2[C:]) + later[j][:, PAIR:]
            grad[here, 512 + PAIR * j : 512 + PAIR * (j + 1)] = dk.astype(BF16)
        for j in PAIRS:
            new = jnp.concatenate((mm_tn(g[j], do[j]), mm_tn(dn[j], part(0, j))), axis=1)
            r[j] += jnp.where(same2, new, 0.0)
        return 0

    lax.fori_loop(0, count, step, 0, unroll=UNROLL)
    for ref, end in zip((r, carry), ends):
        end[...] = ref[...]


def attention_backward(clock, qkvf, saved, d_o, first, count, states=()):
    rows = count * CHUNK
    outs = [shape((rows, 2048))]
    if first - count >= 0:
        outs += [shape((4, PAIR, 2 * PAIR), F32), shape((8, 512), F32)]
    kernel = functools.partial(backward_kernel, first, count, qkvf.shape[0] // CHUNK - 1)
    scratch = [pltpu.VMEM((4, PAIR, 2 * PAIR), F32), pltpu.VMEM((8, 512), F32)]
    return call(clock, kernel, "attention_backward", outs, [qkvf, *saved, d_o, *states], scratch)


def gelu_parts(v):
    c = 0.7978845608028654
    k = c * 0.044715
    v2 = v * v
    half = 0.5 * jnp.tanh(v * (c + k * v2)) + 0.5
    act = v * half
    return act, half + act * (1.0 - half) * (2 * c + (6 * k) * v2)


def middle_kernel(token, tokens, mixed, *refs):
    wo, packs, (resid_out, n2_out, r2_out, a2_out, scr) = refs[:4], refs[4:8], refs[8:]
    blocks = blocks_of(token)
    gain, shift = vector(packs, 256, 128), vector(packs, 384, 128)

    def body(rows):
        resid = tokens[rows, :].astype(F32) + mm(take_blocks(mixed, rows, blocks, 128), stack(wo))
        resid_out[rows, :] = resid
        n2, r2 = stats(resid)
        scr[...] = n2
        n2 = take_blocks(scr, slice(None), blocks, 128)
        n2_out[rows, :] = n2.astype(BF16)
        r2_out[rows, :] = jnp.broadcast_to(r2, (ROWS, 128))
        a2_out[rows, :] = (n2 * gain + shift).astype(BF16)

    row_loop(tokens.shape[0], body)


def middle(clock, tokens, mixed, wo, packs):
    T = tokens.shape[0]
    outs = [shape((T, 512), F32), shape((T, 512)), shape((T, 128), F32), shape((T, 512))]
    return call(clock, middle_kernel, "middle", outs, [tokens, mixed, *wo, *packs], [pltpu.VMEM((ROWS, 512), F32)])


def ffn_inner_kernel(token, a2_ref, *refs):
    wi, packs, (act_out, slope_out) = refs[:-6], refs[-6:-2], refs[-2:]
    cols = wide(blocks_of(token), 512)

    def body(rows):
        a2 = a2_ref[rows, :]
        inner = mm(a2, stack(wi, cols[0]))
        for i in range(4):
            after = mm(a2, stack(wi, cols[i + 1])) if i < 3 else None
            act, slope = gelu_parts(inner + packs[i][128:129, 640:1152].astype(F32))
            act_out[rows, 512 * i : 512 * (i + 1)] = act.astype(BF16)
            slope_out[rows, cols[i]] = slope.astype(BF16)
            inner = after

    row_loop(a2_ref.shape[0], body)


def ffn_inner(clock, a2, wi, packs):
    T = a2.shape[0]
    return call(clock, ffn_inner_kernel, "ffn_inner", [shape((T, 2048)), shape((T, 2048))], [a2, *wi, *packs])


def outer_grad_kernel(_, act, dy, keep, send):
    for i in range(4):
        out = mm_tn(act[:, 512 * i : 512 * (i + 1)], dy[...]).astype(BF16)
        (keep if i < 2 else send)[i % 2] = out


def outer_grad(clock, act, dy):
    return call(clock, outer_grad_kernel, "outer_grad", [shape((2, 512, 512))] * 2, [act, dy])


def ffn_outer_kernel(token, resid, act, *refs):
    wu, vs, (out, bias, result, sem) = refs[:4], refs[4:8], refs[8:]
    put_blocks(bias, slice(None), jnp.broadcast_to(vector(vs, 512, 128), (8, 512)), blocks_of(token), 128)

    def body(rows):
        result[rows, :] = (mm(act[rows, :], stack(wu)) + resid[rows, :] + bias[0:1, :]).astype(BF16)

    row_loop(act.shape[0], body)
    copy = pltpu.make_async_copy(result, out, sem)
    copy.start()
    copy.wait()


def ffn_outer(clock, resid, act, wu, vecs):
    scratch = [pltpu.VMEM((8, 512), F32), pltpu.VMEM(resid.shape, BF16), pltpu.SemaphoreType.DMA]
    return call(clock, ffn_outer_kernel, "ffn_outer", [shape(resid.shape)], [resid, act, *wu, *vecs], scratch, outside=(0,))[0]


def inner_back_kernel(which, more, token, dy, slope, *refs):
    cols = wide(blocks_of(token), 512)
    wu, (din, sums) = refs[:2], refs[-2:]
    if more:
        sums[...] = refs[2][...]
    else:
        sums[...] = jnp.zeros_like(sums)
        sums[1:2, 0:512] = jnp.sum(dy[...].astype(F32), axis=0, keepdims=True)
    for i, u in zip(which, wu):
        d = (mm_nt(dy[...], u[...]) * slope[:, cols[i]].astype(F32)).astype(BF16)
        din[:, cols[i]] = d
        sums[0:1, cols[i]] = jnp.sum(d.astype(F32), axis=0, keepdims=True)


def inner_back(clock, dy, slope, wu, which, sums=()):
    T = dy.shape[0]
    kernel = functools.partial(inner_back_kernel, which, len(sums) > 0)
    return call(clock, kernel, "inner_back", [shape((T, 2048)), shape((8, 2048), F32)], [dy, slope, *wu, *sums], aliases={1: 0})


def inner_grad_kernel(first, _, n2, din, sums, out):
    m = mm_tn(n2[:, 128 * first : 128 * (first + 2)], din[...]).astype(BF16)
    tail = jnp.concatenate((sums[...], jnp.zeros_like(sums)), axis=0).astype(BF16)
    for k in range(2):
        out[k, 0:128, :] = m[128 * k : 128 * (k + 1), :]
        out[k, 128:144, :] = tail


def inner_grad(clock, n2, din, sums, first):
    return call(clock, functools.partial(inner_grad_kernel, first), "inner_grad", [shape((2, 144, 2048))], [n2, din, sums])[0]


def resid_back_kernel(token, dy, n2, r2, din, *refs):
    wo, wi, packs = refs[:4], refs[4:-7], refs[-7:-3]
    dres_out, do_out, scr = refs[-3:]
    blocks = blocks_of(token)
    gain = vector(packs, 256, 128)

    def body(rows):
        da2 = mm_nt(din[rows, :], stack(wi))
        put_blocks(scr, slice(None), norm_back(da2 * gain, n2[rows, :].astype(F32), r2[rows, 0:1]), blocks, 128)
        dres = dy[rows, :].astype(F32) + scr[...]
        dres_out[rows, :] = dres
        d_o = mm_nt(dres.astype(BF16), stack(wo))
        put_blocks(do_out, rows, d_o.astype(BF16), blocks, 128)

    row_loop(dy.shape[0], body)


def resid_back(clock, dy, n2, r2, din, wo, wi, packs):
    T = dy.shape[0]
    outs = [shape((T, 512), F32), shape((T, 512))]
    return call(clock, resid_back_kernel, "resid_back", outs, [dy, n2, r2, din, *wo, *wi, *packs], [pltpu.VMEM((ROWS, 512), F32)])


def project_grad_kernel(first, token, n1, early, late, mixed, dres, out):
    half = early.shape[0]
    blocks = wide(blocks_of(token), 128)
    n = n1[:, 128 * first : 128 * (first + 2)]
    d = dres[...].astype(BF16)
    for start in (0, 1024):
        cols = slice(start, start + 1024)
        m = (mm_tn(n[0:half], early[:, cols]) + mm_tn(n[half:], late[:, cols])).astype(BF16)
        total = sum(jnp.sum(r[:, cols].astype(F32), axis=0, keepdims=True) for r in (early, late))
        tail = jnp.broadcast_to(total, (16, 1024)).astype(BF16)
        for k in range(2):
            out[k, 0:128, cols] = m[128 * k : 128 * (k + 1)]
            out[k, 128:144, cols] = tail
    for k in range(2):
        out[k, 0:128, 2048:] = mm_tn(mixed[:, blocks[first + k]], d).astype(BF16)
        out[k, 128:144, 2048:] = jnp.zeros((16, 512), BF16)


def project_grad(clock, n1, early, late, mixed, dres, first):
    return call(clock, functools.partial(project_grad_kernel, first), "project_grad", [shape((2, 144, 2560))], [n1, early, late, mixed, dres])[0]


def input_grad_kernel(token, tokens, early, late, dres, p0, p1, p2, p3, out, scr, result, sems):
    packs = (p0, p1, p2, p3)
    blocks = blocks_of(token)
    gain = vector(packs, 0, 128)
    w = stack_packs(packs, slice(0, 2048))
    copies = []
    for h, d in enumerate((early, late)):
        rows = slice(ROWS * h, ROWS * (h + 1))
        e = mm_nt(d[...], w) * gain
        n1, r1 = stats(tokens[rows, :].astype(F32))
        scr[...] = n1
        put_blocks(scr, slice(None), norm_back(e, take_blocks(scr, slice(None), blocks, 128), r1), blocks, 128)
        result[rows, :] = (dres[rows, :] + scr[...]).astype(BF16)
        copies.append(pltpu.make_async_copy(result.at[rows, :], out.at[rows, :], sems.at[h]))
        copies[-1].start()
    for copy in copies:
        copy.wait()


def input_grad(clock, tokens, early, late, dres, packs):
    scratch = [pltpu.VMEM((ROWS, 512), F32), pltpu.VMEM(dres.shape, BF16), pltpu.SemaphoreType.DMA((2,))]
    return call(clock, input_grad_kernel, "input_grad", [shape(dres.shape)], [tokens, early, late, dres, *packs], scratch, outside=(0,))[0]


def exchange(value, axis, size, mask):
    return lax.ppermute(value, axis, [(i, i ^ mask) for i in range(size)])


def over_x(value):
    return exchange(value, "fsdp", 4, 2)


def over_core(value):
    return exchange(value, "fsdp", 4, 1)


def add(a, b):
    return a.astype(F32) + b.astype(F32)


def half_at(bit, width):
    return pl.ds(pl.multiple_of(bit * (width // 2), width // 2), width // 2)


def gate_kernel(*refs):
    pass


def gate(clock, waited, values):
    n = len(waited)
    outs = [shape(v.shape, v.dtype) for v in values]
    return call(clock, gate_kernel, "gate", outs, [*waited, *values], limit=1, aliases={n + k: k for k in range(len(values))})


def quarter(ref, token, mask):
    width = ref.shape[1] // 4
    place = position(token, 1) ^ mask
    return pl.ds(pl.multiple_of((2 * lax.rem(place, 2) + lax.rem(lax.div(place, 2), 2)) * width, width), width)


def join_kernel(kind, mask, after, token, keep, *refs):
    after_kind, after_mask, n_sends = after
    n_outs = 1 + n_sends
    gots, outs, whole = refs[: -1 - n_outs], refs[-1 - n_outs : -1], refs[-1]
    bit = lambda m: lax.rem(lax.div(position(token, 1), m), 2)
    if kind == "core":
        rows = keep.shape[1]
        for k in range(2):
            whole[rows * k : rows * (k + 1), :] = add(keep[k], gots[0][k]).astype(BF16)
    elif kind == "beside":
        whole[:, half_at(bit(mask), whole.shape[1])] = keep[...]
        whole[:, half_at(1 - bit(mask), whole.shape[1])] = gots[0][...]
    elif kind == "besides":
        for m, got in enumerate((keep, *gots)):
            whole[:, quarter(whole, token, m)] = got[...]
    elif kind == "x":
        start = 0
        for got in gots:
            rows = slice(start, start + got.shape[0])
            whole[rows, :] = add(keep[rows, :], got[...]).astype(BF16)
            start += got.shape[0]
    else:
        total = keep[...].astype(F32)
        for got in gots:
            total = total + got[...].astype(F32)
        whole[...] = total.astype(BF16)
    if after_kind == "half":
        outs[0][...] = whole[:, half_at(bit(after_mask), whole.shape[1])]
        outs[1][...] = whole[:, half_at(1 - bit(after_mask), whole.shape[1])]
    elif after_kind == "quarter":
        for m, out in enumerate(outs):
            out[...] = whole[:, quarter(whole, token, m)]
    else:
        start = 0
        for out in outs:
            out[...] = whole[start : start + out.shape[0], :]
            start += out.shape[0]


class Chain:
    def __init__(self, clock, dp, steps, send, pieces=()):
        self.clock, self.dp = clock, dp
        self.pieces = pieces or (send.shape[1],)
        masks = [1 << k for k in range(dp.bit_length() - 1)]
        used = [1, 2] if "quarter" in steps else [m for m in masks if f"half{m}" in steps]
        self.todo = []
        for name in steps:
            if name == "all":
                self.todo += [("all", m) for m in masks if m not in used]
            else:
                kind = name.rstrip("0123456789")
                self.todo.append((kind, int(name[len(kind) :] or 0)))
        self.send = [send]
        self.busy = True
        self.launch()

    def launch(self):
        self.kind, self.mask = self.todo.pop(0)
        self.split = 0
        if self.kind == "core":
            self.got = [over_core(self.send[0])]
        elif self.kind == "x":
            self.got = [over_x(self.send.pop(0))]
            self.split = len(self.send)
        elif self.kind == "quarter":
            self.got = [exchange(v, "dp", self.dp, m) for m, v in enumerate(self.send, 1)]
        elif self.kind == "besides":
            self.got = [exchange(self.keep, "dp", self.dp, m) for m in (1, 2, 3)]
        else:
            self.got = [exchange(self.send[0], "dp", self.dp, self.mask)]

    def more(self):
        self.got.append(over_x(gate(self.clock, [self.got[-1]], [self.send.pop(0)])[0]))
        self.split -= 1

    def step(self):
        rows, width = self.keep.shape[-2:]
        rows = 2 * rows if self.kind == "core" else rows
        width = width * {"beside": 2, "besides": 4}.get(self.kind, 1)
        kind, mask = self.todo[0] if self.todo else ("", 0)
        if kind == "half":
            dims = [(rows, width // 2)] * 2
        elif kind == "quarter":
            dims = [(rows, width // 4)] * 4
        elif kind == "x":
            dims = [(n, width) for n in (rows // 2, *self.pieces)]
        else:
            dims = [(rows, width)]
        kernel = functools.partial(join_kernel, self.kind, self.mask, (kind, mask, len(dims) - 1))
        self.keep, *self.send = call(self.clock, kernel, "join", [shape(d) for d in dims], [self.keep, *self.got], [pltpu.VMEM((rows, width), BF16)], limit=JOIN)
        self.send = self.send or [self.keep]
        self.busy = bool(self.todo)
        if self.busy:
            self.launch()


def column(row):
    r = lax.broadcasted_iota(jnp.int32, (128, 128), 0)
    c = lax.broadcasted_iota(jnp.int32, (128, 128), 1)
    return jnp.sum(jnp.where(r == c, row, 0.0), axis=1, keepdims=True)


def as_row(col):
    r = lax.broadcasted_iota(jnp.int32, (128, 128), 0)
    c = lax.broadcasted_iota(jnp.int32, (128, 128), 1)
    return jnp.sum(jnp.where(r == c, col, 0.0), axis=0, keepdims=True)


def send_out(pairs, sems):
    copies = [pltpu.make_async_copy(src, dst, sems.at[k]) for k, (src, dst) in enumerate(pairs)]
    for copy in copies:
        copy.start()
    for copy in copies:
        copy.wait()


def finish_outer_kernel(_, u, out, buf, sems):
    buf[...] = u[...].astype(F32)
    send_out([(buf, out)], sems)


def finish_outer(clock, u):
    return call(clock, finish_outer_kernel, "finish_outer", [shape(u.shape, F32)], [u], [pltpu.VMEM(u.shape, F32), pltpu.SemaphoreType.DMA((1,))], limit=JOIN, outside=(0,))[0]


def finish_inner_kernel(token, total, w, pack, out, gain_out, shift_out, inner_out, outer_out, buf, small, sems):
    gain, shift = (column(pack[128:129, k : k + 128].astype(F32)) for k in (256, 384))
    m = total[0:128, :].astype(F32)
    tail = total[128:144, :].astype(F32)
    buf[...] = gain * m + shift * tail[0:1, :]
    wf = w[...].astype(F32)
    small[0:1, 0:128] = as_row(jnp.sum(wf * m, axis=1, keepdims=True))
    small[1:2, 0:128] = as_row(jnp.sum(wf * tail[0:1, :], axis=1, keepdims=True))
    me = position(token, 0)
    small[2:3, :] = total[128:144, pl.ds(pl.multiple_of(me * 512, 512), 512)].astype(F32)[0:1, :]
    small[3:4, 0:128] = total[128:144, pl.ds(pl.multiple_of(me * 128, 128), 128)].astype(F32)[1:2, :]
    send_out([(buf, out), (small.at[0, 0:128], gain_out), (small.at[1, 0:128], shift_out), (small.at[2], inner_out), (small.at[3, 0:128], outer_out)], sems)


def finish_inner(clock, total, w, pack):
    outs = [shape((128, 2048), F32), shape((128,), F32), shape((128,), F32), shape((512,), F32), shape((128,), F32)]
    scratch = [pltpu.VMEM((128, 2048), F32), pltpu.VMEM((8, 512), F32), pltpu.SemaphoreType.DMA((5,))]
    return call(clock, finish_inner_kernel, "finish_inner", outs, [total, w, pack], scratch, limit=JOIN, outside=range(5))


def finish_project_kernel(_, total, pack, *refs):
    outs, (buf, small, sems) = refs[:-3], refs[-3:]
    gain, shift = (column(pack[128:129, k : k + 128].astype(F32)) for k in (0, 128))
    m = total[0:128, 0:2048].astype(F32)
    tail = total[128:144, 0:2048].astype(F32)[0:1, :]
    buf[:, 0:2048] = gain * m + shift * tail
    buf[:, 2048:2560] = total[0:128, 2048:2560].astype(F32)
    copies = [pltpu.make_async_copy(buf.at[:, 512 * k : 512 * (k + 1)], out, sems.at[k]) for k, out in enumerate(outs[:5])]
    for copy in copies:
        copy.start()
    w = pack[0:128, :].astype(F32)
    small[0:1, :] = as_row(jnp.sum(w * m, axis=1, keepdims=True))
    small[1:2, :] = as_row(jnp.sum(w * tail, axis=1, keepdims=True))
    more = [pltpu.make_async_copy(small.at[k], out, sems.at[5 + k]) for k, out in enumerate(outs[5:])]
    for copy in more:
        copy.start()
    for copy in copies + more:
        copy.wait()


def finish_project(clock, total, pack):
    outs = [shape((128, 512), F32)] * 5 + [shape((128,), F32)] * 2
    scratch = [pltpu.VMEM((128, 2560), F32), pltpu.VMEM((8, 128), F32), pltpu.SemaphoreType.DMA((7,))]
    return call(clock, finish_project_kernel, "finish_project", outs, [total, pack], scratch, limit=JOIN, outside=range(7))


PLAN = (
    "OG", "IA", "WU", "IB", "u", "IS", "IK", "i", "RB", "u", "AE", "u", "i", "AL", "u", "i", "PS", "PK",
    "p", "IN", "i", "u", "FO", "u", "p", "i", "p", "u", "i", "p", "u",
)
STEPS = {
    "u": ("core", "x", "half1", "half2", "all", "beside2", "beside1"),
    "i": ("core", "quarter", "x", "all", "beside2", "beside1"),
    "p": ("core", "x", "quarter", "all", "besides"),
}
PIECES = {"u": (272, 240), "i": (), "p": ()}


def per_device(dp, tokens, first_gain, first_shift, w_query, w_key, w_value, w_control, w_output, second_gain, second_shift, w_inner, inner_bias, w_outer, outer_bias, cotangent):
    clock = Clock(lax.axis_index("fsdp").astype(jnp.int32), lax.axis_index("dp").astype(jnp.int32))
    vectors = (first_gain, first_shift, second_gain, second_shift, outer_bias, inner_bias)
    own, first, second, wi0, wi1 = begin(clock, (w_query, w_key, w_value, w_control), vectors, w_inner)
    mine = [over_x(first), over_x(second)]
    own_core, wi_c = over_core(own), over_core(w_inner)
    n1, n1_low = first_norm(clock, tokens)
    *mine, wi0, wi1, w_output = clock.sync(*mine, wi0, wi1, w_output)
    wi_x0 = over_x(wi0)
    across = assemble(clock, mine, [exchange(v, "dp", dp, k + 1) for k, v in enumerate(mine)], wi_x0)
    packs = [own, across, own_core, over_core(across)]
    wi1, w_output = clock.sync(wi1, w_output)
    wi_x1, wo_x, wo_c = over_x(wi1), over_x(w_output), over_core(w_output)
    qkvf = project(clock, n1, packs)
    w_outer = clock.sync(w_outer)
    wu_x, wu_c = over_x(w_outer), over_core(w_outer)
    mixed, *saved = attention_forward(clock, qkvf)
    wo_x, wi_x1 = clock.sync(wo_x, wi_x1)
    wo = [w_output, wo_x, wo_c, over_core(wo_x)]
    wi = [w_inner, wi_x0, wi_x1, wi_c, over_core(wi_x0), over_core(wi_x1)]
    resid, n2, r2, a2 = middle(clock, tokens, mixed, wo, packs)
    act, slope = ffn_inner(clock, a2, wi, packs)
    chains, made = {}, {}

    def start(name, send, keep):
        chains[name] = Chain(clock, dp, STEPS[name], send, PIECES[name])
        made[name] = keep

    def outer():
        keep, send = outer_grad(clock, act, cotangent)
        start("u", send, lambda: keep)

    def wait_outer():
        wu_x = clock.sync(made["wu"])
        made["wu"] = [w_outer, wu_x, wu_c, over_core(wu_x)]

    def back_near():
        made["din"] = inner_back(clock, cotangent, slope, [w_outer, wu_c], (0, 2))

    def back_far():
        d, partial = made["din"]
        made["din"] = inner_back(clock, cotangent, d, [made["wu"][1], made["wu"][3]], (1, 3), [partial])

    def inner_send():
        start("i", inner_grad(clock, n2, *made["din"], 2), None)

    def inner_keep():
        made["i"] = inner_grad(clock, n2, *made["din"], 0)

    def resid_grad():
        made["dres"], made["do"] = resid_back(clock, cotangent, n2, r2, made["din"][0], wo, wi, packs)

    def early():
        made["early"] = attention_backward(clock, qkvf, saved, made["do"], 7, 4)

    def late():
        made["late"] = attention_backward(clock, qkvf, saved, made["do"], 3, 4, made["early"][1:])

    def project_part(first):
        return project_grad(clock, n1_low, made["late"][0], made["early"][0], mixed, made["dres"], first)

    def project_send():
        start("p", project_part(2), None)

    def project_keep():
        made["p"] = project_part(0)

    def input_part():
        made["tokens"] = input_grad(clock, tokens, made["late"][0], made["early"][0], made["dres"], packs)

    def output_part():
        made["output"] = ffn_outer(clock, resid, act, made["wu"], packs)

    def finish(name):
        total = chains[name].keep
        if name == "u":
            made["outer"] = finish_outer(clock, total)
        elif name == "i":
            made["inner"] = finish_inner(clock, total, w_inner, packs[0])
        else:
            made["project"] = finish_project(clock, total, packs[0])

    def advance(name):
        c = chains[name]
        if not c.busy:
            return
        if c.kind == "core":
            keep = made[name]
            c.keep = keep() if callable(keep) else keep
        if c.split:
            c.more()
        else:
            c.step()
            if not c.busy:
                finish(name)

    made["wu"] = wu_x
    kernels = dict(OG=outer, WU=wait_outer, IA=back_near, IB=back_far, IS=inner_send, IK=inner_keep, RB=resid_grad, AE=early, AL=late, PS=project_send, PK=project_keep, IN=input_part, FO=output_part)
    for word in PLAN:
        if word in kernels:
            kernels[word]()
        else:
            advance(word)
    while any(c.busy for c in chains.values()):
        for name in "uip":
            advance(name)
    output, grad_tokens, grad_outer = made["output"], made["tokens"], made["outer"]
    grad_inner, *vectors = made["inner"]
    grad_query, grad_key, grad_value, grad_control, grad_output, first_gain_grad, first_shift_grad = made["project"]
    second_gain_grad, second_shift_grad, inner_bias_grad, outer_bias_grad = vectors
    return (
        output, grad_tokens, first_gain_grad, first_shift_grad, grad_query, grad_key, grad_value, grad_control,
        grad_output, second_gain_grad, second_shift_grad, grad_inner, inner_bias_grad, grad_outer, outer_bias_grad,
    )


def solution(mesh):
    row, vec, mat = P(("dp", "fsdp"), None), P("fsdp"), P("fsdp", None)
    return jax.shard_map(
        functools.partial(per_device, mesh.shape["dp"]),
        mesh=mesh,
        in_specs=(row, vec, vec, mat, mat, mat, mat, mat, vec, vec, mat, vec, mat, vec, row),
        out_specs=(row, row, vec, vec, mat, mat, mat, mat, mat, vec, vec, mat, vec, mat, vec),
        check_vma=False,
    )
```

```python
import functools

import jax
import jax.numpy as jnp
from jax import lax
from jax.experimental import pallas as pl
from jax.experimental.pallas import tpu as pltpu
from jax.sharding import PartitionSpec as P

F32 = jnp.float32
BF16 = jnp.bfloat16
PAIR = 128
PAIRS = range(4)
SCALE = 64 ** -0.5
CHUNK = 128
UNROLL = 2
JOIN = 4
ROWS = 512
WHOLE = 1024
EPS = 1e-5
WEIGHT = 1000
MASKS = (0, 2, 1, 3)
VM = pl.BlockSpec(memory_space=pltpu.VMEM)
SM = pl.BlockSpec(memory_space=pltpu.SMEM)
ANY = pl.BlockSpec(memory_space=pl.ANY)


def mm(a, b):
    return lax.dot_general(a, b, (((1,), (0,)), ((), ())), preferred_element_type=F32)


def mm_nt(a, b):
    return lax.dot_general(a, b, (((1,), (1,)), ((), ())), preferred_element_type=F32)


def mm_tn(a, b):
    return lax.dot_general(a, b, (((0,), (0,)), ((), ())), preferred_element_type=F32)


def shape(dims, dtype=BF16):
    return jax.ShapeDtypeStruct(dims, dtype)


class Clock:
    def __init__(self, me, place):
        row = lax.broadcasted_iota(jnp.int32, (8, 128), 0)
        self.token = jnp.where(row == 0, me, place)

    def sync(self, *values):
        self.token, values = lax.optimization_barrier((self.token, values))
        return values if len(values) > 1 else values[0]


def call(clock, kernel, name, outs, args, scratch=(), limit=8, outside=(), raw=(), aliases=None):
    n_in, n_out = len(args), len(outs)

    def body(token, *refs):
        outs_at = n_in + n_out
        refs[outs_at][...] = token[...]
        kernel(token, *refs[:outs_at], *refs[outs_at + 1 :])

    place = lambda k, o: (pltpu.HBM if k in outside else pltpu.VMEM)(o.shape, o.dtype)
    args = [pltpu.with_memory_space_constraint(a, pltpu.HBM if k in raw else pltpu.VMEM) for k, a in enumerate(args)]
    *results, clock.token = pl.pallas_call(
        body,
        in_specs=[VM] + [ANY if k in raw else VM for k in range(n_in)],
        out_specs=[ANY if k in outside else VM for k in range(n_out)] + [VM],
        out_shape=[place(k, o) for k, o in enumerate(outs)] + [pltpu.VMEM((8, 128), jnp.int32)],
        scratch_shapes=list(scratch),
        input_output_aliases={i + 1: o for i, o in (aliases or {}).items()},
        compiler_params=pltpu.CompilerParams(vmem_limit_bytes=limit << 20),
        cost_estimate=pl.CostEstimate(flops=WEIGHT, bytes_accessed=1 << 10, transcendentals=0),
        name=name,
    )(pltpu.with_memory_space_constraint(clock.token, pltpu.VMEM), *args)
    return results


def position(token, row):
    return jnp.max(token[row : row + 1, :])


def blocks_of(token):
    me = position(token, 0)
    return [me ^ mask for mask in MASKS]


def wide(blocks, width):
    return [pl.ds(pl.multiple_of(b * width, width), width) for b in blocks]


def take_blocks(ref, rows, blocks, width):
    return jnp.concatenate([ref[rows, cols] for cols in wide(blocks, width)], axis=1)


def put_blocks(ref, rows, values, blocks, width):
    for i, cols in enumerate(wide(blocks, width)):
        ref[rows, cols] = values[:, i * width : (i + 1) * width]


def stack(refs, cols=slice(None)):
    return jnp.concatenate([r[:, cols] for r in refs], axis=0)


def stack_packs(packs, cols):
    return jnp.concatenate([r[0:128, cols] for r in packs], axis=0)


def vector(packs, start, width):
    return jnp.concatenate([r[128:129, start : start + width] for r in packs], axis=1).astype(F32)


def row_loop(T, body, rows=ROWS):
    def step(c, _):
        body(pl.ds(pl.multiple_of(c * rows, rows), rows))
        return 0

    if rows < T:
        lax.fori_loop(0, T // rows, step, 0)
    else:
        body(slice(None))


def stats(x):
    mean = jnp.mean(x, axis=1, keepdims=True)
    centred = x - mean
    inv = lax.rsqrt(jnp.mean(centred * centred, axis=1, keepdims=True) + EPS)
    return centred * inv, inv


def norm_back(grad, normed, inv):
    return inv * (grad - jnp.mean(grad, axis=1, keepdims=True) - normed * jnp.mean(grad * normed, axis=1, keepdims=True))


def parity(token):
    place = position(token, 1)
    return lax.rem(place + lax.div(place, 2), 2)


def begin_kernel(token, *refs):
    weights, vecs, inner, (out, first, second, wi0, wi1), rest = refs[:4], refs[4:10], refs[10], refs[11:16], refs[16:]
    bufs, sems = rest[:6], rest[6]
    cols = [slice(512 * n, 512 * (n + 1)) for n in range(4)]
    copies = [pltpu.make_async_copy(w, out.at[0:128, c], sems.at[n]) for n, (w, c) in enumerate(zip(weights, cols))]
    copies += [pltpu.make_async_copy(v, b, sems.at[4 + n]) for n, (v, b) in enumerate(zip(vecs, bufs))]
    copies += [pltpu.make_async_copy(inner.at[64 * n : 64 * (n + 1), :], w, sems.at[10 + n]) for n, w in enumerate((wi0, wi1))]
    for copy in copies:
        copy.start()
    for copy in copies:
        copy.wait()
    vec = jnp.concatenate([b[...].reshape(1, -1).astype(F32) for b in bufs] + [jnp.zeros((1, 896), F32)], axis=1)
    out[128:144, :] = jnp.broadcast_to(vec, (16, 2048)).astype(BF16)
    odd = parity(token)
    for k, piece in enumerate((first, second)):
        piece[...] = out[:, pl.ds(pl.multiple_of(odd * 1024 + 512 * k, 512), 512)]


def begin(clock, weights, vecs, inner):
    scratch = [pltpu.VMEM(v.shape, BF16) for v in vecs] + [pltpu.SemaphoreType.DMA((12,))]
    outs = [shape((144, 2048)), shape((144, 512)), shape((144, 512)), shape((64, 2048)), shape((64, 2048))]
    return call(clock, begin_kernel, "begin", outs, [*weights, *vecs, inner], scratch, limit=JOIN, raw=range(11))


def assemble_kernel(token, mine0, mine1, other0, other1, _, out):
    odd = parity(token)
    for half, pieces in ((odd, (mine0, mine1)), (1 - odd, (other0, other1))):
        for k, piece in enumerate(pieces):
            out[:, pl.ds(pl.multiple_of(half * 1024 + 512 * k, 512), 512)] = piece[...]


def assemble(clock, mine, other, waited):
    return call(clock, assemble_kernel, "assemble", [shape((144, 2048))], [*mine, *other, waited], limit=JOIN)[0]


def first_norm_kernel(token, tokens, n1, n1_low, scr):
    blocks = blocks_of(token)

    def body(rows):
        n, _ = stats(tokens[rows, :].astype(F32))
        scr[...] = n
        n = take_blocks(scr, slice(None), blocks, 128)
        n1[rows, :] = n
        n1_low[rows, :] = n.astype(BF16)

    row_loop(tokens.shape[0], body)


def first_norm(clock, tokens):
    T = tokens.shape[0]
    return call(clock, first_norm_kernel, "first_norm", [shape((T, 512), F32), shape((T, 512))], [tokens], [pltpu.VMEM((ROWS, 512), F32)])


def project_kernel(_, n1, p0, p1, p2, p3, qkvf):
    packs = (p0, p1, p2, p3)
    gain, shift = vector(packs, 0, 128), vector(packs, 128, 128)

    def body(rows):
        a1 = (n1[rows, :] * gain + shift).astype(BF16)
        for n in range(4):
            cols = slice(512 * n, 512 * (n + 1))
            out = mm(a1, stack_packs(packs, cols))
            qkvf[rows, cols] = (jnp.exp(out) if n == 3 else out).astype(BF16)

    row_loop(n1.shape[0], body, WHOLE)


def project(clock, n1, packs):
    T = n1.shape[0]
    return call(clock, project_kernel, "project", [shape((T, 2048))], [n1, *packs])[0]


def left_half(rows):
    return lax.broadcasted_iota(jnp.int32, (rows, PAIR), 1) < 64


def split_pair(x, left):
    zero = jnp.zeros((), x.dtype)
    return jnp.concatenate((jnp.where(left, x, zero), jnp.where(left, zero, x)), axis=0)


def same_head():
    r = lax.broadcasted_iota(jnp.int32, (PAIR, PAIR), 0) < 64
    c = lax.broadcasted_iota(jnp.int32, (PAIR, PAIR), 1) < 64
    return r == c


def causal_pair(rows):
    r = lax.broadcasted_iota(jnp.int32, (rows, 2 * rows), 0)
    c = lax.broadcasted_iota(jnp.int32, (rows, 2 * rows), 1)
    return r >= jnp.where(c >= rows, c - rows, c)


def triangle(rows):
    return lax.broadcasted_iota(jnp.int32, (rows, rows), 0) >= lax.broadcasted_iota(jnp.int32, (rows, rows), 1)


def half_reduce(x, left, fn, fill):
    a = fn(jnp.where(left, x, fill), axis=1, keepdims=True)
    b = fn(jnp.where(left, fill, x), axis=1, keepdims=True)
    return jnp.where(left, a, b)


def pair_of(j):
    return slice(PAIR * j, PAIR * (j + 1))


def a_of(j):
    return slice(256 * j, 256 * (j + 1))


def b_of(j):
    return slice(1024 + 256 * j, 1024 + 256 * (j + 1))


def s_of(j):
    return slice(2048 + PAIR * j, 2048 + PAIR * (j + 1))


def g_of(j):
    return slice(2560 + PAIR * j, 2560 + PAIR * (j + 1))


KEPT = 3072


def chunk_rows(c):
    return pl.ds(pl.multiple_of(c * CHUNK, CHUNK), CHUNK)


def forward_kernel(_, qkvf, mixed, kept, states, carry_out, s1, s2, carry):
    C = CHUNK
    s1[...] = jnp.zeros_like(s1)
    s2[...] = jnp.zeros_like(s2)
    carry[...] = jnp.zeros_like(carry)
    left = left_half(C)
    causal = causal_pair(C)
    same = same_head()
    lower = triangle(C).astype(BF16)
    zero = jnp.zeros((), BF16)

    def step(c, _):
        rows = chunk_rows(c)
        part = lambda n, j: qkvf[rows, 512 * n + PAIR * j : 512 * n + PAIR * (j + 1)]
        raw = [mm_nt(part(0, j), split_pair(part(1, j), left)) for j in PAIRS]
        carry_out[c] = carry[...]
        denom = mm(lower, qkvf[rows, 1536:2048]) + carry[0:1, :]
        carry[0:1, :] = denom[C - 1 :, :]
        rden_all = 1.0 / denom
        f2 = [split_pair(part(3, j), left) for j in PAIRS]
        numer = []
        for j in PAIRS:
            a2 = jnp.where(causal, raw[j].astype(BF16), zero)
            kept[rows, a_of(j)] = a2
            s1b = s1[j].astype(BF16)
            states[c, :, pair_of(j)] = s1b
            numer.append(mm(a2, f2[j]) + mm(part(0, j), s1b))
        g = []
        for j in PAIRS:
            rden = rden_all[:, pair_of(j)]
            s = numer[j] * rden * SCALE
            kept[rows, s_of(j)] = s.astype(BF16)
            e = jnp.exp(s - half_reduce(s, left, jnp.max, -jnp.inf))
            p = e / half_reduce(e, left, jnp.sum, 0.0)
            g.append((p * rden).astype(BF16))
            kept[rows, g_of(j)] = g[j]
        raw = [mm_nt(g[j], f2[j]) for j in PAIRS]
        for j in PAIRS:
            b2 = jnp.where(causal, raw[j].astype(BF16), zero)
            kept[rows, b_of(j)] = b2
            s2b = s2[j].astype(BF16)
            states[c, :, pair_of(4 + j)] = s2b
            o = mm(b2, split_pair(part(2, j), left)) + mm(g[j], s2b)
            mixed[rows, pair_of(j)] = o.astype(BF16)
        for j in PAIRS:
            s1[j] += jnp.where(same, mm_tn(part(1, j), part(3, j)), 0.0)
            s2[j] += jnp.where(same, mm_tn(part(3, j), part(2, j)), 0.0)
        return 0

    lax.fori_loop(0, qkvf.shape[0] // C, step, 0, unroll=UNROLL)


def state_scratch():
    return [pltpu.VMEM((4, PAIR, PAIR), F32), pltpu.VMEM((4, PAIR, PAIR), F32), pltpu.VMEM((8, 512), F32)]


def attention_forward(clock, qkvf):
    T = qkvf.shape[0]
    n = T // CHUNK
    outs = [shape((T, 512)), shape((T, KEPT)), shape((n, PAIR, 1024)), shape((n, 8, 512), F32)]
    return call(clock, forward_kernel, "attention_forward", outs, [qkvf], state_scratch())


def backward_kernel(first, count, last, _, qkvf, kept, states, carry_in, do_in, *refs):
    C = CHUNK
    r, carry = refs[-2:]
    begins, (grad, *ends) = (refs[:2], refs[2:-2]) if first < last else ((), refs[:-2])
    for ref, old in zip((r, carry), begins or (None,) * 2):
        ref[...] = jnp.zeros_like(ref) if old is None else old[...]
    left = left_half(C)
    causal = causal_pair(C)
    same = same_head()
    same2 = jnp.concatenate((same, same), axis=1)
    lower = triangle(C).astype(BF16)
    upper = lower.T
    upper2 = jnp.concatenate((upper, upper), axis=1)
    zero = jnp.zeros((), BF16)

    def step(t, _):
        c = first - t
        rows = chunk_rows(c)
        here = chunk_rows(count - 1 - t)
        part = lambda n, j: qkvf[rows, 512 * n + PAIR * j : 512 * n + PAIR * (j + 1)]
        do = [do_in[rows, pair_of(j)] for j in PAIRS]
        denoms = mm(lower, qkvf[rows, 1536:2048]) + carry_in[c][0:1, :]
        s1b = [states[c, :, pair_of(j)] for j in PAIRS]
        s2b = [states[c, :, pair_of(4 + j)] for j in PAIRS]
        rb = [r[j].astype(BF16) for j in PAIRS]
        g = [kept[rows, g_of(j)] for j in PAIRS]
        raw = [mm_nt(do[j], split_pair(part(2, j), left)) for j in PAIRS]
        f2 = [split_pair(part(3, j), left) for j in PAIRS]
        db2, dg, dn, dd, later = [], [], [], [], []
        for j in PAIRS:
            db2.append(jnp.where(causal, raw[j].astype(BF16), zero))
            dg.append(mm(db2[j], f2[j]) + mm_nt(do[j], s2b[j]))
        for j in PAIRS:
            later.append(mm(part(3, j), rb[j]))
            dv2 = mm_tn(kept[rows, b_of(j)], do[j])
            dv = jnp.where(left, dv2[:C], dv2[C:]) + later[j][:, :PAIR]
            grad[here, 1024 + PAIR * j : 1024 + PAIR * (j + 1)] = dv.astype(BF16)
        for j in PAIRS:
            denom = denoms[:, pair_of(j)]
            rden = 1.0 / denom
            p = g[j].astype(F32) * denom
            dpp = dg[j] * rden * p
            ds = dpp - p * half_reduce(dpp, left, jnp.sum, 0.0)
            dd.append(-(dpp + ds * kept[rows, s_of(j)].astype(F32)) * rden)
            dn.append((ds * SCALE * rden).astype(BF16))
        raw = [mm_nt(dn[j], f2[j]) for j in PAIRS]
        sums = []
        for k in (0, 2):
            d = jnp.concatenate((dd[k], dd[k + 1]), axis=1)
            hi = d.astype(BF16)
            lo = (d - hi.astype(F32)).astype(BF16)
            total = mm(upper2, jnp.concatenate((hi, lo), axis=0))
            sums += [total[:, :PAIR], total[:, PAIR:]]
        for j in PAIRS:
            df2 = mm_tn(jnp.concatenate((db2[j], kept[rows, a_of(j)]), axis=0), jnp.concatenate((g[j], dn[j]), axis=0))
            df = jnp.where(left, df2[:C], df2[C:]) + mm_nt(jnp.concatenate((part(2, j), part(1, j)), axis=1), rb[j])
            df = df + sums[j] + carry[0:1, pair_of(j)]
            grad[here, 1536 + PAIR * j : 1536 + PAIR * (j + 1)] = (df * part(3, j).astype(F32)).astype(BF16)
            carry[0:1, pair_of(j)] += jnp.sum(dd[j], axis=0, keepdims=True)
        for j in PAIRS:
            da2 = jnp.where(causal, raw[j].astype(BF16), zero)
            dq = mm(da2, split_pair(part(1, j), left)) + mm_nt(dn[j], s1b[j])
            grad[here, pair_of(j)] = dq.astype(BF16)
            dk2 = mm_tn(da2, part(0, j))
            dk = jnp.where(left, dk2[:C], dk2[C:]) + later[j][:, PAIR:]
            grad[here, 512 + PAIR * j : 512 + PAIR * (j + 1)] = dk.astype(BF16)
        for j in PAIRS:
            new = jnp.concatenate((mm_tn(g[j], do[j]), mm_tn(dn[j], part(0, j))), axis=1)
            r[j] += jnp.where(same2, new, 0.0)
        return 0

    lax.fori_loop(0, count, step, 0, unroll=UNROLL)
    for ref, end in zip((r, carry), ends):
        end[...] = ref[...]


def attention_backward(clock, qkvf, saved, d_o, first, count, states=()):
    rows = count * CHUNK
    outs = [shape((rows, 2048))]
    if first - count >= 0:
        outs += [shape((4, PAIR, 2 * PAIR), F32), shape((8, 512), F32)]
    kernel = functools.partial(backward_kernel, first, count, qkvf.shape[0] // CHUNK - 1)
    scratch = [pltpu.VMEM((4, PAIR, 2 * PAIR), F32), pltpu.VMEM((8, 512), F32)]
    return call(clock, kernel, "attention_backward", outs, [qkvf, *saved, d_o, *states], scratch)


def gelu_parts(v):
    c = 0.7978845608028654
    k = c * 0.044715
    v2 = v * v
    half = 0.5 * jnp.tanh(v * (c + k * v2)) + 0.5
    act = v * half
    return act, half + act * (1.0 - half) * (2 * c + (6 * k) * v2)


def middle_kernel(token, tokens, mixed, *refs):
    wo, packs, (resid_out, n2_out, r2_out, a2_out, scr) = refs[:4], refs[4:8], refs[8:]
    blocks = blocks_of(token)
    gain, shift = vector(packs, 256, 128), vector(packs, 384, 128)

    def body(rows):
        resid = tokens[rows, :].astype(F32) + mm(take_blocks(mixed, rows, blocks, 128), stack(wo))
        resid_out[rows, :] = resid
        n2, r2 = stats(resid)
        scr[...] = n2
        n2 = take_blocks(scr, slice(None), blocks, 128)
        n2_out[rows, :] = n2.astype(BF16)
        r2_out[rows, :] = jnp.broadcast_to(r2, (ROWS, 128))
        a2_out[rows, :] = (n2 * gain + shift).astype(BF16)

    row_loop(tokens.shape[0], body)


def middle(clock, tokens, mixed, wo, packs):
    T = tokens.shape[0]
    outs = [shape((T, 512), F32), shape((T, 512)), shape((T, 128), F32), shape((T, 512))]
    return call(clock, middle_kernel, "middle", outs, [tokens, mixed, *wo, *packs], [pltpu.VMEM((ROWS, 512), F32)])


def ffn_inner_kernel(token, a2_ref, *refs):
    wi, packs, (act_out, slope_out) = refs[:-6], refs[-6:-2], refs[-2:]
    cols = wide(blocks_of(token), 512)

    def body(rows):
        a2 = a2_ref[rows, :]
        inner = mm(a2, stack(wi, cols[0]))
        for i in range(4):
            after = mm(a2, stack(wi, cols[i + 1])) if i < 3 else None
            act, slope = gelu_parts(inner + packs[i][128:129, 640:1152].astype(F32))
            act_out[rows, 512 * i : 512 * (i + 1)] = act.astype(BF16)
            slope_out[rows, cols[i]] = slope.astype(BF16)
            inner = after

    row_loop(a2_ref.shape[0], body)


def ffn_inner(clock, a2, wi, packs):
    T = a2.shape[0]
    return call(clock, ffn_inner_kernel, "ffn_inner", [shape((T, 2048)), shape((T, 2048))], [a2, *wi, *packs])


def outer_grad_kernel(_, act, dy, keep, send):
    for i in range(4):
        out = mm_tn(act[:, 512 * i : 512 * (i + 1)], dy[...]).astype(BF16)
        (keep if i < 2 else send)[i % 2] = out


def outer_grad(clock, act, dy):
    return call(clock, outer_grad_kernel, "outer_grad", [shape((2, 512, 512))] * 2, [act, dy])


def ffn_outer_kernel(token, resid, act, *refs):
    wu, vs, (out, bias, result, sem) = refs[:4], refs[4:8], refs[8:]
    put_blocks(bias, slice(None), jnp.broadcast_to(vector(vs, 512, 128), (8, 512)), blocks_of(token), 128)

    def body(rows):
        result[rows, :] = (mm(act[rows, :], stack(wu)) + resid[rows, :] + bias[0:1, :]).astype(BF16)

    row_loop(act.shape[0], body)
    copy = pltpu.make_async_copy(result, out, sem)
    copy.start()
    copy.wait()


def ffn_outer(clock, resid, act, wu, vecs):
    scratch = [pltpu.VMEM((8, 512), F32), pltpu.VMEM(resid.shape, BF16), pltpu.SemaphoreType.DMA]
    return call(clock, ffn_outer_kernel, "ffn_outer", [shape(resid.shape)], [resid, act, *wu, *vecs], scratch, outside=(0,))[0]


def inner_back_kernel(which, more, token, dy, slope, *refs):
    cols = wide(blocks_of(token), 512)
    wu, (din, sums) = refs[:2], refs[-2:]
    if more:
        sums[...] = refs[2][...]
    else:
        sums[...] = jnp.zeros_like(sums)
        sums[1:2, 0:512] = jnp.sum(dy[...].astype(F32), axis=0, keepdims=True)
    for i, u in zip(which, wu):
        d = (mm_nt(dy[...], u[...]) * slope[:, cols[i]].astype(F32)).astype(BF16)
        din[:, cols[i]] = d
        sums[0:1, cols[i]] = jnp.sum(d.astype(F32), axis=0, keepdims=True)


def inner_back(clock, dy, slope, wu, which, sums=()):
    T = dy.shape[0]
    kernel = functools.partial(inner_back_kernel, which, len(sums) > 0)
    return call(clock, kernel, "inner_back", [shape((T, 2048)), shape((8, 2048), F32)], [dy, slope, *wu, *sums], aliases={1: 0})


def inner_grad_kernel(first, _, n2, din, sums, out):
    m = mm_tn(n2[:, 128 * first : 128 * (first + 2)], din[...]).astype(BF16)
    tail = jnp.concatenate((sums[...], jnp.zeros_like(sums)), axis=0).astype(BF16)
    for k in range(2):
        out[k, 0:128, :] = m[128 * k : 128 * (k + 1), :]
        out[k, 128:144, :] = tail


def inner_grad(clock, n2, din, sums, first):
    return call(clock, functools.partial(inner_grad_kernel, first), "inner_grad", [shape((2, 144, 2048))], [n2, din, sums])[0]


def resid_back_kernel(token, dy, n2, r2, din, *refs):
    wo, wi, packs = refs[:4], refs[4:-7], refs[-7:-3]
    dres_out, do_out, scr = refs[-3:]
    blocks = blocks_of(token)
    gain = vector(packs, 256, 128)

    def body(rows):
        da2 = mm_nt(din[rows, :], stack(wi))
        put_blocks(scr, slice(None), norm_back(da2 * gain, n2[rows, :].astype(F32), r2[rows, 0:1]), blocks, 128)
        dres = dy[rows, :].astype(F32) + scr[...]
        dres_out[rows, :] = dres
        d_o = mm_nt(dres.astype(BF16), stack(wo))
        put_blocks(do_out, rows, d_o.astype(BF16), blocks, 128)

    row_loop(dy.shape[0], body)


def resid_back(clock, dy, n2, r2, din, wo, wi, packs):
    T = dy.shape[0]
    outs = [shape((T, 512), F32), shape((T, 512))]
    return call(clock, resid_back_kernel, "resid_back", outs, [dy, n2, r2, din, *wo, *wi, *packs], [pltpu.VMEM((ROWS, 512), F32)])


def project_grad_kernel(first, starts, token, n1, early, late, mixed, dres, out):
    half = early.shape[0]
    blocks = wide(blocks_of(token), 128)
    n = n1[:, 128 * first : 128 * (first + 2)]
    for at, start in enumerate(starts):
        cols, dest = slice(start, start + 1024), slice(1024 * at, 1024 * (at + 1))
        m = (mm_tn(n[0:half], early[:, cols]) + mm_tn(n[half:], late[:, cols])).astype(BF16)
        total = sum(jnp.sum(r[:, cols].astype(F32), axis=0, keepdims=True) for r in (early, late))
        tail = jnp.broadcast_to(total, (16, 1024)).astype(BF16)
        for k in range(2):
            out[k, 0:128, dest] = m[128 * k : 128 * (k + 1)]
            out[k, 128:144, dest] = tail
    rest = 1024 * len(starts)
    if rest < out.shape[2]:
        d = dres[...].astype(BF16)
        for k in range(2):
            out[k, 0:128, rest:] = mm_tn(mixed[:, blocks[first + k]], d).astype(BF16)
            out[k, 128:144, rest:] = jnp.zeros((16, 512), BF16)


def project_grad(clock, n1, early, late, mixed, dres, first, starts=(0, 1024)):
    width = 1024 * len(starts) + (512 if 1024 in starts else 0)
    kernel = functools.partial(project_grad_kernel, first, starts)
    return call(clock, kernel, "project_grad", [shape((2, 144, width))], [n1, early, late, mixed, dres])[0]


def input_grad_kernel(token, tokens, early, late, dres, p0, p1, p2, p3, out, scr, result, sems):
    packs = (p0, p1, p2, p3)
    blocks = blocks_of(token)
    gain = vector(packs, 0, 128)
    w = stack_packs(packs, slice(0, 2048))
    copies = []
    for h, d in enumerate((early, late)):
        rows = slice(ROWS * h, ROWS * (h + 1))
        e = mm_nt(d[...], w) * gain
        n1, r1 = stats(tokens[rows, :].astype(F32))
        scr[...] = n1
        put_blocks(scr, slice(None), norm_back(e, take_blocks(scr, slice(None), blocks, 128), r1), blocks, 128)
        result[rows, :] = (dres[rows, :] + scr[...]).astype(BF16)
        copies.append(pltpu.make_async_copy(result.at[rows, :], out.at[rows, :], sems.at[h]))
        copies[-1].start()
    for copy in copies:
        copy.wait()


def input_grad(clock, tokens, early, late, dres, packs):
    scratch = [pltpu.VMEM((ROWS, 512), F32), pltpu.VMEM(dres.shape, BF16), pltpu.SemaphoreType.DMA((2,))]
    return call(clock, input_grad_kernel, "input_grad", [shape(dres.shape)], [tokens, early, late, dres, *packs], scratch, outside=(0,))[0]


def exchange(value, axis, size, mask):
    return lax.ppermute(value, axis, [(i, i ^ mask) for i in range(size)])


def over_x(value):
    return exchange(value, "fsdp", 4, 2)


def over_core(value):
    return exchange(value, "fsdp", 4, 1)


def add(a, b):
    return a.astype(F32) + b.astype(F32)


def half_at(bit, width):
    return pl.ds(pl.multiple_of(bit * (width // 2), width // 2), width // 2)


def gate_kernel(*refs):
    pass


def gate(clock, waited, values):
    n = len(waited)
    outs = [shape(v.shape, v.dtype) for v in values]
    return call(clock, gate_kernel, "gate", outs, [*waited, *values], limit=1, aliases={n + k: k for k in range(len(values))})


def quarter(ref, token, mask):
    width = ref.shape[1] // 4
    place = position(token, 1) ^ mask
    return pl.ds(pl.multiple_of((2 * lax.rem(place, 2) + lax.rem(lax.div(place, 2), 2)) * width, width), width)


def join_kernel(kind, mask, after, token, keep, *refs):
    after_kind, after_mask, n_sends = after
    n_outs = 1 + n_sends
    gots, outs, whole = refs[: -1 - n_outs], refs[-1 - n_outs : -1], refs[-1]
    bit = lambda m: lax.rem(lax.div(position(token, 1), m), 2)
    if kind == "core":
        rows, start = keep.shape[1], 0
        for got in gots:
            cols = slice(start, start + got.shape[2])
            for k in range(2):
                whole[rows * k : rows * (k + 1), cols] = add(keep[k, :, cols], got[k]).astype(BF16)
            start += got.shape[2]
    elif kind == "beside":
        whole[:, half_at(bit(mask), whole.shape[1])] = keep[...]
        whole[:, half_at(1 - bit(mask), whole.shape[1])] = gots[0][...]
    elif kind == "besides":
        for m, got in enumerate((keep, *gots)):
            whole[:, quarter(whole, token, m)] = got[...]
    elif kind == "x":
        start = 0
        for got in gots:
            rows = slice(start, start + got.shape[0])
            whole[rows, :] = add(keep[rows, :], got[...]).astype(BF16)
            start += got.shape[0]
    else:
        total = keep[...].astype(F32)
        for got in gots:
            total = total + got[...].astype(F32)
        whole[...] = total.astype(BF16)
    if after_kind == "half":
        outs[0][...] = whole[:, half_at(bit(after_mask), whole.shape[1])]
        outs[1][...] = whole[:, half_at(1 - bit(after_mask), whole.shape[1])]
    elif after_kind == "quarter":
        for m, out in enumerate(outs):
            out[...] = whole[:, quarter(whole, token, m)]
    else:
        start = 0
        for out in outs:
            out[...] = whole[start : start + out.shape[0], :]
            start += out.shape[0]


class Chain:
    def __init__(self, clock, dp, steps, send, pieces=()):
        self.clock, self.dp = clock, dp
        self.pieces = pieces or (send[0].shape[1],)
        masks = [1 << k for k in range(dp.bit_length() - 1)]
        used = [1, 2] if "quarter" in steps else [m for m in masks if f"half{m}" in steps]
        self.todo = []
        for name in steps:
            if name == "all":
                self.todo += [("all", m) for m in masks if m not in used]
            else:
                kind = name.rstrip("0123456789")
                self.todo.append((kind, int(name[len(kind) :] or 0)))
        self.send = send
        self.busy = True
        self.launch()

    def launch(self):
        self.kind, self.mask = self.todo.pop(0)
        self.split = 0
        if self.kind == "core":
            self.got = [over_core(v) for v in self.send]
        elif self.kind == "x":
            self.got = [over_x(self.send.pop(0))]
            self.split = len(self.send)
        elif self.kind == "quarter":
            self.got = [exchange(v, "dp", self.dp, m) for m, v in enumerate(self.send, 1)]
        elif self.kind == "besides":
            self.got = [exchange(self.keep, "dp", self.dp, m) for m in (1, 2, 3)]
        else:
            self.got = [exchange(self.send[0], "dp", self.dp, self.mask)]

    def more(self):
        self.got.append(over_x(gate(self.clock, [self.got[-1]], [self.send.pop(0)])[0]))
        self.split -= 1

    def step(self):
        rows, width = self.keep.shape[-2:]
        rows = 2 * rows if self.kind == "core" else rows
        width = width * {"beside": 2, "besides": 4}.get(self.kind, 1)
        kind, mask = self.todo[0] if self.todo else ("", 0)
        if kind == "half":
            dims = [(rows, width // 2)] * 2
        elif kind == "quarter":
            dims = [(rows, width // 4)] * 4
        elif kind == "x":
            dims = [(n, width) for n in (rows // 2, *self.pieces)]
        else:
            dims = [(rows, width)]
        kernel = functools.partial(join_kernel, self.kind, self.mask, (kind, mask, len(dims) - 1))
        self.keep, *self.send = call(self.clock, kernel, "join", [shape(d) for d in dims], [self.keep, *self.got], [pltpu.VMEM((rows, width), BF16)], limit=JOIN)
        self.send = self.send or [self.keep]
        self.busy = bool(self.todo)
        if self.busy:
            self.launch()


def column(row):
    r = lax.broadcasted_iota(jnp.int32, (128, 128), 0)
    c = lax.broadcasted_iota(jnp.int32, (128, 128), 1)
    return jnp.sum(jnp.where(r == c, row, 0.0), axis=1, keepdims=True)


def as_row(col):
    r = lax.broadcasted_iota(jnp.int32, (128, 128), 0)
    c = lax.broadcasted_iota(jnp.int32, (128, 128), 1)
    return jnp.sum(jnp.where(r == c, col, 0.0), axis=0, keepdims=True)


def send_out(pairs, sems):
    copies = [pltpu.make_async_copy(src, dst, sems.at[k]) for k, (src, dst) in enumerate(pairs)]
    for copy in copies:
        copy.start()
    for copy in copies:
        copy.wait()


def finish_outer_kernel(_, u, out, buf, sems):
    buf[...] = u[...].astype(F32)
    send_out([(buf, out)], sems)


def finish_outer(clock, u):
    return call(clock, finish_outer_kernel, "finish_outer", [shape(u.shape, F32)], [u], [pltpu.VMEM(u.shape, F32), pltpu.SemaphoreType.DMA((1,))], limit=JOIN, outside=(0,))[0]


def finish_inner_kernel(token, total, w, pack, out, gain_out, shift_out, inner_out, outer_out, buf, small, sems):
    gain, shift = (column(pack[128:129, k : k + 128].astype(F32)) for k in (256, 384))
    m = total[0:128, :].astype(F32)
    tail = total[128:144, :].astype(F32)
    buf[...] = gain * m + shift * tail[0:1, :]
    wf = w[...].astype(F32)
    small[0:1, 0:128] = as_row(jnp.sum(wf * m, axis=1, keepdims=True))
    small[1:2, 0:128] = as_row(jnp.sum(wf * tail[0:1, :], axis=1, keepdims=True))
    me = position(token, 0)
    small[2:3, :] = total[128:144, pl.ds(pl.multiple_of(me * 512, 512), 512)].astype(F32)[0:1, :]
    small[3:4, 0:128] = total[128:144, pl.ds(pl.multiple_of(me * 128, 128), 128)].astype(F32)[1:2, :]
    send_out([(buf, out), (small.at[0, 0:128], gain_out), (small.at[1, 0:128], shift_out), (small.at[2], inner_out), (small.at[3, 0:128], outer_out)], sems)


def finish_inner(clock, total, w, pack):
    outs = [shape((128, 2048), F32), shape((128,), F32), shape((128,), F32), shape((512,), F32), shape((128,), F32)]
    scratch = [pltpu.VMEM((128, 2048), F32), pltpu.VMEM((8, 512), F32), pltpu.SemaphoreType.DMA((5,))]
    return call(clock, finish_inner_kernel, "finish_inner", outs, [total, w, pack], scratch, limit=JOIN, outside=range(5))


def finish_project_kernel(_, total, pack, *refs):
    outs, (buf, small, sems) = refs[:-3], refs[-3:]
    gain, shift = (column(pack[128:129, k : k + 128].astype(F32)) for k in (0, 128))
    copies = []
    for k, out in enumerate(outs[:5]):
        cols = slice(512 * k, 512 * (k + 1))
        part = total[0:128, cols].astype(F32)
        buf[:, cols] = gain * part + shift * total[128:144, cols].astype(F32)[0:1, :] if k < 4 else part
        copies.append(pltpu.make_async_copy(buf.at[:, cols], out, sems.at[k]))
        copies[-1].start()
    m = total[0:128, 0:2048].astype(F32)
    tail = total[128:144, 0:2048].astype(F32)[0:1, :]
    w = pack[0:128, :].astype(F32)
    small[0:1, :] = as_row(jnp.sum(w * m, axis=1, keepdims=True))
    small[1:2, :] = as_row(jnp.sum(w * tail, axis=1, keepdims=True))
    more = [pltpu.make_async_copy(small.at[k], out, sems.at[5 + k]) for k, out in enumerate(outs[5:])]
    for copy in more:
        copy.start()
    for copy in copies + more:
        copy.wait()


def finish_project(clock, total, pack):
    outs = [shape((128, 512), F32)] * 5 + [shape((128,), F32)] * 2
    scratch = [pltpu.VMEM((128, 2560), F32), pltpu.VMEM((8, 128), F32), pltpu.SemaphoreType.DMA((7,))]
    return call(clock, finish_project_kernel, "finish_project", outs, [total, pack], scratch, limit=JOIN, outside=range(7))


PLAN = (
    "OG", "IA", "WU", "IB", "u", "IS", "IK", "i", "RB", "AE", "u", "i", "AL", "u", "i", "PS", "PK", "p",
    "IN", "u", "i", "FO", "u", "p", "i", "p", "u", "i", "p", "u",
)
STEPS = {
    "u": ("core", "x", "half1", "half2", "all", "beside2", "beside1"),
    "i": ("core", "quarter", "x", "all", "beside2", "beside1"),
    "p": ("core", "x", "quarter", "all", "besides"),
}
PIECES = {"u": (512,), "i": (), "p": ()}


def per_device(dp, tokens, first_gain, first_shift, w_query, w_key, w_value, w_control, w_output, second_gain, second_shift, w_inner, inner_bias, w_outer, outer_bias, cotangent):
    clock = Clock(lax.axis_index("fsdp").astype(jnp.int32), lax.axis_index("dp").astype(jnp.int32))
    vectors = (first_gain, first_shift, second_gain, second_shift, outer_bias, inner_bias)
    own, first, second, wi0, wi1 = begin(clock, (w_query, w_key, w_value, w_control), vectors, w_inner)
    mine = [over_x(first), over_x(second)]
    own_core, wi_c = over_core(own), over_core(w_inner)
    n1, n1_low = first_norm(clock, tokens)
    *mine, wi0, wi1, w_output = clock.sync(*mine, wi0, wi1, w_output)
    wi_x0 = over_x(wi0)
    across = assemble(clock, mine, [exchange(v, "dp", dp, k + 1) for k, v in enumerate(mine)], wi_x0)
    packs = [own, across, own_core, over_core(across)]
    wi1, w_output = clock.sync(wi1, w_output)
    wi_x1, wo_x, wo_c = over_x(wi1), over_x(w_output), over_core(w_output)
    qkvf = project(clock, n1, packs)
    w_outer = clock.sync(w_outer)
    wu_x, wu_c = over_x(w_outer), over_core(w_outer)
    mixed, *saved = attention_forward(clock, qkvf)
    wo_x, wi_x1 = clock.sync(wo_x, wi_x1)
    wo = [w_output, wo_x, wo_c, over_core(wo_x)]
    wi = [w_inner, wi_x0, wi_x1, wi_c, over_core(wi_x0), over_core(wi_x1)]
    resid, n2, r2, a2 = middle(clock, tokens, mixed, wo, packs)
    act, slope = ffn_inner(clock, a2, wi, packs)
    chains, made = {}, {}

    def start(name, send, keep):
        chains[name] = Chain(clock, dp, STEPS[name], send, PIECES[name])
        made[name] = keep

    def outer():
        keep, send = outer_grad(clock, act, cotangent)
        start("u", [send], lambda: keep)

    def wait_outer():
        wu_x = clock.sync(made["wu"])
        made["wu"] = [w_outer, wu_x, wu_c, over_core(wu_x)]

    def back_near():
        made["din"] = inner_back(clock, cotangent, slope, [w_outer, wu_c], (0, 2))

    def back_far():
        d, partial = made["din"]
        made["din"] = inner_back(clock, cotangent, d, [made["wu"][1], made["wu"][3]], (1, 3), [partial])

    def inner_send():
        start("i", [inner_grad(clock, n2, *made["din"], 2)], None)

    def inner_keep():
        made["i"] = inner_grad(clock, n2, *made["din"], 0)

    def resid_grad():
        made["dres"], made["do"] = resid_back(clock, cotangent, n2, r2, made["din"][0], wo, wi, packs)

    def early():
        made["early"] = attention_backward(clock, qkvf, saved, made["do"], 7, 4)

    def late():
        made["late"] = attention_backward(clock, qkvf, saved, made["do"], 3, 4, made["early"][1:])

    def project_part(first):
        return project_grad(clock, n1_low, made["late"][0], made["early"][0], mixed, made["dres"], first)

    def project_send():
        start("p", [project_part(2)], None)

    def project_keep():
        made["p"] = project_part(0)

    def input_part():
        made["tokens"] = input_grad(clock, tokens, made["late"][0], made["early"][0], made["dres"], packs)

    def output_part():
        made["output"] = ffn_outer(clock, resid, act, made["wu"], packs)

    def finish(name):
        total = chains[name].keep
        if name == "u":
            made["outer"] = finish_outer(clock, total)
        elif name == "i":
            made["inner"] = finish_inner(clock, total, w_inner, packs[0])
        else:
            made["project"] = finish_project(clock, total, packs[0])

    def advance(name):
        c = chains[name]
        if not c.busy:
            return
        if c.kind == "core":
            keep = made[name]
            c.keep = keep() if callable(keep) else keep
        if c.split:
            c.more()
        else:
            c.step()
            if not c.busy:
                finish(name)

    made["wu"] = wu_x
    kernels = dict(OG=outer, WU=wait_outer, IA=back_near, IB=back_far, IS=inner_send, IK=inner_keep, RB=resid_grad, AE=early, AL=late, PS=project_send, PK=project_keep, IN=input_part, FO=output_part)
    for word in PLAN:
        if word in kernels:
            kernels[word]()
        else:
            advance(word)
    while any(c.busy for c in chains.values()):
        for name in "uip":
            advance(name)
    output, grad_tokens, grad_outer = made["output"], made["tokens"], made["outer"]
    grad_inner, *vectors = made["inner"]
    grad_query, grad_key, grad_value, grad_control, grad_output, first_gain_grad, first_shift_grad = made["project"]
    second_gain_grad, second_shift_grad, inner_bias_grad, outer_bias_grad = vectors
    return (
        output, grad_tokens, first_gain_grad, first_shift_grad, grad_query, grad_key, grad_value, grad_control,
        grad_output, second_gain_grad, second_shift_grad, grad_inner, inner_bias_grad, grad_outer, outer_bias_grad,
    )


def solution(mesh):
    row, vec, mat = P(("dp", "fsdp"), None), P("fsdp"), P("fsdp", None)
    return jax.shard_map(
        functools.partial(per_device, mesh.shape["dp"]),
        mesh=mesh,
        in_specs=(row, vec, vec, mat, mat, mat, mat, mat, vec, vec, mat, vec, mat, vec, row),
        out_specs=(row, row, vec, vec, mat, mat, mat, mat, mat, vec, vec, mat, vec, mat, vec),
        check_vma=False,
    )
```

```python
import functools

import jax
import jax.numpy as jnp
from jax import lax
from jax.experimental import pallas as pl
from jax.experimental.pallas import tpu as pltpu
from jax.sharding import PartitionSpec as P

F32 = jnp.float32
BF16 = jnp.bfloat16
PAIR = 128
PAIRS = range(4)
SCALE = 64 ** -0.5
CHUNK = 128
UNROLL = 2
JOIN = 4
ROWS = 512
WHOLE = 1024
EPS = 1e-5
WEIGHT = 1000
MASKS = (0, 2, 1, 3)
VM = pl.BlockSpec(memory_space=pltpu.VMEM)
SM = pl.BlockSpec(memory_space=pltpu.SMEM)
ANY = pl.BlockSpec(memory_space=pl.ANY)


def mm(a, b):
    return lax.dot_general(a, b, (((1,), (0,)), ((), ())), preferred_element_type=F32)


def mm_nt(a, b):
    return lax.dot_general(a, b, (((1,), (1,)), ((), ())), preferred_element_type=F32)


def mm_tn(a, b):
    return lax.dot_general(a, b, (((0,), (0,)), ((), ())), preferred_element_type=F32)


def shape(dims, dtype=BF16):
    return jax.ShapeDtypeStruct(dims, dtype)


class Clock:
    def __init__(self, me, place):
        row = lax.broadcasted_iota(jnp.int32, (8, 128), 0)
        self.token = jnp.where(row == 0, me, place)

    def sync(self, *values):
        self.token, values = lax.optimization_barrier((self.token, values))
        return values if len(values) > 1 else values[0]


def call(clock, kernel, name, outs, args, scratch=(), limit=8, outside=(), raw=(), aliases=None):
    n_in, n_out = len(args), len(outs)

    def body(token, *refs):
        outs_at = n_in + n_out
        refs[outs_at][...] = token[...]
        kernel(token, *refs[:outs_at], *refs[outs_at + 1 :])

    place = lambda k, o: (pltpu.HBM if k in outside else pltpu.VMEM)(o.shape, o.dtype)
    args = [pltpu.with_memory_space_constraint(a, pltpu.HBM if k in raw else pltpu.VMEM) for k, a in enumerate(args)]
    *results, clock.token = pl.pallas_call(
        body,
        in_specs=[VM] + [ANY if k in raw else VM for k in range(n_in)],
        out_specs=[ANY if k in outside else VM for k in range(n_out)] + [VM],
        out_shape=[place(k, o) for k, o in enumerate(outs)] + [pltpu.VMEM((8, 128), jnp.int32)],
        scratch_shapes=list(scratch),
        input_output_aliases={i + 1: o for i, o in (aliases or {}).items()},
        compiler_params=pltpu.CompilerParams(vmem_limit_bytes=limit << 20),
        cost_estimate=pl.CostEstimate(flops=WEIGHT, bytes_accessed=1 << 10, transcendentals=0),
        name=name,
    )(pltpu.with_memory_space_constraint(clock.token, pltpu.VMEM), *args)
    return results


def position(token, row):
    return jnp.max(token[row : row + 1, :])


def blocks_of(token):
    me = position(token, 0)
    return [me ^ mask for mask in MASKS]


def wide(blocks, width):
    return [pl.ds(pl.multiple_of(b * width, width), width) for b in blocks]


def take_blocks(ref, rows, blocks, width):
    return jnp.concatenate([ref[rows, cols] for cols in wide(blocks, width)], axis=1)


def put_blocks(ref, rows, values, blocks, width):
    for i, cols in enumerate(wide(blocks, width)):
        ref[rows, cols] = values[:, i * width : (i + 1) * width]


def stack(refs, cols=slice(None)):
    return jnp.concatenate([r[:, cols] for r in refs], axis=0)


def stack_packs(packs, cols):
    return jnp.concatenate([r[0:128, cols] for r in packs], axis=0)


def vector(packs, start, width):
    return jnp.concatenate([r[128:129, start : start + width] for r in packs], axis=1).astype(F32)


def row_loop(T, body, rows=ROWS):
    def step(c, _):
        body(pl.ds(pl.multiple_of(c * rows, rows), rows))
        return 0

    if rows < T:
        lax.fori_loop(0, T // rows, step, 0)
    else:
        body(slice(None))


def stats(x):
    mean = jnp.mean(x, axis=1, keepdims=True)
    centred = x - mean
    inv = lax.rsqrt(jnp.mean(centred * centred, axis=1, keepdims=True) + EPS)
    return centred * inv, inv


def norm_back(grad, normed, inv):
    return inv * (grad - jnp.mean(grad, axis=1, keepdims=True) - normed * jnp.mean(grad * normed, axis=1, keepdims=True))


def parity(token):
    place = position(token, 1)
    return lax.rem(place + lax.div(place, 2), 2)


def begin_kernel(token, *refs):
    weights, vecs, inner, (out, first, second, wi0, wi1), rest = refs[:4], refs[4:10], refs[10], refs[11:16], refs[16:]
    bufs, sems = rest[:6], rest[6]
    cols = [slice(512 * n, 512 * (n + 1)) for n in range(4)]
    copies = [pltpu.make_async_copy(w, out.at[0:128, c], sems.at[n]) for n, (w, c) in enumerate(zip(weights, cols))]
    copies += [pltpu.make_async_copy(v, b, sems.at[4 + n]) for n, (v, b) in enumerate(zip(vecs, bufs))]
    copies += [pltpu.make_async_copy(inner.at[64 * n : 64 * (n + 1), :], w, sems.at[10 + n]) for n, w in enumerate((wi0, wi1))]
    for copy in copies:
        copy.start()
    for copy in copies:
        copy.wait()
    vec = jnp.concatenate([b[...].reshape(1, -1).astype(F32) for b in bufs] + [jnp.zeros((1, 896), F32)], axis=1)
    out[128:144, :] = jnp.broadcast_to(vec, (16, 2048)).astype(BF16)
    odd = parity(token)
    for k, piece in enumerate((first, second)):
        piece[...] = out[:, pl.ds(pl.multiple_of(odd * 1024 + 512 * k, 512), 512)]


def begin(clock, weights, vecs, inner):
    scratch = [pltpu.VMEM(v.shape, BF16) for v in vecs] + [pltpu.SemaphoreType.DMA((12,))]
    outs = [shape((144, 2048)), shape((144, 512)), shape((144, 512)), shape((64, 2048)), shape((64, 2048))]
    return call(clock, begin_kernel, "begin", outs, [*weights, *vecs, inner], scratch, limit=JOIN, raw=range(11))


def assemble_kernel(token, mine0, mine1, other0, other1, _, out):
    odd = parity(token)
    for half, pieces in ((odd, (mine0, mine1)), (1 - odd, (other0, other1))):
        for k, piece in enumerate(pieces):
            out[:, pl.ds(pl.multiple_of(half * 1024 + 512 * k, 512), 512)] = piece[...]


def assemble(clock, mine, other, waited):
    return call(clock, assemble_kernel, "assemble", [shape((144, 2048))], [*mine, *other, waited], limit=JOIN)[0]


def first_norm_kernel(token, tokens, n1, n1_low, scr):
    blocks = blocks_of(token)

    def body(rows):
        n, _ = stats(tokens[rows, :].astype(F32))
        scr[...] = n
        n = take_blocks(scr, slice(None), blocks, 128)
        n1[rows, :] = n
        n1_low[rows, :] = n.astype(BF16)

    row_loop(tokens.shape[0], body)


def first_norm(clock, tokens):
    T = tokens.shape[0]
    return call(clock, first_norm_kernel, "first_norm", [shape((T, 512), F32), shape((T, 512))], [tokens], [pltpu.VMEM((ROWS, 512), F32)])


def project_kernel(_, n1, p0, p1, p2, p3, qkvf):
    packs = (p0, p1, p2, p3)
    gain, shift = vector(packs, 0, 128), vector(packs, 128, 128)

    def body(rows):
        a1 = (n1[rows, :] * gain + shift).astype(BF16)
        for n in range(4):
            cols = slice(512 * n, 512 * (n + 1))
            out = mm(a1, stack_packs(packs, cols))
            qkvf[rows, cols] = (jnp.exp(out) if n == 3 else out).astype(BF16)

    row_loop(n1.shape[0], body, WHOLE)


def project(clock, n1, packs):
    T = n1.shape[0]
    return call(clock, project_kernel, "project", [shape((T, 2048))], [n1, *packs])[0]


def left_half(rows):
    return lax.broadcasted_iota(jnp.int32, (rows, PAIR), 1) < 64


def split_pair(x, left):
    zero = jnp.zeros((), x.dtype)
    return jnp.concatenate((jnp.where(left, x, zero), jnp.where(left, zero, x)), axis=0)


def same_head():
    r = lax.broadcasted_iota(jnp.int32, (PAIR, PAIR), 0) < 64
    c = lax.broadcasted_iota(jnp.int32, (PAIR, PAIR), 1) < 64
    return r == c


def causal_pair(rows):
    r = lax.broadcasted_iota(jnp.int32, (rows, 2 * rows), 0)
    c = lax.broadcasted_iota(jnp.int32, (rows, 2 * rows), 1)
    return r >= jnp.where(c >= rows, c - rows, c)


def triangle(rows):
    return lax.broadcasted_iota(jnp.int32, (rows, rows), 0) >= lax.broadcasted_iota(jnp.int32, (rows, rows), 1)


def half_reduce(x, left, fn, fill):
    a = fn(jnp.where(left, x, fill), axis=1, keepdims=True)
    b = fn(jnp.where(left, fill, x), axis=1, keepdims=True)
    return jnp.where(left, a, b)


def pair_of(j):
    return slice(PAIR * j, PAIR * (j + 1))


def a_of(j):
    return slice(256 * j, 256 * (j + 1))


def b_of(j):
    return slice(1024 + 256 * j, 1024 + 256 * (j + 1))


def s_of(j):
    return slice(2048 + PAIR * j, 2048 + PAIR * (j + 1))


def g_of(j):
    return slice(2560 + PAIR * j, 2560 + PAIR * (j + 1))


KEPT = 3072


def chunk_rows(c):
    return pl.ds(pl.multiple_of(c * CHUNK, CHUNK), CHUNK)


def forward_kernel(_, qkvf, mixed, kept, states, carry_out, s1, s2, carry):
    C = CHUNK
    s1[...] = jnp.zeros_like(s1)
    s2[...] = jnp.zeros_like(s2)
    carry[...] = jnp.zeros_like(carry)
    left = left_half(C)
    causal = causal_pair(C)
    same = same_head()
    lower = triangle(C).astype(BF16)
    zero = jnp.zeros((), BF16)

    def step(c, _):
        rows = chunk_rows(c)
        part = lambda n, j: qkvf[rows, 512 * n + PAIR * j : 512 * n + PAIR * (j + 1)]
        raw = [mm_nt(part(0, j), split_pair(part(1, j), left)) for j in PAIRS]
        carry_out[c] = carry[...]
        denom = mm(lower, qkvf[rows, 1536:2048]) + carry[0:1, :]
        carry[0:1, :] = denom[C - 1 :, :]
        rden_all = 1.0 / denom
        f2 = [split_pair(part(3, j), left) for j in PAIRS]
        numer = []
        for j in PAIRS:
            a2 = jnp.where(causal, raw[j].astype(BF16), zero)
            kept[rows, a_of(j)] = a2
            s1b = s1[j].astype(BF16)
            states[c, :, pair_of(j)] = s1b
            numer.append(mm(a2, f2[j]) + mm(part(0, j), s1b))
        g = []
        for j in PAIRS:
            rden = rden_all[:, pair_of(j)]
            s = numer[j] * rden * SCALE
            kept[rows, s_of(j)] = s.astype(BF16)
            e = jnp.exp(s - half_reduce(s, left, jnp.max, -jnp.inf))
            p = e / half_reduce(e, left, jnp.sum, 0.0)
            g.append((p * rden).astype(BF16))
            kept[rows, g_of(j)] = g[j]
        raw = [mm_nt(g[j], f2[j]) for j in PAIRS]
        for j in PAIRS:
            b2 = jnp.where(causal, raw[j].astype(BF16), zero)
            kept[rows, b_of(j)] = b2
            s2b = s2[j].astype(BF16)
            states[c, :, pair_of(4 + j)] = s2b
            o = mm(b2, split_pair(part(2, j), left)) + mm(g[j], s2b)
            mixed[rows, pair_of(j)] = o.astype(BF16)
        for j in PAIRS:
            s1[j] += jnp.where(same, mm_tn(part(1, j), part(3, j)), 0.0)
            s2[j] += jnp.where(same, mm_tn(part(3, j), part(2, j)), 0.0)
        return 0

    lax.fori_loop(0, qkvf.shape[0] // C, step, 0, unroll=UNROLL)


def state_scratch():
    return [pltpu.VMEM((4, PAIR, PAIR), F32), pltpu.VMEM((4, PAIR, PAIR), F32), pltpu.VMEM((8, 512), F32)]


def attention_forward(clock, qkvf):
    T = qkvf.shape[0]
    n = T // CHUNK
    outs = [shape((T, 512)), shape((T, KEPT)), shape((n, PAIR, 1024)), shape((n, 8, 512), F32)]
    return call(clock, forward_kernel, "attention_forward", outs, [qkvf], state_scratch())


def backward_kernel(first, count, last, _, qkvf, kept, states, carry_in, do_in, *refs):
    C = CHUNK
    r, carry = refs[-2:]
    begins, (grad, *ends) = (refs[:2], refs[2:-2]) if first < last else ((), refs[:-2])
    for ref, old in zip((r, carry), begins or (None,) * 2):
        ref[...] = jnp.zeros_like(ref) if old is None else old[...]
    left = left_half(C)
    causal = causal_pair(C)
    same = same_head()
    same2 = jnp.concatenate((same, same), axis=1)
    lower = triangle(C).astype(BF16)
    upper = lower.T
    upper2 = jnp.concatenate((upper, upper), axis=1)
    zero = jnp.zeros((), BF16)

    def step(t, _):
        c = first - t
        rows = chunk_rows(c)
        here = chunk_rows(count - 1 - t)
        part = lambda n, j: qkvf[rows, 512 * n + PAIR * j : 512 * n + PAIR * (j + 1)]
        do = [do_in[rows, pair_of(j)] for j in PAIRS]
        denoms = mm(lower, qkvf[rows, 1536:2048]) + carry_in[c][0:1, :]
        s1b = [states[c, :, pair_of(j)] for j in PAIRS]
        s2b = [states[c, :, pair_of(4 + j)] for j in PAIRS]
        rb = [r[j].astype(BF16) for j in PAIRS]
        g = [kept[rows, g_of(j)] for j in PAIRS]
        raw = [mm_nt(do[j], split_pair(part(2, j), left)) for j in PAIRS]
        f2 = [split_pair(part(3, j), left) for j in PAIRS]
        db2, dg, dn, dd, later = [], [], [], [], []
        for j in PAIRS:
            db2.append(jnp.where(causal, raw[j].astype(BF16), zero))
            dg.append(mm(db2[j], f2[j]) + mm_nt(do[j], s2b[j]))
        for j in PAIRS:
            later.append(mm(part(3, j), rb[j]))
            dv2 = mm_tn(kept[rows, b_of(j)], do[j])
            dv = jnp.where(left, dv2[:C], dv2[C:]) + later[j][:, :PAIR]
            grad[here, 1024 + PAIR * j : 1024 + PAIR * (j + 1)] = dv.astype(BF16)
        for j in PAIRS:
            denom = denoms[:, pair_of(j)]
            rden = 1.0 / denom
            p = g[j].astype(F32) * denom
            dpp = dg[j] * rden * p
            ds = dpp - p * half_reduce(dpp, left, jnp.sum, 0.0)
            dd.append(-(dpp + ds * kept[rows, s_of(j)].astype(F32)) * rden)
            dn.append((ds * SCALE * rden).astype(BF16))
        raw = [mm_nt(dn[j], f2[j]) for j in PAIRS]
        sums = []
        for k in (0, 2):
            d = jnp.concatenate((dd[k], dd[k + 1]), axis=1)
            hi = d.astype(BF16)
            lo = (d - hi.astype(F32)).astype(BF16)
            total = mm(upper2, jnp.concatenate((hi, lo), axis=0))
            sums += [total[:, :PAIR], total[:, PAIR:]]
        for j in PAIRS:
            df2 = mm_tn(jnp.concatenate((db2[j], kept[rows, a_of(j)]), axis=0), jnp.concatenate((g[j], dn[j]), axis=0))
            df = jnp.where(left, df2[:C], df2[C:]) + mm_nt(jnp.concatenate((part(2, j), part(1, j)), axis=1), rb[j])
            df = df + sums[j] + carry[0:1, pair_of(j)]
            grad[here, 1536 + PAIR * j : 1536 + PAIR * (j + 1)] = (df * part(3, j).astype(F32)).astype(BF16)
            carry[0:1, pair_of(j)] += jnp.sum(dd[j], axis=0, keepdims=True)
        for j in PAIRS:
            da2 = jnp.where(causal, raw[j].astype(BF16), zero)
            dq = mm(da2, split_pair(part(1, j), left)) + mm_nt(dn[j], s1b[j])
            grad[here, pair_of(j)] = dq.astype(BF16)
            dk2 = mm_tn(da2, part(0, j))
            dk = jnp.where(left, dk2[:C], dk2[C:]) + later[j][:, PAIR:]
            grad[here, 512 + PAIR * j : 512 + PAIR * (j + 1)] = dk.astype(BF16)
        for j in PAIRS:
            new = jnp.concatenate((mm_tn(g[j], do[j]), mm_tn(dn[j], part(0, j))), axis=1)
            r[j] += jnp.where(same2, new, 0.0)
        return 0

    lax.fori_loop(0, count, step, 0, unroll=UNROLL)
    for ref, end in zip((r, carry), ends):
        end[...] = ref[...]


def attention_backward(clock, qkvf, saved, d_o, first, count, states=()):
    rows = count * CHUNK
    outs = [shape((rows, 2048))]
    if first - count >= 0:
        outs += [shape((4, PAIR, 2 * PAIR), F32), shape((8, 512), F32)]
    kernel = functools.partial(backward_kernel, first, count, qkvf.shape[0] // CHUNK - 1)
    scratch = [pltpu.VMEM((4, PAIR, 2 * PAIR), F32), pltpu.VMEM((8, 512), F32)]
    return call(clock, kernel, "attention_backward", outs, [qkvf, *saved, d_o, *states], scratch)


def gelu_parts(v):
    c = 0.7978845608028654
    k = c * 0.044715
    v2 = v * v
    half = 0.5 * jnp.tanh(v * (c + k * v2)) + 0.5
    act = v * half
    return act, half + act * (1.0 - half) * (2 * c + (6 * k) * v2)


def middle_kernel(token, tokens, mixed, *refs):
    wo, packs, (resid_out, n2_out, r2_out, a2_out, scr) = refs[:4], refs[4:8], refs[8:]
    blocks = blocks_of(token)
    gain, shift = vector(packs, 256, 128), vector(packs, 384, 128)

    def body(rows):
        resid = tokens[rows, :].astype(F32) + mm(take_blocks(mixed, rows, blocks, 128), stack(wo))
        resid_out[rows, :] = resid
        n2, r2 = stats(resid)
        scr[...] = n2
        n2 = take_blocks(scr, slice(None), blocks, 128)
        n2_out[rows, :] = n2.astype(BF16)
        r2_out[rows, :] = jnp.broadcast_to(r2, (ROWS, 128))
        a2_out[rows, :] = (n2 * gain + shift).astype(BF16)

    row_loop(tokens.shape[0], body)


def middle(clock, tokens, mixed, wo, packs):
    T = tokens.shape[0]
    outs = [shape((T, 512), F32), shape((T, 512)), shape((T, 128), F32), shape((T, 512))]
    return call(clock, middle_kernel, "middle", outs, [tokens, mixed, *wo, *packs], [pltpu.VMEM((ROWS, 512), F32)])


def ffn_inner_kernel(token, a2_ref, *refs):
    wi, packs, (act_out, slope_out) = refs[:-6], refs[-6:-2], refs[-2:]
    cols = wide(blocks_of(token), 512)

    def body(rows):
        a2 = a2_ref[rows, :]
        inner = mm(a2, stack(wi, cols[0]))
        for i in range(4):
            after = mm(a2, stack(wi, cols[i + 1])) if i < 3 else None
            act, slope = gelu_parts(inner + packs[i][128:129, 640:1152].astype(F32))
            act_out[rows, 512 * i : 512 * (i + 1)] = act.astype(BF16)
            slope_out[rows, cols[i]] = slope.astype(BF16)
            inner = after

    row_loop(a2_ref.shape[0], body)


def ffn_inner(clock, a2, wi, packs):
    T = a2.shape[0]
    return call(clock, ffn_inner_kernel, "ffn_inner", [shape((T, 2048)), shape((T, 2048))], [a2, *wi, *packs])


def outer_grad_kernel(_, act, dy, keep, send):
    for i in range(4):
        out = mm_tn(act[:, 512 * i : 512 * (i + 1)], dy[...]).astype(BF16)
        (keep if i < 2 else send)[i % 2] = out


def outer_grad(clock, act, dy):
    return call(clock, outer_grad_kernel, "outer_grad", [shape((2, 512, 512))] * 2, [act, dy])


def ffn_outer_kernel(token, resid, act, *refs):
    wu, vs, (out, bias, result, sem) = refs[:4], refs[4:8], refs[8:]
    put_blocks(bias, slice(None), jnp.broadcast_to(vector(vs, 512, 128), (8, 512)), blocks_of(token), 128)

    def body(rows):
        result[rows, :] = (mm(act[rows, :], stack(wu)) + resid[rows, :] + bias[0:1, :]).astype(BF16)

    row_loop(act.shape[0], body)
    copy = pltpu.make_async_copy(result, out, sem)
    copy.start()
    copy.wait()


def ffn_outer(clock, resid, act, wu, vecs):
    scratch = [pltpu.VMEM((8, 512), F32), pltpu.VMEM(resid.shape, BF16), pltpu.SemaphoreType.DMA]
    return call(clock, ffn_outer_kernel, "ffn_outer", [shape(resid.shape)], [resid, act, *wu, *vecs], scratch, outside=(0,))[0]


def inner_back_kernel(which, more, token, dy, slope, *refs):
    cols = wide(blocks_of(token), 512)
    wu, (din, sums) = refs[:2], refs[-2:]
    if more:
        sums[...] = refs[2][...]
    else:
        sums[...] = jnp.zeros_like(sums)
        sums[1:2, 0:512] = jnp.sum(dy[...].astype(F32), axis=0, keepdims=True)
    for i, u in zip(which, wu):
        d = (mm_nt(dy[...], u[...]) * slope[:, cols[i]].astype(F32)).astype(BF16)
        din[:, cols[i]] = d
        sums[0:1, cols[i]] = jnp.sum(d.astype(F32), axis=0, keepdims=True)


def inner_back(clock, dy, slope, wu, which, sums=()):
    T = dy.shape[0]
    kernel = functools.partial(inner_back_kernel, which, len(sums) > 0)
    return call(clock, kernel, "inner_back", [shape((T, 2048)), shape((8, 2048), F32)], [dy, slope, *wu, *sums], aliases={1: 0})


def inner_grad_kernel(first, _, n2, din, out):
    m = mm_tn(n2[:, 128 * first : 128 * (first + 2)], din[...]).astype(BF16)
    for k in range(2):
        out[k] = m[128 * k : 128 * (k + 1), :]


def inner_grad(clock, n2, din, first):
    return call(clock, functools.partial(inner_grad_kernel, first), "inner_grad", [shape((2, 128, 2048))], [n2, din])[0]


def resid_back_kernel(token, dy, n2, r2, din, *refs):
    wo, wi, packs = refs[:4], refs[4:-7], refs[-7:-3]
    dres_out, do_out, scr = refs[-3:]
    blocks = blocks_of(token)
    gain = vector(packs, 256, 128)

    def body(rows):
        da2 = mm_nt(din[rows, :], stack(wi))
        put_blocks(scr, slice(None), norm_back(da2 * gain, n2[rows, :].astype(F32), r2[rows, 0:1]), blocks, 128)
        dres = dy[rows, :].astype(F32) + scr[...]
        dres_out[rows, :] = dres
        d_o = mm_nt(dres.astype(BF16), stack(wo))
        put_blocks(do_out, rows, d_o.astype(BF16), blocks, 128)

    row_loop(dy.shape[0], body)


def resid_back(clock, dy, n2, r2, din, wo, wi, packs):
    T = dy.shape[0]
    outs = [shape((T, 512), F32), shape((T, 512))]
    return call(clock, resid_back_kernel, "resid_back", outs, [dy, n2, r2, din, *wo, *wi, *packs], [pltpu.VMEM((ROWS, 512), F32)])


def project_grad_kernel(first, starts, token, n1, early, late, mixed, dres, sums, out):
    half = early.shape[0]
    blocks = wide(blocks_of(token), 128)
    n = n1[:, 128 * first : 128 * (first + 2)]
    for at, start in enumerate(starts):
        cols, dest = slice(start, start + 1024), slice(1024 * at, 1024 * (at + 1))
        m = (mm_tn(n[0:half], early[:, cols]) + mm_tn(n[half:], late[:, cols])).astype(BF16)
        total = sum(jnp.sum(r[:, cols].astype(F32), axis=0, keepdims=True) for r in (early, late))
        row = lax.broadcasted_iota(jnp.int32, (16, 1024), 0)
        tail = jnp.where(row == 0, total, jnp.where(row == 1, sums[0:1, cols], sums[1:2, cols])).astype(BF16)
        for k in range(2):
            out[k, 0:128, dest] = m[128 * k : 128 * (k + 1)]
            out[k, 128:144, dest] = tail
    rest = 1024 * len(starts)
    if rest < out.shape[2]:
        d = dres[...].astype(BF16)
        for k in range(2):
            out[k, 0:128, rest:] = mm_tn(mixed[:, blocks[first + k]], d).astype(BF16)
            out[k, 128:144, rest:] = jnp.zeros((16, 512), BF16)


def project_grad(clock, n1, early, late, mixed, dres, sums, first, starts=(0, 1024)):
    width = 1024 * len(starts) + (512 if 1024 in starts else 0)
    kernel = functools.partial(project_grad_kernel, first, starts)
    return call(clock, kernel, "project_grad", [shape((2, 144, width))], [n1, early, late, mixed, dres, sums])[0]


def input_grad_kernel(token, tokens, early, late, dres, p0, p1, p2, p3, out, scr, result, sems):
    packs = (p0, p1, p2, p3)
    blocks = blocks_of(token)
    gain = vector(packs, 0, 128)
    w = stack_packs(packs, slice(0, 2048))
    copies = []
    for h, d in enumerate((early, late)):
        rows = slice(ROWS * h, ROWS * (h + 1))
        e = mm_nt(d[...], w) * gain
        n1, r1 = stats(tokens[rows, :].astype(F32))
        scr[...] = n1
        put_blocks(scr, slice(None), norm_back(e, take_blocks(scr, slice(None), blocks, 128), r1), blocks, 128)
        result[rows, :] = (dres[rows, :] + scr[...]).astype(BF16)
        copies.append(pltpu.make_async_copy(result.at[rows, :], out.at[rows, :], sems.at[h]))
        copies[-1].start()
    for copy in copies:
        copy.wait()


def input_grad(clock, tokens, early, late, dres, packs):
    scratch = [pltpu.VMEM((ROWS, 512), F32), pltpu.VMEM(dres.shape, BF16), pltpu.SemaphoreType.DMA((2,))]
    return call(clock, input_grad_kernel, "input_grad", [shape(dres.shape)], [tokens, early, late, dres, *packs], scratch, outside=(0,))[0]


def exchange(value, axis, size, mask):
    return lax.ppermute(value, axis, [(i, i ^ mask) for i in range(size)])


def over_x(value):
    return exchange(value, "fsdp", 4, 2)


def over_core(value):
    return exchange(value, "fsdp", 4, 1)


def add(a, b):
    return a.astype(F32) + b.astype(F32)


def half_at(bit, width):
    return pl.ds(pl.multiple_of(bit * (width // 2), width // 2), width // 2)


def gate_kernel(*refs):
    pass


def gate(clock, waited, values):
    n = len(waited)
    outs = [shape(v.shape, v.dtype) for v in values]
    return call(clock, gate_kernel, "gate", outs, [*waited, *values], limit=1, aliases={n + k: k for k in range(len(values))})


def quarter(ref, token, mask):
    width = ref.shape[1] // 4
    place = position(token, 1) ^ mask
    return pl.ds(pl.multiple_of((2 * lax.rem(place, 2) + lax.rem(lax.div(place, 2), 2)) * width, width), width)


def join_kernel(kind, mask, after, token, keep, *refs):
    after_kind, after_mask, n_sends = after
    n_outs = 1 + n_sends
    gots, outs, whole = refs[: -1 - n_outs], refs[-1 - n_outs : -1], refs[-1]
    bit = lambda m: lax.rem(lax.div(position(token, 1), m), 2)
    if kind == "core":
        rows, start = keep.shape[1], 0
        for got in gots:
            cols = slice(start, start + got.shape[2])
            for k in range(2):
                whole[rows * k : rows * (k + 1), cols] = add(keep[k, :, cols], got[k]).astype(BF16)
            start += got.shape[2]
    elif kind == "beside":
        whole[:, half_at(bit(mask), whole.shape[1])] = keep[...]
        whole[:, half_at(1 - bit(mask), whole.shape[1])] = gots[0][...]
    elif kind == "besides":
        for m, got in enumerate((keep, *gots)):
            whole[:, quarter(whole, token, m)] = got[...]
    elif kind == "x":
        start = 0
        for got in gots:
            rows = slice(start, start + got.shape[0])
            whole[rows, :] = add(keep[rows, :], got[...]).astype(BF16)
            start += got.shape[0]
    else:
        total = keep[...].astype(F32)
        for got in gots:
            total = total + got[...].astype(F32)
        whole[...] = total.astype(BF16)
    if after_kind == "half":
        outs[0][...] = whole[:, half_at(bit(after_mask), whole.shape[1])]
        outs[1][...] = whole[:, half_at(1 - bit(after_mask), whole.shape[1])]
    elif after_kind == "quarter":
        for m, out in enumerate(outs):
            out[...] = whole[:, quarter(whole, token, m)]
    else:
        start = 0
        for out in outs:
            out[...] = whole[start : start + out.shape[0], :]
            start += out.shape[0]


class Chain:
    def __init__(self, clock, dp, steps, send, pieces=()):
        self.clock, self.dp = clock, dp
        self.pieces = pieces or (send[0].shape[1],)
        masks = [1 << k for k in range(dp.bit_length() - 1)]
        used = [1, 2] if "quarter" in steps else [m for m in masks if f"half{m}" in steps]
        self.todo = []
        for name in steps:
            if name == "all":
                self.todo += [("all", m) for m in masks if m not in used]
            else:
                kind = name.rstrip("0123456789")
                self.todo.append((kind, int(name[len(kind) :] or 0)))
        self.send = send
        self.busy = True
        self.launch()

    def launch(self):
        self.kind, self.mask = self.todo.pop(0)
        self.split = 0
        if self.kind == "core":
            self.got = [over_core(v) for v in self.send]
        elif self.kind == "x":
            self.got = [over_x(self.send.pop(0))]
            self.split = len(self.send)
        elif self.kind == "quarter":
            self.got = [exchange(v, "dp", self.dp, m) for m, v in enumerate(self.send, 1)]
        elif self.kind == "besides":
            self.got = [exchange(self.keep, "dp", self.dp, m) for m in (1, 2, 3)]
        else:
            self.got = [exchange(self.send[0], "dp", self.dp, self.mask)]

    def more(self):
        self.got.append(over_x(gate(self.clock, [self.got[-1]], [self.send.pop(0)])[0]))
        self.split -= 1

    def step(self):
        rows, width = self.keep.shape[-2:]
        rows = 2 * rows if self.kind == "core" else rows
        width = width * {"beside": 2, "besides": 4}.get(self.kind, 1)
        kind, mask = self.todo[0] if self.todo else ("", 0)
        if kind == "half":
            dims = [(rows, width // 2)] * 2
        elif kind == "quarter":
            dims = [(rows, width // 4)] * 4
        elif kind == "x":
            dims = [(n, width) for n in (rows // 2, *self.pieces)]
        else:
            dims = [(rows, width)]
        kernel = functools.partial(join_kernel, self.kind, self.mask, (kind, mask, len(dims) - 1))
        self.keep, *self.send = call(self.clock, kernel, "join", [shape(d) for d in dims], [self.keep, *self.got], [pltpu.VMEM((rows, width), BF16)], limit=JOIN)
        self.send = self.send or [self.keep]
        self.busy = bool(self.todo)
        if self.busy:
            self.launch()


def column(row):
    r = lax.broadcasted_iota(jnp.int32, (128, 128), 0)
    c = lax.broadcasted_iota(jnp.int32, (128, 128), 1)
    return jnp.sum(jnp.where(r == c, row, 0.0), axis=1, keepdims=True)


def as_row(col):
    r = lax.broadcasted_iota(jnp.int32, (128, 128), 0)
    c = lax.broadcasted_iota(jnp.int32, (128, 128), 1)
    return jnp.sum(jnp.where(r == c, col, 0.0), axis=0, keepdims=True)


def send_out(pairs, sems):
    copies = [pltpu.make_async_copy(src, dst, sems.at[k]) for k, (src, dst) in enumerate(pairs)]
    for copy in copies:
        copy.start()
    for copy in copies:
        copy.wait()


def finish_outer_kernel(_, u, out, buf, sems):
    buf[...] = u[...].astype(F32)
    send_out([(buf, out)], sems)


def finish_outer(clock, u):
    return call(clock, finish_outer_kernel, "finish_outer", [shape(u.shape, F32)], [u], [pltpu.VMEM(u.shape, F32), pltpu.SemaphoreType.DMA((1,))], limit=JOIN, outside=(0,))[0]


def finish_kernel(token, total, inner, w_inner, pack, *refs):
    outs, (buf, buf_inner, small, sems) = refs[:-4], refs[-4:]
    gain, shift, gain_two, shift_two = (column(pack[128:129, k : k + 128].astype(F32)) for k in (0, 128, 256, 384))
    copies = []

    def leave(source, k):
        copies.append(pltpu.make_async_copy(source, outs[k], sems.at[k]))
        copies[-1].start()

    sums = total[128:144, 0:2048].astype(F32)
    n = inner[...].astype(F32)
    buf_inner[...] = gain_two * n + shift_two * sums[1:2, :]
    leave(buf_inner, 5)
    for k in range(5):
        cols = slice(512 * k, 512 * (k + 1))
        part = total[0:128, cols].astype(F32)
        buf[:, cols] = gain * part + shift * sums[0:1, cols] if k < 4 else part
        leave(buf.at[:, cols], k)
    w = pack[0:128, :].astype(F32)
    v = w_inner[...].astype(F32)
    for k, product in enumerate((w * total[0:128, 0:2048].astype(F32), w * sums[0:1, :], v * n, v * sums[1:2, :])):
        small[k : k + 1, 0:128] = as_row(jnp.sum(product, axis=1, keepdims=True))
        leave(small.at[k, 0:128], 6 + k)
    me = position(token, 0)
    small[4:5, :] = total[128:144, pl.ds(pl.multiple_of(me * 512, 512), 512)].astype(F32)[1:2, :]
    leave(small.at[4], 10)
    small[5:6, 0:128] = total[128:144, pl.ds(pl.multiple_of(me * 128, 128), 128)].astype(F32)[2:3, :]
    leave(small.at[5, 0:128], 11)
    for copy in copies:
        copy.wait()


def finish_all(clock, total, inner, w_inner, pack):
    outs = [shape((128, 512), F32)] * 5 + [shape((128, 2048), F32)] + [shape((128,), F32)] * 4 + [shape((512,), F32), shape((128,), F32)]
    scratch = [pltpu.VMEM((128, 2560), F32), pltpu.VMEM((128, 2048), F32), pltpu.VMEM((8, 512), F32), pltpu.SemaphoreType.DMA((12,))]
    return call(clock, finish_kernel, "finish_all", outs, [total, inner, w_inner, pack], scratch, limit=12, outside=range(12))


PLAN = (
    "OG", "IA", "WU", "IB", "u", "IS", "IK", "i", "RB", "AE", "u", "i", "AL", "u", "i", "PS", "PK", "p",
    "IN", "u", "i", "FO", "u", "p", "i", "p", "u", "i", "p", "u",
)
STEPS = {
    "u": ("core", "x", "half1", "half2", "all", "beside2", "beside1"),
    "i": ("core", "quarter", "x", "all", "beside2", "beside1"),
    "p": ("core", "x", "quarter", "all", "besides"),
}
PIECES = {"u": (512,), "i": (), "p": ()}


def per_device(dp, tokens, first_gain, first_shift, w_query, w_key, w_value, w_control, w_output, second_gain, second_shift, w_inner, inner_bias, w_outer, outer_bias, cotangent):
    clock = Clock(lax.axis_index("fsdp").astype(jnp.int32), lax.axis_index("dp").astype(jnp.int32))
    vectors = (first_gain, first_shift, second_gain, second_shift, outer_bias, inner_bias)
    own, first, second, wi0, wi1 = begin(clock, (w_query, w_key, w_value, w_control), vectors, w_inner)
    mine = [over_x(first), over_x(second)]
    own_core, wi_c = over_core(own), over_core(w_inner)
    n1, n1_low = first_norm(clock, tokens)
    *mine, wi0, wi1, w_output = clock.sync(*mine, wi0, wi1, w_output)
    wi_x0 = over_x(wi0)
    across = assemble(clock, mine, [exchange(v, "dp", dp, k + 1) for k, v in enumerate(mine)], wi_x0)
    packs = [own, across, own_core, over_core(across)]
    wi1, w_output = clock.sync(wi1, w_output)
    wi_x1, wo_x, wo_c = over_x(wi1), over_x(w_output), over_core(w_output)
    qkvf = project(clock, n1, packs)
    w_outer = clock.sync(w_outer)
    wu_x, wu_c = over_x(w_outer), over_core(w_outer)
    mixed, *saved = attention_forward(clock, qkvf)
    wo_x, wi_x1 = clock.sync(wo_x, wi_x1)
    wo = [w_output, wo_x, wo_c, over_core(wo_x)]
    wi = [w_inner, wi_x0, wi_x1, wi_c, over_core(wi_x0), over_core(wi_x1)]
    resid, n2, r2, a2 = middle(clock, tokens, mixed, wo, packs)
    act, slope = ffn_inner(clock, a2, wi, packs)
    chains, made = {}, {}

    def start(name, send, keep):
        chains[name] = Chain(clock, dp, STEPS[name], send, PIECES[name])
        made[name] = keep

    def outer():
        keep, send = outer_grad(clock, act, cotangent)
        start("u", [send], lambda: keep)

    def wait_outer():
        wu_x = clock.sync(made["wu"])
        made["wu"] = [w_outer, wu_x, wu_c, over_core(wu_x)]

    def back_near():
        made["din"] = inner_back(clock, cotangent, slope, [w_outer, wu_c], (0, 2))

    def back_far():
        d, partial = made["din"]
        made["din"] = inner_back(clock, cotangent, d, [made["wu"][1], made["wu"][3]], (1, 3), [partial])

    def inner_send():
        start("i", [inner_grad(clock, n2, made["din"][0], 2)], None)

    def inner_keep():
        made["i"] = inner_grad(clock, n2, made["din"][0], 0)

    def resid_grad():
        made["dres"], made["do"] = resid_back(clock, cotangent, n2, r2, made["din"][0], wo, wi, packs)

    def early():
        made["early"] = attention_backward(clock, qkvf, saved, made["do"], 7, 4)

    def late():
        made["late"] = attention_backward(clock, qkvf, saved, made["do"], 3, 4, made["early"][1:])

    def project_part(first):
        return project_grad(clock, n1_low, made["late"][0], made["early"][0], mixed, made["dres"], made["din"][1], first)

    def project_send():
        start("p", [project_part(2)], None)

    def project_keep():
        made["p"] = project_part(0)

    def input_part():
        made["tokens"] = input_grad(clock, tokens, made["late"][0], made["early"][0], made["dres"], packs)

    def output_part():
        made["output"] = ffn_outer(clock, resid, act, made["wu"], packs)

    def finish(name):
        if name == "u":
            made["outer"] = finish_outer(clock, chains[name].keep)
        elif not (chains["i"].busy or chains["p"].busy):
            made["rest"] = finish_all(clock, chains["p"].keep, chains["i"].keep, w_inner, packs[0])

    def advance(name):
        c = chains[name]
        if not c.busy:
            return
        if c.kind == "core":
            keep = made[name]
            c.keep = keep() if callable(keep) else keep
        if c.split:
            c.more()
        else:
            c.step()
            if not c.busy:
                finish(name)

    made["wu"] = wu_x
    kernels = dict(OG=outer, WU=wait_outer, IA=back_near, IB=back_far, IS=inner_send, IK=inner_keep, RB=resid_grad, AE=early, AL=late, PS=project_send, PK=project_keep, IN=input_part, FO=output_part)
    for word in PLAN:
        if word in kernels:
            kernels[word]()
        else:
            advance(word)
    while any(c.busy for c in chains.values()):
        for name in "uip":
            advance(name)
    (
        grad_query, grad_key, grad_value, grad_control, grad_output, grad_inner, first_gain_grad, first_shift_grad,
        second_gain_grad, second_shift_grad, inner_bias_grad, outer_bias_grad,
    ) = made["rest"]
    return (
        made["output"], made["tokens"], first_gain_grad, first_shift_grad, grad_query, grad_key, grad_value, grad_control, grad_output,
        second_gain_grad, second_shift_grad, grad_inner, inner_bias_grad, made["outer"], outer_bias_grad,
    )


def solution(mesh):
    row, vec, mat = P(("dp", "fsdp"), None), P("fsdp"), P("fsdp", None)
    return jax.shard_map(
        functools.partial(per_device, mesh.shape["dp"]),
        mesh=mesh,
        in_specs=(row, vec, vec, mat, mat, mat, mat, mat, vec, vec, mat, vec, mat, vec, row),
        out_specs=(row, row, vec, vec, mat, mat, mat, mat, mat, vec, vec, mat, vec, mat, vec),
        check_vma=False,
    )
```

```python
import functools

import jax
import jax.numpy as jnp
from jax import lax
from jax.experimental import pallas as pl
from jax.experimental.pallas import tpu as pltpu
from jax.sharding import PartitionSpec as P

F32 = jnp.float32
BF16 = jnp.bfloat16
PAIR = 128
PAIRS = range(4)
SCALE = 64 ** -0.5
CHUNK = 128
UNROLL = 2
JOIN = 4
ROWS = 512
WHOLE = 1024
EPS = 1e-5
WEIGHT = 1000
MASKS = (0, 2, 1, 3)
VM = pl.BlockSpec(memory_space=pltpu.VMEM)
SM = pl.BlockSpec(memory_space=pltpu.SMEM)
ANY = pl.BlockSpec(memory_space=pl.ANY)


def mm(a, b):
    return lax.dot_general(a, b, (((1,), (0,)), ((), ())), preferred_element_type=F32)


def mm_nt(a, b):
    return lax.dot_general(a, b, (((1,), (1,)), ((), ())), preferred_element_type=F32)


def mm_tn(a, b):
    return lax.dot_general(a, b, (((0,), (0,)), ((), ())), preferred_element_type=F32)


def shape(dims, dtype=BF16):
    return jax.ShapeDtypeStruct(dims, dtype)


class Clock:
    def __init__(self, me, place):
        row = lax.broadcasted_iota(jnp.int32, (8, 128), 0)
        self.token = jnp.where(row == 0, me, place)

    def sync(self, *values):
        self.token, values = lax.optimization_barrier((self.token, values))
        return values if len(values) > 1 else values[0]


def call(clock, kernel, name, outs, args, scratch=(), limit=8, outside=(), raw=(), aliases=None):
    n_in, n_out = len(args), len(outs)

    def body(token, *refs):
        outs_at = n_in + n_out
        refs[outs_at][...] = token[...]
        kernel(token, *refs[:outs_at], *refs[outs_at + 1 :])

    place = lambda k, o: (pltpu.HBM if k in outside else pltpu.VMEM)(o.shape, o.dtype)
    args = [pltpu.with_memory_space_constraint(a, pltpu.HBM if k in raw else pltpu.VMEM) for k, a in enumerate(args)]
    *results, clock.token = pl.pallas_call(
        body,
        in_specs=[VM] + [ANY if k in raw else VM for k in range(n_in)],
        out_specs=[ANY if k in outside else VM for k in range(n_out)] + [VM],
        out_shape=[place(k, o) for k, o in enumerate(outs)] + [pltpu.VMEM((8, 128), jnp.int32)],
        scratch_shapes=list(scratch),
        input_output_aliases={i + 1: o for i, o in (aliases or {}).items()},
        compiler_params=pltpu.CompilerParams(vmem_limit_bytes=limit << 20),
        cost_estimate=pl.CostEstimate(flops=WEIGHT, bytes_accessed=1 << 10, transcendentals=0),
        name=name,
    )(pltpu.with_memory_space_constraint(clock.token, pltpu.VMEM), *args)
    return results


def position(token, row):
    return jnp.max(token[row : row + 1, :])


def blocks_of(token):
    me = position(token, 0)
    return [me ^ mask for mask in MASKS]


def wide(blocks, width):
    return [pl.ds(pl.multiple_of(b * width, width), width) for b in blocks]


def take_blocks(ref, rows, blocks, width):
    return jnp.concatenate([ref[rows, cols] for cols in wide(blocks, width)], axis=1)


def put_blocks(ref, rows, values, blocks, width):
    for i, cols in enumerate(wide(blocks, width)):
        ref[rows, cols] = values[:, i * width : (i + 1) * width]


def stack(refs, cols=slice(None)):
    return jnp.concatenate([r[:, cols] for r in refs], axis=0)


def stack_packs(packs, cols):
    return jnp.concatenate([r[0:128, cols] for r in packs], axis=0)


def vector(packs, start, width):
    return jnp.concatenate([r[128:129, start : start + width] for r in packs], axis=1).astype(F32)


def row_loop(T, body, rows=ROWS):
    def step(c, _):
        body(pl.ds(pl.multiple_of(c * rows, rows), rows))
        return 0

    if rows < T:
        lax.fori_loop(0, T // rows, step, 0)
    else:
        body(slice(None))


def stats(x):
    mean = jnp.mean(x, axis=1, keepdims=True)
    centred = x - mean
    inv = lax.rsqrt(jnp.mean(centred * centred, axis=1, keepdims=True) + EPS)
    return centred * inv, inv


def norm_back(grad, normed, inv):
    return inv * (grad - jnp.mean(grad, axis=1, keepdims=True) - normed * jnp.mean(grad * normed, axis=1, keepdims=True))


def parity(token):
    place = position(token, 1)
    return lax.rem(place + lax.div(place, 2), 2)


def begin_kernel(token, *refs):
    weights, vecs, inner, (out, first, second, wi0, wi1), rest = refs[:4], refs[4:10], refs[10], refs[11:16], refs[16:]
    bufs, sems = rest[:6], rest[6]
    cols = [slice(512 * n, 512 * (n + 1)) for n in range(4)]
    copies = [pltpu.make_async_copy(w, out.at[0:128, c], sems.at[n]) for n, (w, c) in enumerate(zip(weights, cols))]
    copies += [pltpu.make_async_copy(v, b, sems.at[4 + n]) for n, (v, b) in enumerate(zip(vecs, bufs))]
    copies += [pltpu.make_async_copy(inner.at[64 * n : 64 * (n + 1), :], w, sems.at[10 + n]) for n, w in enumerate((wi0, wi1))]
    for copy in copies:
        copy.start()
    for copy in copies:
        copy.wait()
    vec = jnp.concatenate([b[...].reshape(1, -1).astype(F32) for b in bufs] + [jnp.zeros((1, 896), F32)], axis=1)
    out[128:144, :] = jnp.broadcast_to(vec, (16, 2048)).astype(BF16)
    odd = parity(token)
    for k, piece in enumerate((first, second)):
        piece[...] = out[:, pl.ds(pl.multiple_of(odd * 1024 + 512 * k, 512), 512)]


def begin(clock, weights, vecs, inner):
    scratch = [pltpu.VMEM(v.shape, BF16) for v in vecs] + [pltpu.SemaphoreType.DMA((12,))]
    outs = [shape((144, 2048)), shape((144, 512)), shape((144, 512)), shape((64, 2048)), shape((64, 2048))]
    return call(clock, begin_kernel, "begin", outs, [*weights, *vecs, inner], scratch, limit=JOIN, raw=range(11))


def assemble_kernel(token, mine0, mine1, other0, other1, _, out):
    odd = parity(token)
    for half, pieces in ((odd, (mine0, mine1)), (1 - odd, (other0, other1))):
        for k, piece in enumerate(pieces):
            out[:, pl.ds(pl.multiple_of(half * 1024 + 512 * k, 512), 512)] = piece[...]


def assemble(clock, mine, other, waited):
    return call(clock, assemble_kernel, "assemble", [shape((144, 2048))], [*mine, *other, waited], limit=JOIN)[0]


def first_norm_kernel(token, tokens, n1, n1_low, scr):
    blocks = blocks_of(token)

    def body(rows):
        n, _ = stats(tokens[rows, :].astype(F32))
        scr[...] = n
        n = take_blocks(scr, slice(None), blocks, 128)
        n1[rows, :] = n
        n1_low[rows, :] = n.astype(BF16)

    row_loop(tokens.shape[0], body)


def first_norm(clock, tokens):
    T = tokens.shape[0]
    return call(clock, first_norm_kernel, "first_norm", [shape((T, 512), F32), shape((T, 512))], [tokens], [pltpu.VMEM((ROWS, 512), F32)])


def project_kernel(_, n1, p0, p1, p2, p3, qkvf):
    packs = (p0, p1, p2, p3)
    gain, shift = vector(packs, 0, 128), vector(packs, 128, 128)

    def body(rows):
        a1 = (n1[rows, :] * gain + shift).astype(BF16)
        for n in range(4):
            cols = slice(512 * n, 512 * (n + 1))
            out = mm(a1, stack_packs(packs, cols))
            qkvf[rows, cols] = (jnp.exp(out) if n == 3 else out).astype(BF16)

    row_loop(n1.shape[0], body, WHOLE)


def project(clock, n1, packs):
    T = n1.shape[0]
    return call(clock, project_kernel, "project", [shape((T, 2048))], [n1, *packs])[0]


def left_half(rows):
    return lax.broadcasted_iota(jnp.int32, (rows, PAIR), 1) < 64


def split_pair(x, left):
    zero = jnp.zeros((), x.dtype)
    return jnp.concatenate((jnp.where(left, x, zero), jnp.where(left, zero, x)), axis=0)


def same_head():
    r = lax.broadcasted_iota(jnp.int32, (PAIR, PAIR), 0) < 64
    c = lax.broadcasted_iota(jnp.int32, (PAIR, PAIR), 1) < 64
    return r == c


def causal_pair(rows):
    r = lax.broadcasted_iota(jnp.int32, (rows, 2 * rows), 0)
    c = lax.broadcasted_iota(jnp.int32, (rows, 2 * rows), 1)
    return r >= jnp.where(c >= rows, c - rows, c)


def triangle(rows):
    return lax.broadcasted_iota(jnp.int32, (rows, rows), 0) >= lax.broadcasted_iota(jnp.int32, (rows, rows), 1)


def half_reduce(x, left, fn, fill):
    a = fn(jnp.where(left, x, fill), axis=1, keepdims=True)
    b = fn(jnp.where(left, fill, x), axis=1, keepdims=True)
    return jnp.where(left, a, b)


def pair_of(j):
    return slice(PAIR * j, PAIR * (j + 1))


def a_of(j):
    return slice(256 * j, 256 * (j + 1))


def b_of(j):
    return slice(1024 + 256 * j, 1024 + 256 * (j + 1))


def s_of(j):
    return slice(2048 + PAIR * j, 2048 + PAIR * (j + 1))


def g_of(j):
    return slice(2560 + PAIR * j, 2560 + PAIR * (j + 1))


KEPT = 3072


def chunk_rows(c):
    return pl.ds(pl.multiple_of(c * CHUNK, CHUNK), CHUNK)


def forward_kernel(_, qkvf, mixed, kept, states, carry_out, s1, s2, carry):
    C = CHUNK
    s1[...] = jnp.zeros_like(s1)
    s2[...] = jnp.zeros_like(s2)
    carry[...] = jnp.zeros_like(carry)
    left = left_half(C)
    causal = causal_pair(C)
    same = same_head()
    lower = triangle(C).astype(BF16)
    zero = jnp.zeros((), BF16)

    def step(c, _):
        rows = chunk_rows(c)
        part = lambda n, j: qkvf[rows, 512 * n + PAIR * j : 512 * n + PAIR * (j + 1)]
        raw = [mm_nt(part(0, j), split_pair(part(1, j), left)) for j in PAIRS]
        carry_out[c] = carry[...]
        denom = mm(lower, qkvf[rows, 1536:2048]) + carry[0:1, :]
        carry[0:1, :] = denom[C - 1 :, :]
        rden_all = 1.0 / denom
        f2 = [split_pair(part(3, j), left) for j in PAIRS]
        numer = []
        for j in PAIRS:
            a2 = jnp.where(causal, raw[j].astype(BF16), zero)
            kept[rows, a_of(j)] = a2
            s1b = s1[j].astype(BF16)
            states[c, :, pair_of(j)] = s1b
            numer.append(mm(a2, f2[j]) + mm(part(0, j), s1b))
        g = []
        for j in PAIRS:
            rden = rden_all[:, pair_of(j)]
            s = numer[j] * rden * SCALE
            kept[rows, s_of(j)] = s.astype(BF16)
            e = jnp.exp(s - half_reduce(s, left, jnp.max, -jnp.inf))
            p = e / half_reduce(e, left, jnp.sum, 0.0)
            g.append((p * rden).astype(BF16))
            kept[rows, g_of(j)] = g[j]
        raw = [mm_nt(g[j], f2[j]) for j in PAIRS]
        for j in PAIRS:
            b2 = jnp.where(causal, raw[j].astype(BF16), zero)
            kept[rows, b_of(j)] = b2
            s2b = s2[j].astype(BF16)
            states[c, :, pair_of(4 + j)] = s2b
            o = mm(b2, split_pair(part(2, j), left)) + mm(g[j], s2b)
            mixed[rows, pair_of(j)] = o.astype(BF16)
        for j in PAIRS:
            s1[j] += jnp.where(same, mm_tn(part(1, j), part(3, j)), 0.0)
            s2[j] += jnp.where(same, mm_tn(part(3, j), part(2, j)), 0.0)
        return 0

    lax.fori_loop(0, qkvf.shape[0] // C, step, 0, unroll=UNROLL)


def state_scratch():
    return [pltpu.VMEM((4, PAIR, PAIR), F32), pltpu.VMEM((4, PAIR, PAIR), F32), pltpu.VMEM((8, 512), F32)]


def attention_forward(clock, qkvf):
    T = qkvf.shape[0]
    n = T // CHUNK
    outs = [shape((T, 512)), shape((T, KEPT)), shape((n, PAIR, 1024)), shape((n, 8, 512), F32)]
    return call(clock, forward_kernel, "attention_forward", outs, [qkvf], state_scratch())


def backward_kernel(first, count, last, _, qkvf, kept, states, carry_in, do_in, *refs):
    C = CHUNK
    r, carry = refs[-2:]
    begins, (grad, *ends) = (refs[:2], refs[2:-2]) if first < last else ((), refs[:-2])
    for ref, old in zip((r, carry), begins or (None,) * 2):
        ref[...] = jnp.zeros_like(ref) if old is None else old[...]
    left = left_half(C)
    causal = causal_pair(C)
    same = same_head()
    same2 = jnp.concatenate((same, same), axis=1)
    lower = triangle(C).astype(BF16)
    upper = lower.T
    upper2 = jnp.concatenate((upper, upper), axis=1)
    zero = jnp.zeros((), BF16)

    def step(t, _):
        c = first - t
        rows = chunk_rows(c)
        here = chunk_rows(count - 1 - t)
        part = lambda n, j: qkvf[rows, 512 * n + PAIR * j : 512 * n + PAIR * (j + 1)]
        do = [do_in[rows, pair_of(j)] for j in PAIRS]
        denoms = mm(lower, qkvf[rows, 1536:2048]) + carry_in[c][0:1, :]
        s1b = [states[c, :, pair_of(j)] for j in PAIRS]
        s2b = [states[c, :, pair_of(4 + j)] for j in PAIRS]
        rb = [r[j].astype(BF16) for j in PAIRS]
        g = [kept[rows, g_of(j)] for j in PAIRS]
        raw = [mm_nt(do[j], split_pair(part(2, j), left)) for j in PAIRS]
        f2 = [split_pair(part(3, j), left) for j in PAIRS]
        db2, dg, dn, dd, later = [], [], [], [], []
        for j in PAIRS:
            db2.append(jnp.where(causal, raw[j].astype(BF16), zero))
            dg.append(mm(db2[j], f2[j]) + mm_nt(do[j], s2b[j]))
        for j in PAIRS:
            later.append(mm(part(3, j), rb[j]))
            dv2 = mm_tn(kept[rows, b_of(j)], do[j])
            dv = jnp.where(left, dv2[:C], dv2[C:]) + later[j][:, :PAIR]
            grad[here, 1024 + PAIR * j : 1024 + PAIR * (j + 1)] = dv.astype(BF16)
        for j in PAIRS:
            denom = denoms[:, pair_of(j)]
            rden = 1.0 / denom
            p = g[j].astype(F32) * denom
            dpp = dg[j] * rden * p
            ds = dpp - p * half_reduce(dpp, left, jnp.sum, 0.0)
            dd.append(-(dpp + ds * kept[rows, s_of(j)].astype(F32)) * rden)
            dn.append((ds * SCALE * rden).astype(BF16))
        raw = [mm_nt(dn[j], f2[j]) for j in PAIRS]
        sums = []
        for k in (0, 2):
            d = jnp.concatenate((dd[k], dd[k + 1]), axis=1)
            hi = d.astype(BF16)
            lo = (d - hi.astype(F32)).astype(BF16)
            total = mm(upper2, jnp.concatenate((hi, lo), axis=0))
            sums += [total[:, :PAIR], total[:, PAIR:]]
        for j in PAIRS:
            df2 = mm_tn(jnp.concatenate((db2[j], kept[rows, a_of(j)]), axis=0), jnp.concatenate((g[j], dn[j]), axis=0))
            df = jnp.where(left, df2[:C], df2[C:]) + mm_nt(jnp.concatenate((part(2, j), part(1, j)), axis=1), rb[j])
            df = df + sums[j] + carry[0:1, pair_of(j)]
            grad[here, 1536 + PAIR * j : 1536 + PAIR * (j + 1)] = (df * part(3, j).astype(F32)).astype(BF16)
            carry[0:1, pair_of(j)] += jnp.sum(dd[j], axis=0, keepdims=True)
        for j in PAIRS:
            da2 = jnp.where(causal, raw[j].astype(BF16), zero)
            dq = mm(da2, split_pair(part(1, j), left)) + mm_nt(dn[j], s1b[j])
            grad[here, pair_of(j)] = dq.astype(BF16)
            dk2 = mm_tn(da2, part(0, j))
            dk = jnp.where(left, dk2[:C], dk2[C:]) + later[j][:, PAIR:]
            grad[here, 512 + PAIR * j : 512 + PAIR * (j + 1)] = dk.astype(BF16)
        for j in PAIRS:
            new = jnp.concatenate((mm_tn(g[j], do[j]), mm_tn(dn[j], part(0, j))), axis=1)
            r[j] += jnp.where(same2, new, 0.0)
        return 0

    lax.fori_loop(0, count, step, 0, unroll=UNROLL)
    for ref, end in zip((r, carry), ends):
        end[...] = ref[...]


def attention_backward(clock, qkvf, saved, d_o, first, count, states=()):
    rows = count * CHUNK
    outs = [shape((rows, 2048))]
    if first - count >= 0:
        outs += [shape((4, PAIR, 2 * PAIR), F32), shape((8, 512), F32)]
    kernel = functools.partial(backward_kernel, first, count, qkvf.shape[0] // CHUNK - 1)
    scratch = [pltpu.VMEM((4, PAIR, 2 * PAIR), F32), pltpu.VMEM((8, 512), F32)]
    return call(clock, kernel, "attention_backward", outs, [qkvf, *saved, d_o, *states], scratch)


def gelu_parts(v):
    c = 0.7978845608028654
    k = c * 0.044715
    v2 = v * v
    half = 0.5 * jnp.tanh(v * (c + k * v2)) + 0.5
    act = v * half
    return act, half + act * (1.0 - half) * (2 * c + (6 * k) * v2)


def middle_kernel(token, tokens, mixed, *refs):
    wo, packs, (resid_out, n2_out, r2_out, a2_out, scr) = refs[:4], refs[4:8], refs[8:]
    blocks = blocks_of(token)
    gain, shift = vector(packs, 256, 128), vector(packs, 384, 128)

    def body(rows):
        resid = tokens[rows, :].astype(F32) + mm(take_blocks(mixed, rows, blocks, 128), stack(wo))
        resid_out[rows, :] = resid
        n2, r2 = stats(resid)
        scr[...] = n2
        n2 = take_blocks(scr, slice(None), blocks, 128)
        n2_out[rows, :] = n2.astype(BF16)
        r2_out[rows, :] = jnp.broadcast_to(r2, (ROWS, 128))
        a2_out[rows, :] = (n2 * gain + shift).astype(BF16)

    row_loop(tokens.shape[0], body)


def middle(clock, tokens, mixed, wo, packs):
    T = tokens.shape[0]
    outs = [shape((T, 512), F32), shape((T, 512)), shape((T, 128), F32), shape((T, 512))]
    return call(clock, middle_kernel, "middle", outs, [tokens, mixed, *wo, *packs], [pltpu.VMEM((ROWS, 512), F32)])


def ffn_inner_kernel(token, a2_ref, *refs):
    wi, packs, (act_out, slope_out) = refs[:-6], refs[-6:-2], refs[-2:]
    cols = wide(blocks_of(token), 512)

    def body(rows):
        a2 = a2_ref[rows, :]
        inner = mm(a2, stack(wi, cols[0]))
        for i in range(4):
            after = mm(a2, stack(wi, cols[i + 1])) if i < 3 else None
            act, slope = gelu_parts(inner + packs[i][128:129, 640:1152].astype(F32))
            act_out[rows, 512 * i : 512 * (i + 1)] = act.astype(BF16)
            slope_out[rows, cols[i]] = slope.astype(BF16)
            inner = after

    row_loop(a2_ref.shape[0], body)


def ffn_inner(clock, a2, wi, packs):
    T = a2.shape[0]
    return call(clock, ffn_inner_kernel, "ffn_inner", [shape((T, 2048)), shape((T, 2048))], [a2, *wi, *packs])


def outer_grad_kernel(_, act, dy, keep, send):
    for i in range(4):
        out = mm_tn(act[:, 512 * i : 512 * (i + 1)], dy[...]).astype(BF16)
        (keep if i < 2 else send)[i % 2] = out


def outer_grad(clock, act, dy):
    return call(clock, outer_grad_kernel, "outer_grad", [shape((2, 512, 512))] * 2, [act, dy])


def ffn_outer_kernel(token, resid, act, *refs):
    wu, vs, (out, bias, result, sem) = refs[:4], refs[4:8], refs[8:]
    put_blocks(bias, slice(None), jnp.broadcast_to(vector(vs, 512, 128), (8, 512)), blocks_of(token), 128)

    def body(rows):
        result[rows, :] = (mm(act[rows, :], stack(wu)) + resid[rows, :] + bias[0:1, :]).astype(BF16)

    row_loop(act.shape[0], body)
    copy = pltpu.make_async_copy(result, out, sem)
    copy.start()
    copy.wait()


def ffn_outer(clock, resid, act, wu, vecs):
    scratch = [pltpu.VMEM((8, 512), F32), pltpu.VMEM(resid.shape, BF16), pltpu.SemaphoreType.DMA]
    return call(clock, ffn_outer_kernel, "ffn_outer", [shape(resid.shape)], [resid, act, *wu, *vecs], scratch, outside=(0,))[0]


def inner_back_kernel(which, more, token, dy, slope, *refs):
    cols = wide(blocks_of(token), 512)
    wu, (din, sums) = refs[: len(which)], refs[-2:]
    if more:
        sums[...] = refs[len(which)][...]
    else:
        sums[...] = jnp.zeros_like(sums)
        sums[1:2, 0:512] = jnp.sum(dy[...].astype(F32), axis=0, keepdims=True)
    for i, u in zip(which, wu):
        d = (mm_nt(dy[...], u[...]) * slope[:, cols[i]].astype(F32)).astype(BF16)
        din[:, cols[i]] = d
        sums[0:1, cols[i]] = jnp.sum(d.astype(F32), axis=0, keepdims=True)


def inner_back(clock, dy, slope, wu, which, sums=()):
    T = dy.shape[0]
    kernel = functools.partial(inner_back_kernel, which, len(sums) > 0)
    return call(clock, kernel, "inner_back", [shape((T, 2048)), shape((8, 2048), F32)], [dy, slope, *wu, *sums], aliases={1: 0})


def inner_grad_kernel(first, _, n2, din, out):
    m = mm_tn(n2[:, 128 * first : 128 * (first + 2)], din[...]).astype(BF16)
    for k in range(2):
        out[k] = m[128 * k : 128 * (k + 1), :]


def inner_grad(clock, n2, din, first):
    return call(clock, functools.partial(inner_grad_kernel, first), "inner_grad", [shape((2, 128, 2048))], [n2, din])[0]


def resid_back_kernel(token, dy, n2, r2, din, *refs):
    wo, wi, packs = refs[:4], refs[4:-7], refs[-7:-3]
    dres_out, do_out, scr = refs[-3:]
    blocks = blocks_of(token)
    gain = vector(packs, 256, 128)

    def body(rows):
        da2 = mm_nt(din[rows, :], stack(wi))
        put_blocks(scr, slice(None), norm_back(da2 * gain, n2[rows, :].astype(F32), r2[rows, 0:1]), blocks, 128)
        dres = dy[rows, :].astype(F32) + scr[...]
        dres_out[rows, :] = dres
        d_o = mm_nt(dres.astype(BF16), stack(wo))
        put_blocks(do_out, rows, d_o.astype(BF16), blocks, 128)

    row_loop(dy.shape[0], body)


def resid_back(clock, dy, n2, r2, din, wo, wi, packs):
    T = dy.shape[0]
    outs = [shape((T, 512), F32), shape((T, 512))]
    return call(clock, resid_back_kernel, "resid_back", outs, [dy, n2, r2, din, *wo, *wi, *packs], [pltpu.VMEM((ROWS, 512), F32)])


def project_grad_kernel(first, starts, token, n1, early, late, mixed, dres, sums, out):
    half = early.shape[0]
    blocks = wide(blocks_of(token), 128)
    n = n1[:, 128 * first : 128 * (first + 2)]
    for at, start in enumerate(starts):
        cols, dest = slice(start, start + 1024), slice(1024 * at, 1024 * (at + 1))
        m = (mm_tn(n[0:half], early[:, cols]) + mm_tn(n[half:], late[:, cols])).astype(BF16)
        total = sum(jnp.sum(r[:, cols].astype(F32), axis=0, keepdims=True) for r in (early, late))
        row = lax.broadcasted_iota(jnp.int32, (16, 1024), 0)
        tail = jnp.where(row == 0, total, jnp.where(row == 1, sums[0:1, cols], sums[1:2, cols])).astype(BF16)
        for k in range(2):
            out[k, 0:128, dest] = m[128 * k : 128 * (k + 1)]
            out[k, 128:144, dest] = tail
    rest = 1024 * len(starts)
    if rest < out.shape[2]:
        d = dres[...].astype(BF16)
        for k in range(2):
            out[k, 0:128, rest:] = mm_tn(mixed[:, blocks[first + k]], d).astype(BF16)
            out[k, 128:144, rest:] = jnp.zeros((16, 512), BF16)


def project_grad(clock, n1, early, late, mixed, dres, sums, first, starts=(0, 1024)):
    width = 1024 * len(starts) + (512 if 1024 in starts else 0)
    kernel = functools.partial(project_grad_kernel, first, starts)
    return call(clock, kernel, "project_grad", [shape((2, 144, width))], [n1, early, late, mixed, dres, sums])[0]


def input_grad_kernel(token, tokens, early, late, dres, p0, p1, p2, p3, out, scr, result, sems):
    packs = (p0, p1, p2, p3)
    blocks = blocks_of(token)
    gain = vector(packs, 0, 128)
    w = stack_packs(packs, slice(0, 2048))
    copies = []
    for h, d in enumerate((early, late)):
        rows = slice(ROWS * h, ROWS * (h + 1))
        e = mm_nt(d[...], w) * gain
        n1, r1 = stats(tokens[rows, :].astype(F32))
        scr[...] = n1
        put_blocks(scr, slice(None), norm_back(e, take_blocks(scr, slice(None), blocks, 128), r1), blocks, 128)
        result[rows, :] = (dres[rows, :] + scr[...]).astype(BF16)
        copies.append(pltpu.make_async_copy(result.at[rows, :], out.at[rows, :], sems.at[h]))
        copies[-1].start()
    for copy in copies:
        copy.wait()


def input_grad(clock, tokens, early, late, dres, packs):
    scratch = [pltpu.VMEM((ROWS, 512), F32), pltpu.VMEM(dres.shape, BF16), pltpu.SemaphoreType.DMA((2,))]
    return call(clock, input_grad_kernel, "input_grad", [shape(dres.shape)], [tokens, early, late, dres, *packs], scratch, outside=(0,))[0]


def exchange(value, axis, size, mask):
    return lax.ppermute(value, axis, [(i, i ^ mask) for i in range(size)])


def over_x(value):
    return exchange(value, "fsdp", 4, 2)


def over_core(value):
    return exchange(value, "fsdp", 4, 1)


def add(a, b):
    return a.astype(F32) + b.astype(F32)


def half_at(bit, width):
    return pl.ds(pl.multiple_of(bit * (width // 2), width // 2), width // 2)


def gate_kernel(*refs):
    pass


def gate(clock, waited, values):
    n = len(waited)
    outs = [shape(v.shape, v.dtype) for v in values]
    return call(clock, gate_kernel, "gate", outs, [*waited, *values], limit=1, aliases={n + k: k for k in range(len(values))})


def quarter(ref, token, mask):
    width = ref.shape[1] // 4
    place = position(token, 1) ^ mask
    return pl.ds(pl.multiple_of((2 * lax.rem(place, 2) + lax.rem(lax.div(place, 2), 2)) * width, width), width)


def join_kernel(kind, mask, after, token, keep, *refs):
    after_kind, after_mask, n_sends = after
    n_outs = 1 + n_sends
    gots, outs, whole = refs[: -1 - n_outs], refs[-1 - n_outs : -1], refs[-1]
    bit = lambda m: lax.rem(lax.div(position(token, 1), m), 2)
    if kind == "core":
        rows, start = keep.shape[1], 0
        for got in gots:
            cols = slice(start, start + got.shape[2])
            for k in range(2):
                whole[rows * k : rows * (k + 1), cols] = add(keep[k, :, cols], got[k]).astype(BF16)
            start += got.shape[2]
    elif kind == "beside":
        whole[:, half_at(bit(mask), whole.shape[1])] = keep[...]
        whole[:, half_at(1 - bit(mask), whole.shape[1])] = gots[0][...]
    elif kind == "besides":
        for m, got in enumerate((keep, *gots)):
            whole[:, quarter(whole, token, m)] = got[...]
    elif kind == "x":
        start = 0
        for got in gots:
            rows = slice(start, start + got.shape[0])
            whole[rows, :] = add(keep[rows, :], got[...]).astype(BF16)
            start += got.shape[0]
    else:
        total = keep[...].astype(F32)
        for got in gots:
            total = total + got[...].astype(F32)
        whole[...] = total.astype(BF16)
    if after_kind == "half":
        outs[0][...] = whole[:, half_at(bit(after_mask), whole.shape[1])]
        outs[1][...] = whole[:, half_at(1 - bit(after_mask), whole.shape[1])]
    elif after_kind == "quarter":
        for m, out in enumerate(outs):
            out[...] = whole[:, quarter(whole, token, m)]
    else:
        start = 0
        for out in outs:
            out[...] = whole[start : start + out.shape[0], :]
            start += out.shape[0]


class Chain:
    def __init__(self, clock, dp, steps, send, pieces=()):
        self.clock, self.dp = clock, dp
        self.pieces = pieces or (send[0].shape[1],)
        masks = [1 << k for k in range(dp.bit_length() - 1)]
        used = [1, 2] if "quarter" in steps else [m for m in masks if f"half{m}" in steps]
        self.todo = []
        for name in steps:
            if name == "all":
                self.todo += [("all", m) for m in masks if m not in used]
            else:
                kind = name.rstrip("0123456789")
                self.todo.append((kind, int(name[len(kind) :] or 0)))
        self.send = send
        self.busy = True
        self.launch()

    def launch(self):
        self.kind, self.mask = self.todo.pop(0)
        self.split = 0
        if self.kind == "core":
            self.got = [over_core(v) for v in self.send]
        elif self.kind == "x":
            self.got = [over_x(self.send.pop(0))]
            self.split = len(self.send)
        elif self.kind == "quarter":
            self.got = [exchange(v, "dp", self.dp, m) for m, v in enumerate(self.send, 1)]
        elif self.kind == "besides":
            self.got = [exchange(self.keep, "dp", self.dp, m) for m in (1, 2, 3)]
        else:
            self.got = [exchange(self.send[0], "dp", self.dp, self.mask)]

    def more(self):
        self.got.append(over_x(gate(self.clock, [self.got[-1]], [self.send.pop(0)])[0]))
        self.split -= 1

    def step(self):
        rows, width = self.keep.shape[-2:]
        rows = 2 * rows if self.kind == "core" else rows
        width = width * {"beside": 2, "besides": 4}.get(self.kind, 1)
        kind, mask = self.todo[0] if self.todo else ("", 0)
        if kind == "half":
            dims = [(rows, width // 2)] * 2
        elif kind == "quarter":
            dims = [(rows, width // 4)] * 4
        elif kind == "x":
            dims = [(n, width) for n in (rows // 2, *self.pieces)]
        else:
            dims = [(rows, width)]
        kernel = functools.partial(join_kernel, self.kind, self.mask, (kind, mask, len(dims) - 1))
        self.keep, *self.send = call(self.clock, kernel, "join", [shape(d) for d in dims], [self.keep, *self.got], [pltpu.VMEM((rows, width), BF16)], limit=JOIN)
        self.send = self.send or [self.keep]
        self.busy = bool(self.todo)
        if self.busy:
            self.launch()


def column(row):
    r = lax.broadcasted_iota(jnp.int32, (128, 128), 0)
    c = lax.broadcasted_iota(jnp.int32, (128, 128), 1)
    return jnp.sum(jnp.where(r == c, row, 0.0), axis=1, keepdims=True)


def as_row(col):
    r = lax.broadcasted_iota(jnp.int32, (128, 128), 0)
    c = lax.broadcasted_iota(jnp.int32, (128, 128), 1)
    return jnp.sum(jnp.where(r == c, col, 0.0), axis=0, keepdims=True)


def send_out(pairs, sems):
    copies = [pltpu.make_async_copy(src, dst, sems.at[k]) for k, (src, dst) in enumerate(pairs)]
    for copy in copies:
        copy.start()
    for copy in copies:
        copy.wait()


def finish_outer_kernel(_, u, out, buf, sems):
    buf[...] = u[...].astype(F32)
    send_out([(buf, out)], sems)


def finish_outer(clock, u):
    return call(clock, finish_outer_kernel, "finish_outer", [shape(u.shape, F32)], [u], [pltpu.VMEM(u.shape, F32), pltpu.SemaphoreType.DMA((1,))], limit=JOIN, outside=(0,))[0]


def finish_kernel(token, total, inner, w_inner, pack, *refs):
    outs, (buf, buf_inner, small, sems) = refs[:-4], refs[-4:]
    gain, shift, gain_two, shift_two = (column(pack[128:129, k : k + 128].astype(F32)) for k in (0, 128, 256, 384))
    copies = []

    def leave(source, k):
        copies.append(pltpu.make_async_copy(source, outs[k], sems.at[k]))
        copies[-1].start()

    sums = total[128:144, 0:2048].astype(F32)
    n = inner[...].astype(F32)
    buf_inner[...] = gain_two * n + shift_two * sums[1:2, :]
    leave(buf_inner, 5)
    for k in range(5):
        cols = slice(512 * k, 512 * (k + 1))
        part = total[0:128, cols].astype(F32)
        buf[:, cols] = gain * part + shift * sums[0:1, cols] if k < 4 else part
        leave(buf.at[:, cols], k)
    w = pack[0:128, :].astype(F32)
    v = w_inner[...].astype(F32)
    for k, product in enumerate((w * total[0:128, 0:2048].astype(F32), w * sums[0:1, :], v * n, v * sums[1:2, :])):
        small[k : k + 1, 0:128] = as_row(jnp.sum(product, axis=1, keepdims=True))
        leave(small.at[k, 0:128], 6 + k)
    me = position(token, 0)
    small[4:5, :] = total[128:144, pl.ds(pl.multiple_of(me * 512, 512), 512)].astype(F32)[1:2, :]
    leave(small.at[4], 10)
    small[5:6, 0:128] = total[128:144, pl.ds(pl.multiple_of(me * 128, 128), 128)].astype(F32)[2:3, :]
    leave(small.at[5, 0:128], 11)
    for copy in copies:
        copy.wait()


def finish_all(clock, total, inner, w_inner, pack):
    outs = [shape((128, 512), F32)] * 5 + [shape((128, 2048), F32)] + [shape((128,), F32)] * 4 + [shape((512,), F32), shape((128,), F32)]
    scratch = [pltpu.VMEM((128, 2560), F32), pltpu.VMEM((128, 2048), F32), pltpu.VMEM((8, 512), F32), pltpu.SemaphoreType.DMA((12,))]
    return call(clock, finish_kernel, "finish_all", outs, [total, inner, w_inner, pack], scratch, limit=12, outside=range(12))


PLAN = (
    "OG", "IA", "WU", "IB", "u", "IC", "IS", "IK", "i", "RB", "AE", "u", "i", "AL", "u", "i", "PS", "PK", "p",
    "IN", "u", "i", "FO", "u", "p", "i", "p", "u", "i", "p", "u",
)
STEPS = {
    "u": ("core", "x", "half1", "half2", "all", "beside2", "beside1"),
    "i": ("core", "quarter", "x", "all", "beside2", "beside1"),
    "p": ("core", "x", "quarter", "all", "besides"),
}
PIECES = {"u": (512,), "i": (), "p": ()}


def per_device(dp, tokens, first_gain, first_shift, w_query, w_key, w_value, w_control, w_output, second_gain, second_shift, w_inner, inner_bias, w_outer, outer_bias, cotangent):
    clock = Clock(lax.axis_index("fsdp").astype(jnp.int32), lax.axis_index("dp").astype(jnp.int32))
    vectors = (first_gain, first_shift, second_gain, second_shift, outer_bias, inner_bias)
    own, first, second, wi0, wi1 = begin(clock, (w_query, w_key, w_value, w_control), vectors, w_inner)
    mine = [over_x(first), over_x(second)]
    own_core, wi_c = over_core(own), over_core(w_inner)
    n1, n1_low = first_norm(clock, tokens)
    *mine, wi0, wi1, w_output = clock.sync(*mine, wi0, wi1, w_output)
    wi_x0 = over_x(wi0)
    across = assemble(clock, mine, [exchange(v, "dp", dp, k + 1) for k, v in enumerate(mine)], wi_x0)
    packs = [own, across, own_core, over_core(across)]
    wi1, w_output = clock.sync(wi1, w_output)
    wi_x1, wo_x, wo_c = over_x(wi1), over_x(w_output), over_core(w_output)
    qkvf = project(clock, n1, packs)
    w_outer = clock.sync(w_outer)
    wu_x, wu_c = over_x(w_outer), over_core(w_outer)
    mixed, *saved = attention_forward(clock, qkvf)
    wo_x, wi_x1 = clock.sync(wo_x, wi_x1)
    wo = [w_output, wo_x, wo_c, over_core(wo_x)]
    wi = [w_inner, wi_x0, wi_x1, wi_c, over_core(wi_x0), over_core(wi_x1)]
    resid, n2, r2, a2 = middle(clock, tokens, mixed, wo, packs)
    act, slope = ffn_inner(clock, a2, wi, packs)
    chains, made = {}, {}

    def start(name, send, keep):
        chains[name] = Chain(clock, dp, STEPS[name], send, PIECES[name])
        made[name] = keep

    def outer():
        keep, send = outer_grad(clock, act, cotangent)
        start("u", [send], lambda: keep)

    def wait_outer():
        wu_x = clock.sync(made["wu"])
        made["wu"] = [w_outer, wu_x, wu_c, over_core(wu_x)]

    def back_near():
        made["din"] = inner_back(clock, cotangent, slope, [w_outer, wu_c], (0, 2))

    def back_far():
        d, partial = made["din"]
        made["din"] = inner_back(clock, cotangent, d, [made["wu"][1]], (1,), [partial])

    def back_last():
        d, partial = made["din"]
        made["din"] = inner_back(clock, cotangent, d, [made["wu"][3]], (3,), [partial])

    def inner_send():
        start("i", [inner_grad(clock, n2, made["din"][0], 2)], None)

    def inner_keep():
        made["i"] = inner_grad(clock, n2, made["din"][0], 0)

    def resid_grad():
        made["dres"], made["do"] = resid_back(clock, cotangent, n2, r2, made["din"][0], wo, wi, packs)

    def early():
        made["early"] = attention_backward(clock, qkvf, saved, made["do"], 7, 4)

    def late():
        made["late"] = attention_backward(clock, qkvf, saved, made["do"], 3, 4, made["early"][1:])

    def project_part(first):
        return project_grad(clock, n1_low, made["late"][0], made["early"][0], mixed, made["dres"], made["din"][1], first)

    def project_send():
        start("p", [project_part(2)], None)

    def project_keep():
        made["p"] = project_part(0)

    def input_part():
        made["tokens"] = input_grad(clock, tokens, made["late"][0], made["early"][0], made["dres"], packs)

    def output_part():
        made["output"] = ffn_outer(clock, resid, act, made["wu"], packs)

    def finish(name):
        if name == "u":
            made["outer"] = finish_outer(clock, chains[name].keep)
        elif not (chains["i"].busy or chains["p"].busy):
            made["rest"] = finish_all(clock, chains["p"].keep, chains["i"].keep, w_inner, packs[0])

    def advance(name):
        c = chains[name]
        if not c.busy:
            return
        if c.kind == "core":
            keep = made[name]
            c.keep = keep() if callable(keep) else keep
        if c.split:
            c.more()
        else:
            c.step()
            if not c.busy:
                finish(name)

    made["wu"] = wu_x
    kernels = dict(OG=outer, WU=wait_outer, IA=back_near, IB=back_far, IC=back_last, IS=inner_send, IK=inner_keep, RB=resid_grad, AE=early, AL=late, PS=project_send, PK=project_keep, IN=input_part, FO=output_part)
    for word in PLAN:
        if word in kernels:
            kernels[word]()
        else:
            advance(word)
    while any(c.busy for c in chains.values()):
        for name in "uip":
            advance(name)
    (
        grad_query, grad_key, grad_value, grad_control, grad_output, grad_inner, first_gain_grad, first_shift_grad,
        second_gain_grad, second_shift_grad, inner_bias_grad, outer_bias_grad,
    ) = made["rest"]
    return (
        made["output"], made["tokens"], first_gain_grad, first_shift_grad, grad_query, grad_key, grad_value, grad_control, grad_output,
        second_gain_grad, second_shift_grad, grad_inner, inner_bias_grad, made["outer"], outer_bias_grad,
    )


def solution(mesh):
    row, vec, mat = P(("dp", "fsdp"), None), P("fsdp"), P("fsdp", None)
    return jax.shard_map(
        functools.partial(per_device, mesh.shape["dp"]),
        mesh=mesh,
        in_specs=(row, vec, vec, mat, mat, mat, mat, mat, vec, vec, mat, vec, mat, vec, row),
        out_specs=(row, row, vec, vec, mat, mat, mat, mat, mat, vec, vec, mat, vec, mat, vec),
        check_vma=False,
    )
```
